32 devices in a mesh: wide: 8 (over z, x), narrow: 4 (over y, core).
Axes of the slice: x: 2, y: 2, z: 4, core: 2. Of those that a mesh axis runs over, the one named last changes fastest.
Arguments:
- block_input: bfloat16 [64, 2048, 1024], P(('wide', 'narrow')), may hold values from -6 to 6
- query_weight: bfloat16 [1024, 1024], P('wide'), may hold values from -0.1875 to 0.1875
- key_weight: bfloat16 [1024, 1024], P('wide'), may hold values from -0.1875 to 0.1875
- value_weight: bfloat16 [1024, 1024], P('wide'), may hold values from -0.1875 to 0.1875
- out_weight: bfloat16 [1024, 1024], P('wide'), may hold values from -0.75 to 0.75
- up_weight: bfloat16 [1024, 4096], P('wide'), may hold values from -0.1875 to 0.1875
- down_weight: bfloat16 [4096, 1024], P('wide'), may hold values from -0.09375 to 0.09375
- attn_gain: bfloat16 [1024], P('wide'), may hold values from 0.099609375 to 1.8984375
- mlp_gain: bfloat16 [1024], P('wide'), may hold values from 0.099609375 to 1.8984375
- router_weight: bfloat16 [1024], replicated, may hold values from -0.1875 to 0.1875
- slots: int32 [64, 256], P(('wide', 'narrow')), may hold values from 0 to 2047, as said below
- segments: int32 [64, 2048], P(('wide', 'narrow')), may hold values from 0 to 7, never falling along the last dimension, each value on 1 to 512 neighbouring positions
- pad_mask: int32 [64, 2048], P(('wide', 'narrow')), may hold values from 0 to 1, as said below
- cotangent: bfloat16 [64, 2048, 1024], P(('wide', 'narrow')), may hold values from -6 to 6
Outputs:
- block_output: bfloat16 [64, 2048, 1024], P(('wide', 'narrow'))
- input_grad: bfloat16 [64, 2048, 1024], P(('wide', 'narrow'))
- grad_query: float32 [1024, 1024], P('wide')
- grad_key: float32 [1024, 1024], P('wide')
- grad_value: float32 [1024, 1024], P('wide')
- grad_out: float32 [1024, 1024], P('wide')
- grad_up: float32 [1024, 4096], P('wide')
- grad_down: float32 [4096, 1024], P('wide')
- grad_attn_gain: float32 [1024], P('wide')
- grad_mlp_gain: float32 [1024], P('wide')
- grad_router: float32 [1024], replicated
- statistics: float32 [2], replicated
The draws below stay inside these ranges and needn't reach their ends.
Inputs may be any that keep to these rules, and one draw needn't show every extreme that they name: `slots`: each row holds 256 different positions in increasing order, each where pad_mask is 1. `pad_mask`: in each row the ones come first, then the zeros, with more than 256 ones.
All inputs are finite; a program needn't handle non-finite values.
Results may differ from the reference program's by a relative error of at most 0.012.
Values may be sent and summed in bfloat16 or wider, within the bound.
A program may use at most 256 MiB of HBM per device.

```python
import math
import jax
import jax.numpy as jnp
import numpy as np
from jax import lax

D = 1024
HEADS = 16
HEAD_DIM = 64
FF = 4096
SEQ = 2048
DOCS = 8
CAP = 256
BATCH = 64


def valid_lengths(key):
    jitter = jax.random.randint(key, (BATCH,), 0, SEQ // 16 + 1)
    rank = jnp.arange(BATCH, dtype=jnp.int32)
    jitter = jnp.where(rank == BATCH - 1, 0, jitter)
    return SEQ // 3 + (SEQ - SEQ // 3) * (rank + 1) // BATCH - jitter


def draw_pad_mask(key, part):
    lengths = valid_lengths(key)
    positions = jnp.arange(SEQ, dtype=jnp.int32)
    return (positions[None, :] < lengths[:, None]).astype(jnp.int32)


def draw_slots(key, part):
    lengths = valid_lengths(key)
    key = jax.random.fold_in(key, 7)
    positions = jnp.arange(SEQ, dtype=jnp.int32)[None, :]
    ranking = jax.random.randint(key, (BATCH, SEQ), 0, 2 ** 14) * SEQ + positions
    ranking = jnp.where(positions >= lengths[:, None], ranking + 2 ** 28, ranking)
    ends = (positions == 0) | (positions == lengths[:, None] - 1)
    ranking = jnp.where(ends, -1 - positions, ranking)
    chosen = jnp.argsort(ranking, axis=1, stable=True)[:, :CAP]
    return jnp.sort(chosen, axis=1).astype(jnp.int32)


def block_scale(key, dims, cuts, smallest, high):
    factor_of = 1.0
    for position, parts in cuts:
        heights = jax.random.uniform(jax.random.fold_in(jax.random.fold_in(key, 6), position), (parts,), jnp.float32, smallest / len(cuts), high / len(cuts))
        factor_of = factor_of * jnp.repeat(jnp.exp(heights), dims[position] // parts).reshape((-1,) + (1,) * (len(dims) - 1 - position))
    return factor_of


def profile(count, total, limit, lean):
    portions = [(1 << 20) // math.isqrt(rank ** lean) + 1 for rank in range(2, count + 1)]
    rest, holding = total - limit - (count - 1), [1] * (count - 1)
    while rest > 0:
        movable = [i for i in range(count - 1) if holding[i] < limit]
        pool, budget = sum([portions[i] for i in movable]), rest
        for i in movable:
            addition = min(limit - holding[i], max(1, budget * portions[i] // pool), rest)
            holding[i] = holding[i] + addition
            rest = rest - addition
    return np.array([limit] + holding)


def ragged(key, count, total, most, slope):
    if count == 2:
        one = jax.random.randint(key, (), max(1, total - most), min(most, total - 1) + 1)
        return jnp.stack([one, total - one])
    sizes = jnp.asarray(profile(count, total, most, slope), jnp.int32)
    couples = (count - 1) // 2
    giver, taker = sizes[1:1 + 2 * couples:2], sizes[2:2 + 2 * couples:2]
    room = jnp.minimum(giver - 1, most - taker)
    moved = jax.random.randint(jax.random.fold_in(key, 1), (couples,), 0, 1 << 20) % (room + 1)
    sizes = sizes.at[1:1 + 2 * couples:2].set(giver - moved).at[2:2 + 2 * couples:2].set(taker + moved)
    return sizes[jax.random.permutation(jax.random.fold_in(key, 2), count)]


def scatter_about(key, extent, spread, reach, split=(), kind=jnp.bfloat16):
    factor_of = block_scale(key, extent, split, -0.22, 0.18) if split else 1.0
    drawn = jax.random.normal(key, extent, jnp.float32) * spread * factor_of
    return jnp.minimum(jnp.maximum(drawn, -reach), reach).astype(kind)


def setup_inputs(seed: int = 0) -> dict:
    key_list = jax.random.split(jax.random.key(seed), 15)
    return {
        "block_input": scatter_about(key_list[0], (BATCH, SEQ, D), 1.0, 6.0, ((0, 32),)),
        "query_weight": scatter_about(key_list[1], (D, D), D ** -0.5, 0.1875, ((0, 8),)),
        "key_weight": scatter_about(key_list[2], (D, D), D ** -0.5, 0.1875, ((0, 8),)),
        "value_weight": scatter_about(key_list[3], (D, D), D ** -0.5, 0.1875, ((0, 8),)),
        "out_weight": scatter_about(key_list[4], (D, D), (D // 16) ** -0.5, 0.75, ((0, 8),)),
        "up_weight": scatter_about(key_list[5], (D, FF), D ** -0.5, 0.1875, ((0, 8),)),
        "down_weight": scatter_about(key_list[6], (FF, D), FF ** -0.5, 0.09375, ((0, 8),)),
        "attn_gain": jnp.clip(1.0 + 0.18 * jax.random.normal(key_list[7], (D,), jnp.float32), 0.099609375, 1.8984375).astype(jnp.bfloat16),
        "mlp_gain": jnp.clip(1.0 + 0.18 * jax.random.normal(key_list[8], (D,), jnp.float32), 0.099609375, 1.8984375).astype(jnp.bfloat16),
        "router_weight": scatter_about(key_list[9], (D,), D ** -0.5, 0.1875),
        "slots": draw_slots(jax.random.fold_in(key_list[14], 71), 0),
        "segments": jax.vmap(lambda own: jnp.searchsorted(jnp.cumsum(ragged(own, DOCS, SEQ, SEQ // 4, 0)), jnp.arange(SEQ), side="right"))(jax.random.split(key_list[11], BATCH)).reshape((BATCH, SEQ)).astype(jnp.int32),
        "pad_mask": draw_pad_mask(jax.random.fold_in(key_list[14], 71), 0),
        "cotangent": scatter_about(key_list[13], (BATCH, SEQ, D), 1.0, 6.0, ((0, 32),)),
    }


@jax.custom_vjp
def low(v):
    return lax.optimization_barrier(v.astype(jnp.bfloat16)).astype(jnp.float32)

@jax.custom_vjp
def low_back(v):
    return v

def low_keep(v):
    return (low(v), None)

def low_pass(kept, grad):
    return (grad,)

def back_keep(v):
    return (v, None)

def back_low(kept, grad):
    return (low(grad),)
low.defvjp(low_keep, low_pass)
low_back.defvjp(back_keep, back_low)
highest = lax.Precision.HIGHEST

def rms_gain(values, gain):
    return values * lax.rsqrt(lax.optimization_barrier(jnp.mean(values * values, axis=-1, keepdims=True)) + 1e-06) * gain

def one_sequence(seq_rows, weights, slot_row, seg_row):
    w_query, w_key, w_value, w_out, w_up, w_down, gain_attn, gain_mlp, w_router = weights
    routed = seq_rows[slot_row]
    router_gate = jax.nn.sigmoid(jnp.dot(routed, w_router, precision=highest))
    normed_one = low(rms_gain(routed, gain_attn))
    queries = low(low_back(jnp.dot(normed_one, w_query, precision=highest))).reshape(CAP, HEADS, HEAD_DIM)
    keys = low(low_back(jnp.dot(normed_one, w_key, precision=highest))).reshape(CAP, HEADS, HEAD_DIM)
    values = low(low_back(jnp.dot(normed_one, w_value, precision=highest))).reshape(CAP, HEADS, HEAD_DIM)
    slot_segs = seg_row[slot_row]
    order = jnp.arange(CAP, dtype=jnp.int32)
    allowed = (order[:, None] >= order[None, :]) & (slot_segs[:, None] == slot_segs[None, :])
    logits = low_back(jnp.einsum('qhe,khe->hqk', queries, keys, precision=highest) * HEAD_DIM ** (-0.5))
    logits = jnp.where(allowed[None], logits, -1e+30)
    shifted = logits - lax.optimization_barrier(jnp.max(logits, axis=-1, keepdims=True))
    weights_exp = jnp.exp(shifted)
    probs = low(weights_exp / lax.optimization_barrier(jnp.sum(weights_exp, axis=-1, keepdims=True)))
    mixed = jnp.einsum('hqk,khe->qhe', probs, values, precision=highest).reshape(CAP, D)
    mixed = low(low_back(mixed))
    attn_out = low_back(jnp.dot(mixed, w_out, precision=highest))
    resid = routed + attn_out
    normed_two = low(rms_gain(resid, gain_mlp))
    pre_act = low_back(jnp.dot(normed_two, w_up, precision=highest))
    activ = low(jax.nn.gelu(pre_act))
    mlp_out = low_back(jnp.dot(activ, w_down, precision=highest))
    new_rows = routed + router_gate[:, None] * (attn_out + mlp_out)
    return seq_rows.at[slot_row].set(new_rows)

def reference(block_input, query_weight, key_weight, value_weight, out_weight, up_weight, down_weight, attn_gain, mlp_gain, router_weight, slots, segments, pad_mask, cotangent):
    weights = tuple((w.astype(jnp.float32) for w in (query_weight, key_weight, value_weight, out_weight, up_weight, down_weight, attn_gain, mlp_gain, router_weight)))

    def step(carry, item):
        seq_rows, seq_grad, slot_row, seg_row, mask_row = item
        seq_float = seq_rows.astype(jnp.float32)
        mask_float = mask_row.astype(jnp.float32)

        def forward(rows_in, *params):
            all_gates = jax.nn.sigmoid(jnp.dot(rows_in, params[8], precision=highest))
            sums = jnp.stack([jnp.sum(mask_float[slot_row]), jnp.sum(mask_float), jnp.sum(mask_float * all_gates)])
            return (one_sequence(rows_in, params, slot_row, seg_row), sums)
        result, back, sums = jax.vjp(forward, seq_float, *weights, has_aux=True)
        grads = back(seq_grad.astype(jnp.float32))
        updated = tuple((c + g for c, g in zip(carry, grads[1:])))
        return (updated, (result.astype(jnp.bfloat16), grads[0].astype(jnp.bfloat16), sums))
    zeros = tuple((jnp.zeros_like(w) for w in weights))
    totals, (outputs, input_grads, sums) = lax.scan(step, zeros, (block_input, cotangent, slots, segments, pad_mask))
    overall = lax.optimization_barrier(jnp.sum(sums, axis=0))
    statistics = jnp.stack([overall[0] / overall[1], overall[2] / overall[1]])
    return (outputs, input_grads, totals[0], totals[1], totals[2], totals[3], totals[4], totals[5], totals[6], totals[7], totals[8], statistics)
```

```python
import functools
import math

import jax
import jax.numpy as jnp
from jax import lax
from jax.experimental import pallas as pl
from jax.experimental.pallas import tpu as pltpu
from jax.sharding import PartitionSpec as P

HEADS = 16
HEAD_DIM = 64
EPS = 1e-06
LANES = 128
MESH = pl.DeviceIdType.MESH
f32 = jnp.float32
bf16 = jnp.bfloat16
MIB = 2**20
CHUNK = 512
DEBUG = ()


def dot(a, b, ca, cb):
    return lax.dot_general(a, b, (((ca,), (cb,)), ((), ())), preferred_element_type=f32)


def aligned(start, size):
    return pl.ds(pl.multiple_of(start, size), size)


def loop(count, step):
    def run(i, carry):
        step(i)
        return carry

    lax.fori_loop(0, count, run, 0)


class Links:
    def __init__(self, send, recv):
        self.send, self.recv, self.count, self.open = send, recv, 0, []

    def make(self, src, dst, device):
        i = self.count
        self.count += 1
        return pltpu.make_async_remote_copy(
            src_ref=src,
            dst_ref=dst,
            send_sem=self.send.at[i],
            recv_sem=self.recv.at[i],
            device_id=device,
            device_id_type=MESH,
        )

    def go(self, src, dst, device):
        copy = self.make(src, dst, device)
        copy.start()
        self.open.append(copy)
        return copy

    def sent(self, copy):
        copy.wait_send()
        self.open = [other for other in self.open if other is not copy]

    def sent_all(self, copies):
        for copy in copies:
            self.sent(copy)

    def drain(self):
        for copy in self.open:
            copy.wait_send()
        self.open = []


def copy_count(far):
    near = far - 1
    gather = 2 * (8 * near + 2) + 3 * (2 * near + 1)
    narrow = 2 * 6 + 2 * 3
    reduce_mlp = 2 * (far + near + 3)
    reduce_attn = 4 * (1 + 2 * far + near + 3)
    return gather + narrow + reduce_mlp + reduce_attn + 3 + near


def block_kernel(dims, names, *refs):
    r = dict(zip(names, refs))
    A, R, T, S, CAP, SEQ, D, RB = (
        dims[k] for k in ("A", "R", "T", "S", "CAP", "SEQ", "D", "RB")
    )
    Wd = 2 * A
    half, quart = D // 2, D // 4
    scale = 1.0 / math.sqrt(HEAD_DIM)
    w, n = lax.axis_index("wide"), lax.axis_index("narrow")
    z, x = w // 2, w % 2
    y, c = n // 2, n % 2
    WA, WU, WD, GP = r["WA"], r["WU"], r["WD"], r["GP"]
    NT, MG, ACT, DG = r["NT"], r["MG"], r["ACT"], r["DG"]
    QKVM, N1, RT, OG = r["QKVM"], r["N1"], r["RT"], r["OG"]
    AO, NG, MO = r["AO"], r["NG"], r["MO"]
    PS, PR, YS, YR = r["PS"], r["PR"], r["YS"], r["YR"]
    GATE, R1, R2, LG = r["GATE"], r["R1"], r["R2"], r["LG"]
    SEGC, SEGR, STAT, SM = r["SEGC"], r["SEGR"], r["STAT"], r["SM"]
    local, credit = r["local"], r["credit"]
    links = Links(r["send"], r["recv"])

    def dev(zz, xx, yy, cc):
        return (zz * 2 + xx, yy * 2 + cc)

    to_x, to_y, to_c = dev(z, 1 - x, y, c), dev(z, x, 1 - y, c), dev(z, x, y, 1 - c)
    ahead = [(z + dz) % A for dz in range(A)]
    behind = [(z - dz + A) % A for dz in range(A)]

    own = [
        pltpu.make_async_copy(r["w_query"], WA.at[0, w], local.at[0]),
        pltpu.make_async_copy(r["w_key"], WA.at[1, w], local.at[1]),
        pltpu.make_async_copy(r["w_value"], WA.at[2, w], local.at[2]),
        pltpu.make_async_copy(r["w_out"], WA.at[3, w], local.at[3]),
        pltpu.make_async_copy(r["w_up"], WU.at[z, x], local.at[4]),
        pltpu.make_async_copy(r["w_down"].at[aligned(n * R, R)], WD.at[z, x], local.at[5]),
        pltpu.make_async_copy(r["gains"], GP.at[w], local.at[6]),
    ]
    for copy in own:
        copy.start()
    fetches = {}

    def fetch(i, slot):
        s, k = i // (SEQ // CHUNK), i % (SEQ // CHUNK)
        return [
            pltpu.make_async_copy(
                r[name].at[s, aligned(k * CHUNK, CHUNK)], QKVM.at[2 * slot + a], local.at[7 + 2 * slot + a]
            )
            for a, name in enumerate(("block_input", "cotangent"))
        ]

    for copy in fetch(0, 0):
        copy.start()
    barrier = pltpu.get_barrier_semaphore()
    peers = [dev(ahead[dz], x, y, c) for dz in range(1, A)] + [to_x, to_y, to_c]
    for peer in peers:
        pl.semaphore_signal(barrier, inc=1, device_id=peer, device_id_type=MESH)
    pl.semaphore_wait(barrier, len(peers))
    for copy in own:
        copy.wait()

    class AttnGather:
        def __init__(self, first, count):
            self.first, self.count = first, count

        def piece(self, zz, xx, yy):
            return WA.at[pl.ds(self.first, self.count), zz * 2 + xx, :, aligned(c * half + yy * quart, quart)]

        def wide_piece(self, zz, xx):
            return WA.at[pl.ds(self.first, self.count), zz * 2 + xx, :, aligned(c * half, half)]

        def start(self):
            p, q = self.piece(z, x, y), self.wide_piece(z, x)
            self.far = {dz: links.go(p, p, dev(ahead[dz], x, y, c)) for dz in range(1, A)}
            self.x0 = links.go(q, q, to_x)
            self.x1, self.y1, self.second, self.core = {}, {}, {}, []

        def to_core(self, p):
            self.core.append(links.go(p, p, to_c))

        def relay(self, dz):
            self.far[dz].wait_recv()
            p = self.piece(behind[dz], x, y)
            self.x1[dz] = links.go(p, p, to_x)
            self.y1[dz] = links.go(p, p, to_y)
            self.to_core(p)

        def relay_own(self):
            self.x0.wait_recv()
            self.to_core(self.wide_piece(z, 1 - x))

        def relay_second(self, dz):
            self.x1[dz].wait_recv()
            p = self.piece(behind[dz], 1 - x, y)
            if dz % 2:
                self.second[dz] = links.go(p, p, to_y)
            self.to_core(p)
            self.y1[dz].wait_recv()
            p = self.piece(behind[dz], x, 1 - y)
            if not dz % 2:
                self.second[dz] = links.go(p, p, to_x)
            self.to_core(p)

        def relay_third(self, dz):
            self.second[dz].wait_recv()
            self.to_core(self.piece(behind[dz], 1 - x, 1 - y))

        def finish(self):
            for copy in self.core:
                copy.wait_recv()

    class WideGather:
        def __init__(self, at):
            self.at = at

        def start(self):
            p = self.at(z, x)
            self.far = {dz: links.go(p, p, dev(ahead[dz], x, y, c)) for dz in range(1, A)}
            self.near = [links.go(p, p, to_x)]

        def relay(self, dz):
            self.far[dz].wait_recv()
            p = self.at(behind[dz], x)
            self.near.append(links.go(p, p, to_x))

        def finish(self):
            for copy in self.near:
                copy.wait_recv()

        def release(self):
            links.sent_all(list(self.far.values()) + self.near)

    gains = WideGather(lambda zz, xx: GP.at[zz * 2 + xx])
    qkv, out = AttnGather(0, 3), AttnGather(3, 1)
    up = WideGather(lambda zz, xx: WU.at[zz, xx])
    down = WideGather(lambda zz, xx: WD.at[zz, xx])
    gains.start()
    qkv.start()
    out.start()

    AO[...] = jnp.zeros_like(AO)
    NG[...] = jnp.zeros_like(NG)
    SEGC[...] = jnp.zeros_like(SEGC)
    SEGR[...] = jnp.zeros_like(SEGR)
    STAT[...] = jnp.zeros_like(STAT)
    steps = S * (SEQ // CHUNK)

    def gather_step(i):
        slot = i % 2
        s, k = i // (SEQ // CHUNK), i % (SEQ // CHUNK)

        @pl.when(i + 1 < steps)
        def _():
            for copy in fetch(i + 1, (i + 1) % 2):
                copy.start()

        for copy in fetch(i, slot):
            copy.wait()
        position = lax.broadcasted_iota(jnp.int32, (CAP, CHUNK), 1) + k * CHUNK
        onehot = jnp.where(r["slots"][s] == position, 1.0, 0.0).astype(bf16)
        rows = aligned(s * CAP, CAP)
        tokens = QKVM[2 * slot]
        AO[rows, :] += dot(onehot, tokens, 1, 0)
        NG[rows, :] += dot(onehot, QKVM[2 * slot + 1], 1, 0)
        marks = r["marks"][s, :, aligned(k * CHUNK, CHUNK)]
        mask = marks[1:2].astype(f32)
        gate_logits = dot(r["router"][...], tokens, 1, 1)[0:1]
        STAT[0:1] += mask * jax.nn.sigmoid(gate_logits)
        STAT[1:2] += mask
        SEGR[s] += dot(marks, onehot, 1, 1)
        SEGC[s] += dot(onehot, jnp.broadcast_to(marks[0:1].astype(f32), (LANES, CHUNK)).astype(bf16), 1, 1)

    loop(steps, gather_step)

    step_rows = T // 4
    router_row = r["router"][0:1].astype(f32)

    def gate_step(i):
        rows = aligned(i * step_rows, step_rows)
        v, g = AO[rows, :], NG[rows, :]
        gate = jax.nn.sigmoid(jnp.sum(v * router_row, axis=-1, keepdims=True))
        GATE[rows, :] = gate
        R1[rows, :] = lax.rsqrt(jnp.mean(v * v, axis=-1, keepdims=True) + EPS)
        RT[rows, :] = v.astype(bf16)
        OG[rows, :] = g.astype(bf16)
        MG[n, rows, :] = (gate * g).astype(bf16)

    loop(4, gate_step)

    class RowShare:
        def __init__(self, at):
            self.at = at

        def start(self, k):
            p = self.at(n, k)
            self.core = getattr(self, "core", {})
            self.far = getattr(self, "far", {})
            self.core[k] = links.go(p, p, to_c)
            self.far[k] = links.go(p, p, to_y)

        def relay(self, k):
            self.far[k].wait_recv()
            p = self.at((1 - y) * 2 + c, k)
            self.last = getattr(self, "last", {})
            self.last[k] = links.go(p, p, to_c)

        def release(self):
            for copies in (self.core, self.far, self.last):
                links.sent_all(list(copies.values()))

    rows_half = T // 2
    share_mg = RowShare(lambda b, k: MG.at[b, pl.ds(k * rows_half, rows_half)])
    share_nt = RowShare(lambda b, k: NT.at[b, pl.ds(k * (A // 2), A // 2)])

    for dz in range(1, A):
        gains.relay(dz)
    for dz in range(1, A):
        qkv.relay(dz)
    up.start()
    for dz in range(1, A):
        out.relay(dz)
    share_mg.start(0)
    gains.finish()
    gain_rows = jnp.sum(GP[...], axis=0)
    r["GN"][...] = gain_rows

    def norm_one_step(i):
        rows = aligned(i * step_rows, step_rows)
        N1[rows, :] = (RT[rows, :].astype(f32) * R1[rows, :] * r["GN"][0:1]).astype(bf16)

    loop(4, norm_one_step)
    qkv.relay_own()
    for dz in range(1, A):
        qkv.relay_second(dz)
    out.relay_own()
    for dz in range(1, A):
        qkv.relay_third(dz)
    qkv.finish()

    def project(i):
        cols = aligned((i % 4) * quart, quart)
        g = i // 4
        QKVM[g, :, cols] = dot(N1[...], WA[g, :, :, cols].reshape(D, quart), 1, 0).astype(bf16)

    loop(12, project)
    for dz in range(1, A):
        out.relay_second(dz)
    for dz in range(1, A):
        out.relay_third(dz)
    for dz in range(1, A):
        up.relay(dz)
    down.start()

    lane = lax.broadcasted_iota(jnp.int32, (1, LANES), 1)
    low_lanes = lane < HEAD_DIM
    causal = lax.broadcasted_iota(jnp.int32, (CAP, CAP), 0) >= lax.broadcasted_iota(jnp.int32, (CAP, CAP), 1)

    def pick(h, v):
        return jnp.where(low_lanes if h == 0 else ~low_lanes, v, jnp.zeros_like(v))

    def place(i):
        return aligned((i // (D // LANES)) * CAP, CAP), aligned((i % (D // LANES)) * LANES, LANES)

    def softmax_of(s, q, k, h):
        logits = dot(pick(h, q), k, 1, 1) * scale
        same = SEGC[s][:, 0:1] == SEGR[s][0:1]
        logits = jnp.where(causal & same, logits, -1e30)
        e = jnp.exp(logits - jnp.max(logits, axis=-1, keepdims=True))
        return e * (1.0 / jnp.sum(e, axis=-1, keepdims=True))

    def attend(i):
        rows, cols = place(i)
        s = i // (D // LANES)
        q, k, v = QKVM[0, rows, cols], QKVM[1, rows, cols], QKVM[2, rows, cols]
        o = [dot(softmax_of(s, q, k, h).astype(bf16), v, 1, 0) for h in range(2)]
        QKVM[3, rows, cols] = jnp.where(low_lanes, o[0], o[1]).astype(bf16)

    pairs = S * (D // LANES)
    loop(pairs, attend)
    out.finish()

    def project_out(i):
        cols = aligned(i * quart, quart)
        AO[:, cols] = dot(QKVM[3], WA[3, :, :, cols].reshape(D, quart), 1, 0)

    loop(4, project_out)

    def norm_two(k):
        def step(i):
            rows = aligned(k * rows_half + i * (rows_half // 2), rows_half // 2)
            v = RT[rows, :].astype(f32) + AO[rows, :]
            scale_two = lax.rsqrt(jnp.mean(v * v, axis=-1, keepdims=True) + EPS)
            R2[rows, :] = scale_two
            part = (v * scale_two * r["GN"][1:2]).astype(bf16)
            NT[n, pl.ds(k * (A // 2) + i * (A // 4), A // 4)] = part.reshape(A // 4, 2, RB, D)

        loop(2, step)

    for k in range(2):
        norm_two(k)
        share_nt.start(k)
    share_mg.start(1)

    def block_of(ref, b):
        return ref.at[b // 2, pl.ds((b % 2) * (A // 2), A // 2)]

    tanh_k = math.sqrt(2.0 / math.pi)

    def up_block(b):
        rows = NT[b].reshape(T, D)

        def step(i):
            cols = aligned(i * quart, quart)
            v = dot(NT[b].reshape(T, D), WU[:, :, :, cols].reshape(D, quart), 1, 0)
            vv = v * v
            t = jnp.tanh(tanh_k * v * (1.0 + 0.044715 * vv))
            act = 0.5 * v * (1.0 + t)
            slope = 0.5 * (1.0 + t) + 0.5 * v * (1.0 - t * t) * (tanh_k * (1.0 + 0.134145 * vv))
            block_of(ACT, b)[..., cols] = act.astype(bf16).reshape(A // 2, 2, 2, RB, quart)
            block_of(DG, b)[..., cols] = slope.astype(bf16).reshape(A // 2, 2, 2, RB, quart)

        loop(4, step)

    up.finish()
    up_block(n)
    for k in range(2):
        share_nt.core[k].wait_recv()
    up_block(y * 2 + 1 - c)
    for dz in range(1, A):
        down.relay(dz)
    for k in range(2):
        share_mg.relay(k) if k == 0 else None
        share_nt.relay(k)
    share_mg.relay(1)
    up_block((1 - y) * 2 + c)
    for k in range(2):
        share_nt.last[k].wait_recv()
    up_block((1 - y) * 2 + 1 - c)
    for k in range(2):
        share_mg.core[k].wait_recv()
        share_mg.last[k].wait_recv()
    down.finish()

    def act_grad_step(i):
        b, j = i // 4, i % 4
        cols = aligned(j * quart, quart)
        rows = WD[pl.ds(j * (A // 4), A // 4)].reshape(quart, D)
        v = dot(MG[b], rows, 1, 1)
        at = block_of(DG, b)
        slope = at[..., cols].reshape(T, quart).astype(f32)
        at[..., cols] = (v * slope).astype(bf16).reshape(A // 2, 2, 2, RB, quart)

    loop(16, act_grad_step)

    class NarrowReduce:
        def __init__(self, part, k, total):
            self.part, self.k, self.total = part, k, total

        def run(self, b, store):
            def step(j):
                cols = aligned(j * quart, quart)
                store(cols, self.part(b, j))

            loop(4, step)

        def start(self):
            self.core = []
            for q, yy in enumerate((1 - y, y)):

                def put(cols, v, q=q):
                    PS[q, :, cols] = v.astype(bf16)

                self.run(yy * 2 + 1 - c, put)
                self.core.append(links.go(PS.at[q], PR.at[q], to_c))
            self.core[0].wait_recv()

            def put_far(cols, v):
                YS[:, cols] = (v + PR[0, :, cols].astype(f32)).astype(bf16)

            self.run((1 - y) * 2 + c, put_far)
            self.far = links.go(YS, YR.at[self.k], to_y)
            self.core[1].wait_recv()

            def put_own(cols, v):
                self.total[:, cols] = v + PR[1, :, cols].astype(f32)

            self.run(n, put_own)

    def norm_two_part(b, j):
        rows = WU[pl.ds(j * (A // 4), A // 4)].reshape(quart, D)
        return dot(block_of(DG, b)[...].reshape(T, D), rows, 1, 1)

    def mlp_part(b, j):
        cols = aligned(j * quart, quart)
        return dot(block_of(ACT, b)[...].reshape(T, D), WD[:, :, :, cols].reshape(D, quart), 1, 0)

    reduce_nt = NarrowReduce(norm_two_part, 0, NG)
    reduce_nt.start()
    pl.semaphore_signal(credit.at[0], inc=1, device_id=to_c, device_id_type=MESH)

    class WideReduce:
        def __init__(self, grad, k):
            self.grad, self.k = grad, k

        def compute(self, lhs, rhs):
            def step(i):
                cols = aligned(i * quart, quart)
                v = dot(lhs(cols), rhs(), 0, 0)
                self.grad[pl.ds(i * (A // 4), A // 4)] = v.astype(bf16).reshape(A // 4, 2, R, D)

            loop(4, step)

        def start(self):
            self.x = {}
            for dz in list(range(1, A)) + [0]:
                self.x[dz] = links.go(self.grad.at[ahead[dz], 1 - x], r["GXR"].at[self.k, dz], to_x)

        def middle(self):
            self.far = {}
            for dz in list(range(1, A)) + [0]:
                self.x[dz].wait_recv()
                p = self.grad.at[ahead[dz], x]
                p[...] = (p[...].astype(f32) + r["GXR"][self.k, dz].astype(f32)).astype(bf16)
                if dz:
                    self.far[dz] = links.go(p, r["GZR"].at[self.k, dz - 1], dev(ahead[dz], x, y, c))

        def last(self):
            total = self.grad[z, x].astype(f32)
            for dz in range(1, A):
                self.far[dz].wait_recv()
                total = total + r["GZR"][self.k, dz - 1].astype(f32)
            r["FIN"][self.k, n] = total.astype(bf16)
            p = r["FIN"].at[self.k, n]
            self.core = [links.go(p, p, to_c)]
            self.yy = links.go(p, p, to_y)

        def finish(self):
            self.yy.wait_recv()
            p = r["FIN"].at[self.k, (1 - y) * 2 + c]
            self.core.append(links.go(p, p, to_c))
            for copy in self.core:
                copy.wait_recv()

    reduce_up, reduce_down = WideReduce(WU, 0), WideReduce(WD, 1)
    up.release()
    reduce_up.compute(lambda cols: NT[..., cols].reshape(4 * T, quart), lambda: DG[...].reshape(4 * T, D))
    reduce_up.start()
    share_nt.release()
    pl.semaphore_signal(credit.at[1], inc=1, device_id=to_c, device_id_type=MESH)

    reduce_mo = NarrowReduce(mlp_part, 1, MO)
    pl.semaphore_wait(credit.at[0], 1)
    links.sent_all(reduce_nt.core)
    links.sent(reduce_nt.far)
    reduce_mo.start()
    down.release()
    reduce_down.compute(lambda cols: ACT[..., cols].reshape(4 * T, quart), lambda: MG[...].reshape(4 * T, D))
    reduce_down.start()
    reduce_up.middle()

    reduce_nt.far.wait_recv()
    links.sent_all(reduce_mo.core)
    SM[...] = jnp.zeros_like(SM)

    def norm_two_back(i):
        rows = aligned(i * step_rows, step_rows)
        dy = NG[rows, :] + YR[0, rows, :].astype(f32)
        v = RT[rows, :].astype(f32) + AO[rows, :]
        s2 = R2[rows, :]
        dyg = dy * r["GN"][1:2]
        mean = jnp.mean(dyg * v, axis=-1, keepdims=True)
        grad = s2 * dyg - v * (s2 * s2 * s2 * mean)
        SM[1:2] += jnp.sum(dy * (v * s2), axis=0, keepdims=True)
        NG[rows, :] = grad
        PS[0, rows, :] = (GATE[rows, :] * OG[rows, :].astype(f32) + grad).astype(bf16)

    loop(4, norm_two_back)

    class AttnReduce:
        def __init__(self, buf, at, k):
            self.buf, self.at, self.k = buf, at, k

        def compute(self, lhs, rhs):
            def step(i):
                cols = aligned(i * quart, quart)
                v = dot(lhs(cols), rhs(), 0, 0)
                self.buf[self.at, pl.ds(i * (A // 4), A // 4)] = v.astype(bf16).reshape(A // 4, 2, 2, RB, D)

            loop(4, step)

        def start(self):
            self.core = [links.go(self.buf.at[self.at, :, :, 1 - c], NT.at[self.k], to_c)]

        def part(self, zz, xx, cols=None):
            if cols is None:
                return self.buf.at[self.at, zz, xx, c]
            return self.buf.at[self.at, zz, xx, c, :, aligned(cols * half, half)]

        def first(self):
            self.core[0].wait_recv()

            def step(i):
                p = self.buf.at[self.at, i // 2, i % 2, c]
                p[...] = (p[...].astype(f32) + NT[self.k, i // 2, i % 2].astype(f32)).astype(bf16)

            loop(2 * A, step)
            self.one, self.two, self.far = {}, {}, {}
            for dz in range(A):
                d = (dz + 1) % A
                zz = ahead[d]
                if d < A // 2:
                    self.one[d] = links.go(self.part(zz, 1 - x), r["XRA"].at[self.k, d], to_x)
                else:
                    e = d - A // 2
                    cols = aligned((1 - y) * half, half)
                    self.one[d] = links.go(self.buf.at[self.at, zz, :, c, :, cols], r["YRB"].at[self.k, e], to_y)

        def add(self, p, q):
            p[...] = (p[...].astype(f32) + q[...].astype(f32)).astype(bf16)

        def second(self):
            for dz in range(A):
                d = (dz + 1) % A
                zz = ahead[d]
                self.one[d].wait_recv()
                if d < A // 2:
                    self.add(self.part(zz, x), r["XRA"].at[self.k, d])
                    self.two[d] = links.go(self.part(zz, x, 1 - y), r["YRA"].at[self.k, d], to_y)
                else:
                    e = d - A // 2
                    p = self.buf.at[self.at, zz, :, c, :, aligned(y * half, half)]
                    self.add(p, r["YRB"].at[self.k, e])
                    self.two[d] = links.go(self.part(zz, 1 - x, y), r["XRB"].at[self.k, e], to_x)

        def third(self):
            for dz in range(A):
                d = (dz + 1) % A
                zz = ahead[d]
                self.two[d].wait_recv()
                p = self.part(zz, x, y)
                self.add(p, r["YRA"].at[self.k, d] if d < A // 2 else r["XRB"].at[self.k, d - A // 2])
                if d:
                    self.far[d] = links.go(p, r["ZR"].at[self.k, d - 1], dev(zz, x, y, c))

        def fin(self, yy):
            return r["FINA"].at[self.k, c, :, aligned(yy * half, half)]

        def last(self):
            total = self.part(z, x, y)[...].astype(f32)
            for d in range(1, A):
                self.far[d].wait_recv()
                total = total + r["ZR"][self.k, d - 1].astype(f32)
            p = self.fin(y)
            p[...] = total.astype(bf16)
            self.core.append(links.go(p, p, to_c))
            self.yy = links.go(p, p, to_y)

        def finish(self):
            self.yy.wait_recv()
            p = self.fin(1 - y)
            self.core.append(links.go(p, p, to_c))
            for copy in self.core[1:]:
                copy.wait_recv()

    reduce_o = AttnReduce(ACT, 0, 3)
    reduce_v = AttnReduce(ACT, 1, 2)
    reduce_k = AttnReduce(DG, 0, 1)
    reduce_q = AttnReduce(DG, 1, 0)
    reduce_o.compute(lambda cols: QKVM[3, :, cols], lambda: PS[0])
    pl.semaphore_wait(credit.at[1], 1)
    reduce_o.start()

    def mixed_back(j):
        rows = WA[3, pl.ds(j * (Wd // 4), Wd // 4)].reshape(quart, D)
        MG[3, :, aligned(j * quart, quart)] = dot(PS[0], rows, 1, 1).astype(bf16)

    share_mg.release()
    loop(4, mixed_back)
    reduce_o.first()
    reduce_down.middle()

    def attend_back(i):
        rows, cols = place(i)
        s = i // (D // LANES)
        q, k, v = QKVM[0, rows, cols], QKVM[1, rows, cols], QKVM[2, rows, cols]
        dm = MG[3, rows, cols]
        dq, dk, dv = [], [], []
        for h in range(2):
            p = softmax_of(s, q, k, h)
            dp = dot(pick(h, dm), v, 1, 1)
            dl = (p * (dp - jnp.sum(p * dp, axis=-1, keepdims=True))).astype(bf16)
            dq.append(dot(dl, k, 1, 0))
            dk.append(dot(dl, q, 0, 0))
            dv.append(dot(p.astype(bf16), dm, 0, 0))
        MG[0, rows, cols] = (jnp.where(low_lanes, dq[0], dq[1]) * scale).astype(bf16)
        MG[1, rows, cols] = (jnp.where(low_lanes, dk[0], dk[1]) * scale).astype(bf16)
        MG[2, rows, cols] = jnp.where(low_lanes, dv[0], dv[1]).astype(bf16)

    loop(pairs, attend_back)
    reduce_up.last()
    reduce_o.second()
    for k, red in ((2, reduce_v), (1, reduce_k), (0, reduce_q)):
        red.compute(lambda cols: N1[:, cols], lambda k=k: MG[k])
        red.start()
    reduce_v.first()
    reduce_k.first()
    reduce_q.first()
    reduce_o.third()
    reduce_up.finish()
    reduce_down.last()

    reduce_mo.far.wait_recv()

    def output_step(i):
        rows = aligned(i * step_rows, step_rows)
        v = RT[rows, :].astype(f32)
        g = OG[rows, :].astype(f32)
        gate = GATE[rows, :]
        branch = AO[rows, :] + MO[rows, :] + YR[1, rows, :].astype(f32)
        lg = jnp.sum(g * branch, axis=-1, keepdims=True) * gate * (1.0 - gate)
        LG[rows, :] = lg
        SM[2:3] += jnp.sum(lg * v, axis=0, keepdims=True)
        QKVM[3, rows, :] = (v + gate * branch).astype(bf16)

    loop(4, output_step)
    new_copy = pltpu.make_async_copy(QKVM.at[3], r["new_rows"], local.at[0])
    new_copy.start()

    reduce_v.second()
    reduce_k.second()
    reduce_q.second()
    reduce_v.third()
    reduce_down.finish()
    reduce_o.last()

    def norm_one_grad(j):
        rows = pl.ds(j * (Wd // 4), Wd // 4)
        v = dot(MG[0], WA[0, rows].reshape(quart, D), 1, 1)
        v = v + dot(MG[1], WA[1, rows].reshape(quart, D), 1, 1)
        v = v + dot(MG[2], WA[2, rows].reshape(quart, D), 1, 1)
        MO[:, aligned(j * quart, quart)] = v

    loop(4, norm_one_grad)

    def norm_one_back(i):
        rows = aligned(i * step_rows, step_rows)
        dy = MO[rows, :]
        v = RT[rows, :].astype(f32)
        s1 = R1[rows, :]
        dyg = dy * r["GN"][0:1]
        mean = jnp.mean(dyg * v, axis=-1, keepdims=True)
        SM[0:1] += jnp.sum(dy * (v * s1), axis=0, keepdims=True)
        grad = s1 * dyg - v * (s1 * s1 * s1 * mean)
        grad = OG[rows, :].astype(f32) + NG[rows, :] + grad + LG[rows, :] * router_row
        QKVM[0, rows, :] = grad.astype(bf16)

    loop(4, norm_one_back)
    grad_copy = pltpu.make_async_copy(QKVM.at[0], r["row_grads"], local.at[1])
    grad_copy.start()

    total = lambda v: jnp.sum(jnp.sum(v, axis=1, keepdims=True), axis=0, keepdims=True)
    chosen = total(jnp.sum(SEGR[...], axis=0)[1:2])
    lanes = lax.broadcasted_iota(jnp.int32, (1, D), 1)
    SM[3:4] = (
        jnp.where(lanes == 0, chosen, 0.0)
        + jnp.where(lanes == 1, total(STAT[1:2]), 0.0)
        + jnp.where(lanes == 2, total(STAT[0:1]), 0.0)
    )
    SMS, SMR, SMZ = r["SMS"], r["SMR"], r["SMZ"]
    sums = [links.go(SM, SMR.at[0], to_c)]
    reduce_k.third()
    sums[0].wait_recv()
    SMS[0] = SM[...] + SMR[0]
    sums.append(links.go(SMS.at[0], SMR.at[1], to_x))
    reduce_q.third()
    reduce_o.finish()
    sums[1].wait_recv()
    SMS[1] = SMS[0] + SMR[1]
    sums.append(links.go(SMS.at[1], SMR.at[2], to_y))
    reduce_v.last()
    sums[2].wait_recv()
    SMZ[z] = SMS[1] + SMR[2]
    sums = [links.go(SMZ.at[z], SMZ.at[z], dev(ahead[dz], x, y, c)) for dz in range(1, A)]
    reduce_k.last()
    reduce_q.last()
    for copy in sums:
        copy.wait_recv()
    r["small"][...] = jnp.sum(SMZ[...], axis=0)
    reduce_v.finish()
    reduce_k.finish()
    reduce_q.finish()
    outs = [
        pltpu.make_async_copy(r["FIN"], r["mlp_grads"], local.at[2]),
        pltpu.make_async_copy(r["FINA"], r["attn_grads"], local.at[3]),
    ]
    for copy in outs:
        copy.start()
    links.drain()
    for copy in outs + [new_copy, grad_copy]:
        copy.wait()
    for k, name in enumerate(DEBUG):
        copy = pltpu.make_async_copy(r[name], r["dbg_" + name], local.at[4])
        copy.start()
        copy.wait()


def scatter_kernel(rows_ref, slots_ref, base_ref, out_ref):
    k = pl.program_id(2)
    size = base_ref.shape[-2]
    cap = slots_ref.shape[-1]
    position = lax.broadcasted_iota(jnp.int32, (size, cap), 0) + k * size
    onehot = jnp.where(slots_ref[0] == position, 1.0, 0.0)
    hit = jnp.max(onehot, axis=-1, keepdims=True) > 0.5
    picked = dot(onehot.astype(bf16), rows_ref[0, 0], 1, 0)
    base = base_ref[0]
    out_ref[0] = jnp.where(hit, picked, base.astype(f32)).astype(bf16)


def scatter_rows(rows, slots, base):
    count, length, width = base.shape
    cap = slots.shape[1]
    size = 512
    return pl.pallas_call(
        scatter_kernel,
        grid=(1, count, length // size),
        out_shape=jax.ShapeDtypeStruct(base.shape, base.dtype),
        in_specs=[
            pl.BlockSpec((1, 1, cap, width), lambda a, s, k: (0, s, 0, 0)),
            pl.BlockSpec((1, 1, cap), lambda a, s, k: (s, 0, 0)),
            pl.BlockSpec((1, size, width), lambda a, s, k: (s, k, 0)),
        ],
        out_specs=pl.BlockSpec((1, size, width), lambda a, s, k: (s, k, 0)),
        compiler_params=pltpu.CompilerParams(vmem_limit_bytes=32 * MIB),
        name="scatter_rows",
    )(rows.reshape(1, count, cap, width), slots.reshape(count, 1, cap), base)


def run_block(mesh, inputs, S, SEQ, CAP, D, R):
    Wd = mesh.shape["wide"]
    A, RB, T = Wd // 2, R // 2, S * CAP
    dims = dict(A=A, R=R, T=T, S=S, CAP=CAP, SEQ=SEQ, D=D, RB=RB)
    out_shapes = {
        "new_rows": ((T, D), bf16),
        "row_grads": ((T, D), bf16),
        "mlp_grads": ((2, 4, R, D), bf16),
        "attn_grads": ((4, 2, RB, D), bf16),
        "small": ((8, D), f32),
    }
    scratch = {
        "WA": ((4, Wd, R, D), bf16),
        "WU": ((A, 2, R, D), bf16),
        "WD": ((A, 2, R, D), bf16),
        "GP": ((Wd, 8, D), f32),
        "GN": ((8, D), f32),
        "NT": ((4, A, 2, RB, D), bf16),
        "MG": ((4, T, D), bf16),
        "ACT": ((2, A, 2, 2, RB, D), bf16),
        "DG": ((2, A, 2, 2, RB, D), bf16),
        "QKVM": ((4, T, D), bf16),
        "N1": ((T, D), bf16),
        "RT": ((T, D), bf16),
        "OG": ((T, D), bf16),
        "AO": ((T, D), f32),
        "NG": ((T, D), f32),
        "MO": ((T, D), f32),
        "PS": ((2, T, D), bf16),
        "PR": ((2, T, D), bf16),
        "YS": ((T, D), bf16),
        "YR": ((2, T, D), bf16),
        "GXR": ((2, A, R, D), bf16),
        "GZR": ((2, A - 1, R, D), bf16),
        "FIN": ((2, 4, R, D), bf16),
        "XRA": ((4, A // 2, RB, D), bf16),
        "YRA": ((4, A // 2, RB, D // 2), bf16),
        "YRB": ((4, A // 2, 2, RB, D // 2), bf16),
        "XRB": ((4, A // 2, RB, D // 2), bf16),
        "ZR": ((4, A - 1, RB, D // 2), bf16),
        "FINA": ((4, 2, RB, D), bf16),
        "GATE": ((T, 1), f32),
        "R1": ((T, 1), f32),
        "R2": ((T, 1), f32),
        "LG": ((T, 1), f32),
        "SEGC": ((S, CAP, LANES), f32),
        "SEGR": ((S, 16, CAP), f32),
        "STAT": ((8, CHUNK), f32),
        "SM": ((8, D), f32),
        "SMS": ((2, 8, D), f32),
        "SMR": ((3, 8, D), f32),
        "SMZ": ((A, 8, D), f32),
    }
    for name in DEBUG:
        out_shapes["dbg_" + name] = scratch[name]
    count = copy_count(A)
    semaphores = {
        "send": pltpu.SemaphoreType.DMA((count,)),
        "recv": pltpu.SemaphoreType.DMA((count,)),
        "local": pltpu.SemaphoreType.DMA((11,)),
        "credit": pltpu.SemaphoreType.REGULAR((2,)),
    }
    in_vmem = ("gains", "router", "slots", "marks")
    hbm, vmem = pl.BlockSpec(memory_space=pl.ANY), pl.BlockSpec(memory_space=pltpu.VMEM)
    names = list(inputs) + list(out_shapes) + list(scratch) + list(semaphores)
    results = pl.pallas_call(
        functools.partial(block_kernel, dims, names),
        out_shape=[jax.ShapeDtypeStruct(*v) for v in out_shapes.values()],
        in_specs=[vmem if k in in_vmem else hbm for k in inputs],
        out_specs=[vmem if k == "small" else hbm for k in out_shapes],
        scratch_shapes=[pltpu.VMEM(*v) for v in scratch.values()] + list(semaphores.values()),
        compiler_params=pltpu.CompilerParams(
            collective_id=0, has_side_effects=True, vmem_limit_bytes=64 * MIB - 65536
        ),
        name="routed_block",
    )(*inputs.values())
    return dict(zip(out_shapes, results))


def body(mesh, block_input, query_weight, key_weight, value_weight, out_weight, up_weight, down_weight,
         attn_gain, mlp_gain, router_weight, slots, segments, pad_mask, cotangent):
    S, SEQ, D = block_input.shape
    CAP = slots.shape[1]
    R, FF = up_weight.shape
    Wd = mesh.shape["wide"]
    w, n = lax.axis_index("wide"), lax.axis_index("narrow")
    part = FF // (4 * Wd)
    assert FF == 4 * D and 2 * S * CAP == D and part == R and mesh.shape["narrow"] == 4
    w_up = lax.dynamic_index_in_dim(up_weight.reshape(R, Wd, 4, part), n, axis=2, keepdims=False)
    shard = jnp.stack([attn_gain, mlp_gain]).astype(f32)
    gains = lax.dynamic_update_slice(jnp.zeros((8, D), f32), shard, (0, w * R))
    marks = jnp.zeros((S, 16, SEQ), bf16)
    marks = marks.at[:, 0].set(segments.astype(bf16)).at[:, 1].set(pad_mask.astype(bf16))
    inputs = {
        "block_input": block_input,
        "cotangent": cotangent,
        "w_query": query_weight,
        "w_key": key_weight,
        "w_value": value_weight,
        "w_out": out_weight,
        "w_up": w_up.reshape(R, D),
        "w_down": down_weight,
        "gains": gains,
        "router": jnp.zeros((16, D), bf16).at[0].set(router_weight),
        "slots": slots.reshape(S, CAP, 1),
        "marks": marks,
    }
    res = run_block(mesh, inputs, S, SEQ, CAP, D, R)
    block_output = scatter_rows(res["new_rows"], slots, block_input)
    input_grad = scatter_rows(res["row_grads"], slots, cotangent)
    small = res["small"]
    attn = res["attn_grads"].reshape(4, R, D).astype(f32)
    mlp = res["mlp_grads"].astype(f32)
    grad_up = mlp[0].reshape(4, R, Wd, part).transpose(1, 2, 0, 3).reshape(R, FF)
    grad_down = mlp[1].reshape(4 * R, D)
    gain_grads = lax.dynamic_slice(small, (0, w * R), (2, R))
    statistics = jnp.stack([small[3, 0] / small[3, 1], small[3, 2] / small[3, 1]])
    result = (block_output, input_grad, attn[0], attn[1], attn[2], attn[3], grad_up, grad_down,
              gain_grads[0], gain_grads[1], small[2], statistics)
    if DEBUG:
        return result, {k: res["dbg_" + k] for k in DEBUG}
    return result


def solution(mesh):
    rows, wide = P(("wide", "narrow")), P("wide")
    return jax.shard_map(
        functools.partial(body, mesh),
        mesh=mesh,
        in_specs=(rows,) + (wide,) * 8 + (P(),) + (rows,) * 4,
        out_specs=(rows, rows) + (wide,) * 8 + (P(), P()),
        check_vma=False,
    )
```

```python
import functools
import math

import jax
import jax.numpy as jnp
from jax import lax
from jax.experimental import pallas as pl
from jax.experimental.pallas import tpu as pltpu
from jax.sharding import PartitionSpec as P

HEADS = 16
HEAD_DIM = 64
EPS = 1e-06
LANES = 128
MESH = pl.DeviceIdType.MESH
f32 = jnp.float32
bf16 = jnp.bfloat16
MIB = 2**20
CHUNK = 512
DEBUG = ()


def dot(a, b, ca, cb):
    return lax.dot_general(a, b, (((ca,), (cb,)), ((), ())), preferred_element_type=f32)


def aligned(start, size):
    return pl.ds(pl.multiple_of(start, size), size)


def loop(count, step):
    def run(i, carry):
        step(i)
        return carry

    lax.fori_loop(0, count, run, 0)


class Links:
    def __init__(self, send, recv):
        self.send, self.recv, self.count, self.open = send, recv, 0, []

    def make(self, src, dst, device):
        i = self.count
        self.count += 1
        return pltpu.make_async_remote_copy(
            src_ref=src,
            dst_ref=dst,
            send_sem=self.send.at[i],
            recv_sem=self.recv.at[i],
            device_id=device,
            device_id_type=MESH,
        )

    def go(self, src, dst, device):
        copy = self.make(src, dst, device)
        copy.start()
        self.open.append(copy)
        return copy

    def sent(self, copy):
        copy.wait_send()
        self.open = [other for other in self.open if other is not copy]

    def sent_all(self, copies):
        for copy in copies:
            self.sent(copy)

    def drain(self):
        for copy in self.open:
            copy.wait_send()
        self.open = []


def copy_count(far):
    near = far - 1
    gather = 2 * (8 * near + 2) + 3 * (2 * near + 1)
    narrow = 2 * 6 + 2 * 3
    reduce_mlp = 2 * (far + near + 3)
    reduce_attn = 4 * (1 + 2 * far + near + 3)
    return gather + narrow + reduce_mlp + reduce_attn + 3 + near


def block_kernel(dims, names, *refs):
    r = dict(zip(names, refs))
    A, R, T, S, CAP, SEQ, D, RB = (
        dims[k] for k in ("A", "R", "T", "S", "CAP", "SEQ", "D", "RB")
    )
    Wd = 2 * A
    half, quart = D // 2, D // 4
    scale = 1.0 / math.sqrt(HEAD_DIM)
    w, n = lax.axis_index("wide"), lax.axis_index("narrow")
    z, x = w // 2, w % 2
    y, c = n // 2, n % 2
    WA, WU, WD, GP = r["WA"], r["WU"], r["WD"], r["GP"]
    NT, MG, ACT, DG = r["NT"], r["MG"], r["ACT"], r["DG"]
    QKVM, N1, RT, OG = r["QKVM"], r["N1"], r["RT"], r["OG"]
    AO, NG, MO = r["AO"], r["NG"], r["MO"]
    PS, PR, YS, YR = r["PS"], r["PR"], r["YS"], r["YR"]
    GATE, R1, R2, LG = r["GATE"], r["R1"], r["R2"], r["LG"]
    SEGC, SEGR, STAT, SM = r["SEGC"], r["SEGR"], r["STAT"], r["SM"]
    local, credit = r["local"], r["credit"]
    links = Links(r["send"], r["recv"])

    def dev(zz, xx, yy, cc):
        return (zz * 2 + xx, yy * 2 + cc)

    to_x, to_y, to_c = dev(z, 1 - x, y, c), dev(z, x, 1 - y, c), dev(z, x, y, 1 - c)
    ahead = [(z + dz) % A for dz in range(A)]
    behind = [(z - dz + A) % A for dz in range(A)]

    own = [
        pltpu.make_async_copy(r["w_query"], WA.at[0, w], local.at[0]),
        pltpu.make_async_copy(r["w_key"], WA.at[1, w], local.at[1]),
        pltpu.make_async_copy(r["w_value"], WA.at[2, w], local.at[2]),
        pltpu.make_async_copy(r["w_out"], WA.at[3, w], local.at[3]),
        pltpu.make_async_copy(r["w_down"].at[aligned(n * R, R)], WD.at[z, x], local.at[5]),
        pltpu.make_async_copy(r["gains"], GP.at[w], local.at[6]),
    ]
    if r["w_up"].shape[1] == D:
        own.append(pltpu.make_async_copy(r["w_up"], WU.at[z, x], local.at[4]))
    else:
        own += [
            pltpu.make_async_copy(
                r["w_up"].at[:, aligned((v * 4 + n) * R, R)], WU.at[z, x, :, pl.ds(v * R, R)], local.at[11 + v]
            )
            for v in range(Wd)
        ]
    for copy in own:
        copy.start()
    fetches = {}

    def fetch(i, slot):
        s, k = i // (SEQ // CHUNK), i % (SEQ // CHUNK)
        return [
            pltpu.make_async_copy(
                r[name].at[s, aligned(k * CHUNK, CHUNK)], QKVM.at[2 * slot + a], local.at[7 + 2 * slot + a]
            )
            for a, name in enumerate(("block_input", "cotangent"))
        ]

    for copy in fetch(0, 0):
        copy.start()
    barrier = pltpu.get_barrier_semaphore()
    peers = [dev(ahead[dz], x, y, c) for dz in range(1, A)] + [to_x, to_y, to_c]
    for peer in peers:
        pl.semaphore_signal(barrier, inc=1, device_id=peer, device_id_type=MESH)
    pl.semaphore_wait(barrier, len(peers))
    for copy in own:
        copy.wait()

    class AttnGather:
        def __init__(self, first, count):
            self.first, self.count = first, count

        def piece(self, zz, xx, yy):
            return WA.at[pl.ds(self.first, self.count), zz * 2 + xx, :, aligned(c * half + yy * quart, quart)]

        def wide_piece(self, zz, xx):
            return WA.at[pl.ds(self.first, self.count), zz * 2 + xx, :, aligned(c * half, half)]

        def start(self):
            p, q = self.piece(z, x, y), self.wide_piece(z, x)
            self.far = {dz: links.go(p, p, dev(ahead[dz], x, y, c)) for dz in range(1, A)}
            self.x0 = links.go(q, q, to_x)
            self.x1, self.y1, self.second, self.core = {}, {}, {}, []

        def to_core(self, p):
            self.core.append(links.go(p, p, to_c))

        def relay(self, dz):
            self.far[dz].wait_recv()
            p = self.piece(behind[dz], x, y)
            self.x1[dz] = links.go(p, p, to_x)
            self.y1[dz] = links.go(p, p, to_y)
            self.to_core(p)

        def relay_own(self):
            self.x0.wait_recv()
            self.to_core(self.wide_piece(z, 1 - x))

        def relay_second(self, dz):
            self.x1[dz].wait_recv()
            p = self.piece(behind[dz], 1 - x, y)
            if dz % 2:
                self.second[dz] = links.go(p, p, to_y)
            self.to_core(p)
            self.y1[dz].wait_recv()
            p = self.piece(behind[dz], x, 1 - y)
            if not dz % 2:
                self.second[dz] = links.go(p, p, to_x)
            self.to_core(p)

        def relay_third(self, dz):
            self.second[dz].wait_recv()
            self.to_core(self.piece(behind[dz], 1 - x, 1 - y))

        def finish(self):
            for copy in self.core:
                copy.wait_recv()

    class WideGather:
        def __init__(self, at):
            self.at = at

        def start(self):
            p = self.at(z, x)
            self.far = {dz: links.go(p, p, dev(ahead[dz], x, y, c)) for dz in range(1, A)}
            self.near = [links.go(p, p, to_x)]

        def relay(self, dz):
            self.far[dz].wait_recv()
            p = self.at(behind[dz], x)
            self.near.append(links.go(p, p, to_x))

        def finish(self):
            for copy in self.near:
                copy.wait_recv()

        def release(self):
            links.sent_all(list(self.far.values()) + self.near)

    gains = WideGather(lambda zz, xx: GP.at[zz * 2 + xx])
    qkv, out = AttnGather(0, 3), AttnGather(3, 1)
    up = WideGather(lambda zz, xx: WU.at[zz, xx])
    down = WideGather(lambda zz, xx: WD.at[zz, xx])
    gains.start()
    qkv.start()
    out.start()

    AO[...] = jnp.zeros_like(AO)
    NG[...] = jnp.zeros_like(NG)
    SEGC[...] = jnp.zeros_like(SEGC)
    SEGR[...] = jnp.zeros_like(SEGR)
    STAT[...] = jnp.zeros_like(STAT)
    eye = lax.broadcasted_iota(jnp.int32, (CAP, CAP), 0) == lax.broadcasted_iota(jnp.int32, (CAP, CAP), 1)
    for s in range(S):
        row = r["slots"][s : s + 1, :].astype(f32)
        r["SLOT"][s] = jnp.sum(jnp.where(eye, row, 0.0), axis=1, keepdims=True).astype(jnp.int32)
    router_row = r["router"][...].astype(f32)
    router_tile = jnp.broadcast_to(router_row, (16, D)).astype(bf16)
    steps = S * (SEQ // CHUNK)

    def gather_step(i):
        slot = i % 2
        s, k = i // (SEQ // CHUNK), i % (SEQ // CHUNK)

        @pl.when(i + 1 < steps)
        def _():
            for copy in fetch(i + 1, (i + 1) % 2):
                copy.start()

        for copy in fetch(i, slot):
            copy.wait()
        position = lax.broadcasted_iota(jnp.int32, (CAP, CHUNK), 1) + k * CHUNK
        onehot = jnp.where(r["SLOT"][s] == position, 1.0, 0.0).astype(bf16)
        rows = aligned(s * CAP, CAP)
        tokens = QKVM[2 * slot]
        AO[rows, :] += dot(onehot, tokens, 1, 0)
        NG[rows, :] += dot(onehot, QKVM[2 * slot + 1], 1, 0)
        at = (pl.ds(s, 1), aligned(k * CHUNK, CHUNK))
        segment, mask = r["segments"][at].astype(f32), r["pad_mask"][at].astype(f32)
        line = lax.broadcasted_iota(jnp.int32, (16, CHUNK), 0)
        marks = jnp.where(line == 0, segment, jnp.where(line == 1, mask, 0.0)).astype(bf16)
        gate_logits = dot(router_tile, tokens, 1, 1)[0:1]
        STAT[0:1] += mask * jax.nn.sigmoid(gate_logits)
        STAT[1:2] += mask
        SEGR[s] += dot(marks, onehot, 1, 1)
        SEGC[s] += dot(onehot, jnp.broadcast_to(segment, (LANES, CHUNK)).astype(bf16), 1, 1)

    loop(steps, gather_step)

    step_rows = T // 4

    def gate_step(i):
        rows = aligned(i * step_rows, step_rows)
        v, g = AO[rows, :], NG[rows, :]
        gate = jax.nn.sigmoid(jnp.sum(v * router_row, axis=-1, keepdims=True))
        GATE[rows, :] = gate
        R1[rows, :] = lax.rsqrt(jnp.mean(v * v, axis=-1, keepdims=True) + EPS)
        RT[rows, :] = v.astype(bf16)
        OG[rows, :] = g.astype(bf16)
        MG[n, rows, :] = (gate * g).astype(bf16)

    loop(4, gate_step)

    class RowShare:
        def __init__(self, at):
            self.at = at

        def start(self, k):
            p = self.at(n, k)
            self.core = getattr(self, "core", {})
            self.far = getattr(self, "far", {})
            self.core[k] = links.go(p, p, to_c)
            self.far[k] = links.go(p, p, to_y)

        def relay(self, k):
            self.far[k].wait_recv()
            p = self.at((1 - y) * 2 + c, k)
            self.last = getattr(self, "last", {})
            self.last[k] = links.go(p, p, to_c)

        def release(self):
            for copies in (self.core, self.far, self.last):
                links.sent_all(list(copies.values()))

    rows_half = T // 2
    share_mg = RowShare(lambda b, k: MG.at[b, pl.ds(k * rows_half, rows_half)])
    share_nt = RowShare(lambda b, k: NT.at[b, pl.ds(k * (A // 2), A // 2)])

    for dz in range(1, A):
        gains.relay(dz)
    for dz in range(1, A):
        qkv.relay(dz)
    up.start()
    for dz in range(1, A):
        out.relay(dz)
    share_mg.start(0)
    gains.finish()
    gain_rows = jnp.sum(GP[...], axis=0)
    r["GN"][...] = gain_rows

    def norm_one_step(i):
        rows = aligned(i * step_rows, step_rows)
        N1[rows, :] = (RT[rows, :].astype(f32) * R1[rows, :] * r["GN"][0:1]).astype(bf16)

    loop(4, norm_one_step)
    qkv.relay_own()
    for dz in range(1, A):
        qkv.relay_second(dz)
    out.relay_own()
    for dz in range(1, A):
        qkv.relay_third(dz)
    qkv.finish()

    def project(i):
        cols = aligned((i % 4) * quart, quart)
        g = i // 4
        QKVM[g, :, cols] = dot(N1[...], WA[g, :, :, cols].reshape(D, quart), 1, 0).astype(bf16)

    loop(12, project)
    for dz in range(1, A):
        out.relay_second(dz)
    for dz in range(1, A):
        out.relay_third(dz)
    for dz in range(1, A):
        up.relay(dz)
    down.start()

    lane = lax.broadcasted_iota(jnp.int32, (1, LANES), 1)
    low_lanes = lane < HEAD_DIM
    causal = lax.broadcasted_iota(jnp.int32, (CAP, CAP), 0) >= lax.broadcasted_iota(jnp.int32, (CAP, CAP), 1)

    def pick(h, v):
        return jnp.where(low_lanes if h == 0 else ~low_lanes, v, jnp.zeros_like(v))

    def place(i):
        return aligned((i // (D // LANES)) * CAP, CAP), aligned((i % (D // LANES)) * LANES, LANES)

    def softmax_of(s, q, k, h):
        logits = dot(pick(h, q), k, 1, 1) * scale
        same = SEGC[s][:, 0:1] == SEGR[s][0:1]
        logits = jnp.where(causal & same, logits, -1e30)
        e = jnp.exp(logits - jnp.max(logits, axis=-1, keepdims=True))
        return e * (1.0 / jnp.sum(e, axis=-1, keepdims=True))

    def attend(i):
        rows, cols = place(i)
        s = i // (D // LANES)
        q, k, v = QKVM[0, rows, cols], QKVM[1, rows, cols], QKVM[2, rows, cols]
        o = [dot(softmax_of(s, q, k, h).astype(bf16), v, 1, 0) for h in range(2)]
        QKVM[3, rows, cols] = jnp.where(low_lanes, o[0], o[1]).astype(bf16)

    pairs = S * (D // LANES)
    loop(pairs, attend)
    out.finish()

    def project_out(i):
        cols = aligned(i * quart, quart)
        AO[:, cols] = dot(QKVM[3], WA[3, :, :, cols].reshape(D, quart), 1, 0)

    loop(4, project_out)

    def norm_two(k):
        def step(i):
            rows = aligned(k * rows_half + i * (rows_half // 2), rows_half // 2)
            v = RT[rows, :].astype(f32) + AO[rows, :]
            scale_two = lax.rsqrt(jnp.mean(v * v, axis=-1, keepdims=True) + EPS)
            R2[rows, :] = scale_two
            part = (v * scale_two * r["GN"][1:2]).astype(bf16)
            NT[n, pl.ds(k * (A // 2) + i * (A // 4), A // 4)] = part.reshape(A // 4, 2, RB, D)

        loop(2, step)

    for k in range(2):
        norm_two(k)
        share_nt.start(k)
    share_mg.start(1)

    def block_of(ref, b):
        return ref.at[b // 2, pl.ds((b % 2) * (A // 2), A // 2)]

    tanh_k = math.sqrt(2.0 / math.pi)

    def up_block(b):
        rows = NT[b].reshape(T, D)

        def step(i):
            cols = aligned(i * quart, quart)
            v = dot(NT[b].reshape(T, D), WU[:, :, :, cols].reshape(D, quart), 1, 0)
            vv = v * v
            t = jnp.tanh(tanh_k * v * (1.0 + 0.044715 * vv))
            act = 0.5 * v * (1.0 + t)
            slope = 0.5 * (1.0 + t) + 0.5 * v * (1.0 - t * t) * (tanh_k * (1.0 + 0.134145 * vv))
            block_of(ACT, b)[..., cols] = act.astype(bf16).reshape(A // 2, 2, 2, RB, quart)
            block_of(DG, b)[..., cols] = slope.astype(bf16).reshape(A // 2, 2, 2, RB, quart)

        loop(4, step)

    up.finish()
    up_block(n)
    for k in range(2):
        share_nt.core[k].wait_recv()
    up_block(y * 2 + 1 - c)
    for dz in range(1, A):
        down.relay(dz)
    for k in range(2):
        share_mg.relay(k) if k == 0 else None
        share_nt.relay(k)
    share_mg.relay(1)
    up_block((1 - y) * 2 + c)
    for k in range(2):
        share_nt.last[k].wait_recv()
    up_block((1 - y) * 2 + 1 - c)
    for k in range(2):
        share_mg.core[k].wait_recv()
        share_mg.last[k].wait_recv()
    down.finish()

    def act_grad_step(i):
        b, j = i // 4, i % 4
        cols = aligned(j * quart, quart)
        rows = WD[pl.ds(j * (A // 4), A // 4)].reshape(quart, D)
        v = dot(MG[b], rows, 1, 1)
        at = block_of(DG, b)
        slope = at[..., cols].reshape(T, quart).astype(f32)
        at[..., cols] = (v * slope).astype(bf16).reshape(A // 2, 2, 2, RB, quart)

    loop(16, act_grad_step)

    class NarrowReduce:
        def __init__(self, part, k, total):
            self.part, self.k, self.total = part, k, total

        def run(self, b, store):
            def step(j):
                cols = aligned(j * quart, quart)
                store(cols, self.part(b, j))

            loop(4, step)

        def start(self):
            self.core = []
            for q, yy in enumerate((1 - y, y)):

                def put(cols, v, q=q):
                    PS[q, :, cols] = v.astype(bf16)

                self.run(yy * 2 + 1 - c, put)
                self.core.append(links.go(PS.at[q], PR.at[q], to_c))
            self.core[0].wait_recv()

            def put_far(cols, v):
                YS[:, cols] = (v + PR[0, :, cols].astype(f32)).astype(bf16)

            self.run((1 - y) * 2 + c, put_far)
            self.far = links.go(YS, YR.at[self.k], to_y)
            self.core[1].wait_recv()

            def put_own(cols, v):
                self.total[:, cols] = v + PR[1, :, cols].astype(f32)

            self.run(n, put_own)

    def norm_two_part(b, j):
        rows = WU[pl.ds(j * (A // 4), A // 4)].reshape(quart, D)
        return dot(block_of(DG, b)[...].reshape(T, D), rows, 1, 1)

    def mlp_part(b, j):
        cols = aligned(j * quart, quart)
        return dot(block_of(ACT, b)[...].reshape(T, D), WD[:, :, :, cols].reshape(D, quart), 1, 0)

    reduce_nt = NarrowReduce(norm_two_part, 0, NG)
    reduce_nt.start()
    pl.semaphore_signal(credit.at[0], inc=1, device_id=to_c, device_id_type=MESH)

    class WideReduce:
        def __init__(self, grad, k):
            self.grad, self.k = grad, k

        def compute(self, lhs, rhs):
            def step(i):
                cols = aligned(i * quart, quart)
                v = dot(lhs(cols), rhs(), 0, 0)
                self.grad[pl.ds(i * (A // 4), A // 4)] = v.astype(bf16).reshape(A // 4, 2, R, D)

            loop(4, step)

        def start(self):
            self.x = {}
            for dz in list(range(1, A)) + [0]:
                self.x[dz] = links.go(self.grad.at[ahead[dz], 1 - x], r["GXR"].at[self.k, dz], to_x)

        def middle(self):
            self.far = {}
            for dz in list(range(1, A)) + [0]:
                self.x[dz].wait_recv()
                p = self.grad.at[ahead[dz], x]
                p[...] = (p[...].astype(f32) + r["GXR"][self.k, dz].astype(f32)).astype(bf16)
                if dz:
                    self.far[dz] = links.go(p, r["GZR"].at[self.k, dz - 1], dev(ahead[dz], x, y, c))

        def last(self):
            total = self.grad[z, x].astype(f32)
            for dz in range(1, A):
                self.far[dz].wait_recv()
                total = total + r["GZR"][self.k, dz - 1].astype(f32)
            r["FIN"][self.k, n] = total.astype(bf16)
            p = r["FIN"].at[self.k, n]
            self.core = [links.go(p, p, to_c)]
            self.yy = links.go(p, p, to_y)

        def finish(self):
            self.yy.wait_recv()
            p = r["FIN"].at[self.k, (1 - y) * 2 + c]
            self.core.append(links.go(p, p, to_c))
            for copy in self.core:
                copy.wait_recv()

    reduce_up, reduce_down = WideReduce(WU, 0), WideReduce(WD, 1)
    up.release()
    reduce_up.compute(lambda cols: NT[..., cols].reshape(4 * T, quart), lambda: DG[...].reshape(4 * T, D))
    reduce_up.start()
    share_nt.release()
    pl.semaphore_signal(credit.at[1], inc=1, device_id=to_c, device_id_type=MESH)

    reduce_mo = NarrowReduce(mlp_part, 1, MO)
    pl.semaphore_wait(credit.at[0], 1)
    links.sent_all(reduce_nt.core)
    links.sent(reduce_nt.far)
    reduce_mo.start()
    down.release()
    reduce_down.compute(lambda cols: ACT[..., cols].reshape(4 * T, quart), lambda: MG[...].reshape(4 * T, D))
    reduce_down.start()
    reduce_up.middle()

    reduce_nt.far.wait_recv()
    links.sent_all(reduce_mo.core)
    SM[...] = jnp.zeros_like(SM)

    def norm_two_back(i):
        rows = aligned(i * step_rows, step_rows)
        dy = NG[rows, :] + YR[0, rows, :].astype(f32)
        v = RT[rows, :].astype(f32) + AO[rows, :]
        s2 = R2[rows, :]
        dyg = dy * r["GN"][1:2]
        mean = jnp.mean(dyg * v, axis=-1, keepdims=True)
        grad = s2 * dyg - v * (s2 * s2 * s2 * mean)
        SM[1:2] += jnp.sum(dy * (v * s2), axis=0, keepdims=True)
        NG[rows, :] = grad
        PS[0, rows, :] = (GATE[rows, :] * OG[rows, :].astype(f32) + grad).astype(bf16)

    loop(4, norm_two_back)

    class AttnReduce:
        def __init__(self, buf, at, k):
            self.buf, self.at, self.k = buf, at, k

        def compute(self, lhs, rhs):
            def step(i):
                cols = aligned(i * quart, quart)
                v = dot(lhs(cols), rhs(), 0, 0)
                self.buf[self.at, pl.ds(i * (A // 4), A // 4)] = v.astype(bf16).reshape(A // 4, 2, 2, RB, D)

            loop(4, step)

        def start(self):
            self.core = [links.go(self.buf.at[self.at, :, :, 1 - c], NT.at[self.k], to_c)]

        def part(self, zz, xx, cols=None):
            if cols is None:
                return self.buf.at[self.at, zz, xx, c]
            return self.buf.at[self.at, zz, xx, c, :, aligned(cols * half, half)]

        def first(self):
            self.core[0].wait_recv()

            def step(i):
                p = self.buf.at[self.at, i // 2, i % 2, c]
                p[...] = (p[...].astype(f32) + NT[self.k, i // 2, i % 2].astype(f32)).astype(bf16)

            loop(2 * A, step)
            self.one, self.two, self.far = {}, {}, {}
            for dz in range(A):
                d = (dz + 1) % A
                zz = ahead[d]
                if d < A // 2:
                    self.one[d] = links.go(self.part(zz, 1 - x), r["XRA"].at[self.k, d], to_x)
                else:
                    e = d - A // 2
                    cols = aligned((1 - y) * half, half)
                    self.one[d] = links.go(self.buf.at[self.at, zz, :, c, :, cols], r["YRB"].at[self.k, e], to_y)

        def add(self, p, q):
            p[...] = (p[...].astype(f32) + q[...].astype(f32)).astype(bf16)

        def second(self):
            for dz in range(A):
                d = (dz + 1) % A
                zz = ahead[d]
                self.one[d].wait_recv()
                if d < A // 2:
                    self.add(self.part(zz, x), r["XRA"].at[self.k, d])
                    self.two[d] = links.go(self.part(zz, x, 1 - y), r["YRA"].at[self.k, d], to_y)
                else:
                    e = d - A // 2
                    p = self.buf.at[self.at, zz, :, c, :, aligned(y * half, half)]
                    self.add(p, r["YRB"].at[self.k, e])
                    self.two[d] = links.go(self.part(zz, 1 - x, y), r["XRB"].at[self.k, e], to_x)

        def third(self):
            for dz in range(A):
                d = (dz + 1) % A
                zz = ahead[d]
                self.two[d].wait_recv()
                p = self.part(zz, x, y)
                self.add(p, r["YRA"].at[self.k, d] if d < A // 2 else r["XRB"].at[self.k, d - A // 2])
                if d:
                    self.far[d] = links.go(p, r["ZR"].at[self.k, d - 1], dev(zz, x, y, c))

        def fin(self, yy):
            return r["FINA"].at[self.k, c, :, aligned(yy * half, half)]

        def last(self):
            total = self.part(z, x, y)[...].astype(f32)
            for d in range(1, A):
                self.far[d].wait_recv()
                total = total + r["ZR"][self.k, d - 1].astype(f32)
            p = self.fin(y)
            p[...] = total.astype(bf16)
            self.core.append(links.go(p, p, to_c))
            self.yy = links.go(p, p, to_y)

        def finish(self):
            self.yy.wait_recv()
            p = self.fin(1 - y)
            self.core.append(links.go(p, p, to_c))
            for copy in self.core[1:]:
                copy.wait_recv()

    reduce_o = AttnReduce(ACT, 0, 3)
    reduce_v = AttnReduce(ACT, 1, 2)
    reduce_k = AttnReduce(DG, 0, 1)
    reduce_q = AttnReduce(DG, 1, 0)
    reduce_o.compute(lambda cols: QKVM[3, :, cols], lambda: PS[0])
    pl.semaphore_wait(credit.at[1], 1)
    reduce_o.start()

    def mixed_back(j):
        rows = WA[3, pl.ds(j * (Wd // 4), Wd // 4)].reshape(quart, D)
        MG[3, :, aligned(j * quart, quart)] = dot(PS[0], rows, 1, 1).astype(bf16)

    share_mg.release()
    loop(4, mixed_back)
    reduce_o.first()
    reduce_down.middle()

    def attend_back(i):
        rows, cols = place(i)
        s = i // (D // LANES)
        q, k, v = QKVM[0, rows, cols], QKVM[1, rows, cols], QKVM[2, rows, cols]
        dm = MG[3, rows, cols]
        dq, dk, dv = [], [], []
        for h in range(2):
            p = softmax_of(s, q, k, h)
            dp = dot(pick(h, dm), v, 1, 1)
            dl = (p * (dp - jnp.sum(p * dp, axis=-1, keepdims=True))).astype(bf16)
            dq.append(dot(dl, k, 1, 0))
            dk.append(dot(dl, q, 0, 0))
            dv.append(dot(p.astype(bf16), dm, 0, 0))
        MG[0, rows, cols] = (jnp.where(low_lanes, dq[0], dq[1]) * scale).astype(bf16)
        MG[1, rows, cols] = (jnp.where(low_lanes, dk[0], dk[1]) * scale).astype(bf16)
        MG[2, rows, cols] = jnp.where(low_lanes, dv[0], dv[1]).astype(bf16)

    loop(pairs, attend_back)
    reduce_up.last()
    reduce_o.second()
    for k, red in ((2, reduce_v), (1, reduce_k), (0, reduce_q)):
        red.compute(lambda cols: N1[:, cols], lambda k=k: MG[k])
        red.start()
    reduce_v.first()
    reduce_k.first()
    reduce_q.first()
    reduce_o.third()
    reduce_up.finish()
    reduce_down.last()

    reduce_mo.far.wait_recv()

    def output_step(i):
        rows = aligned(i * step_rows, step_rows)
        v = RT[rows, :].astype(f32)
        g = OG[rows, :].astype(f32)
        gate = GATE[rows, :]
        branch = AO[rows, :] + MO[rows, :] + YR[1, rows, :].astype(f32)
        lg = jnp.sum(g * branch, axis=-1, keepdims=True) * gate * (1.0 - gate)
        LG[rows, :] = lg
        SM[2:3] += jnp.sum(lg * v, axis=0, keepdims=True)
        QKVM[3, rows, :] = (v + gate * branch).astype(bf16)

    loop(4, output_step)
    new_copy = pltpu.make_async_copy(QKVM.at[3], r["new_rows"], local.at[0])
    new_copy.start()

    reduce_v.second()
    reduce_k.second()
    reduce_q.second()
    reduce_v.third()
    reduce_down.finish()
    reduce_o.last()

    def norm_one_grad(j):
        rows = pl.ds(j * (Wd // 4), Wd // 4)
        v = dot(MG[0], WA[0, rows].reshape(quart, D), 1, 1)
        v = v + dot(MG[1], WA[1, rows].reshape(quart, D), 1, 1)
        v = v + dot(MG[2], WA[2, rows].reshape(quart, D), 1, 1)
        MO[:, aligned(j * quart, quart)] = v

    loop(4, norm_one_grad)

    def norm_one_back(i):
        rows = aligned(i * step_rows, step_rows)
        dy = MO[rows, :]
        v = RT[rows, :].astype(f32)
        s1 = R1[rows, :]
        dyg = dy * r["GN"][0:1]
        mean = jnp.mean(dyg * v, axis=-1, keepdims=True)
        SM[0:1] += jnp.sum(dy * (v * s1), axis=0, keepdims=True)
        grad = s1 * dyg - v * (s1 * s1 * s1 * mean)
        grad = OG[rows, :].astype(f32) + NG[rows, :] + grad + LG[rows, :] * router_row
        QKVM[0, rows, :] = grad.astype(bf16)

    loop(4, norm_one_back)
    grad_copy = pltpu.make_async_copy(QKVM.at[0], r["row_grads"], local.at[1])
    grad_copy.start()

    total = lambda v: jnp.sum(jnp.sum(v, axis=1, keepdims=True), axis=0, keepdims=True)
    chosen = total(jnp.sum(SEGR[...], axis=0)[1:2])
    lanes = lax.broadcasted_iota(jnp.int32, (1, D), 1)
    SM[3:4] = (
        jnp.where(lanes == 0, chosen, 0.0)
        + jnp.where(lanes == 1, total(STAT[1:2]), 0.0)
        + jnp.where(lanes == 2, total(STAT[0:1]), 0.0)
    )
    SMS, SMR, SMZ = r["SMS"], r["SMR"], r["SMZ"]
    sums = [links.go(SM, SMR.at[0], to_c)]
    reduce_k.third()
    sums[0].wait_recv()
    SMS[0] = SM[...] + SMR[0]
    sums.append(links.go(SMS.at[0], SMR.at[1], to_x))
    reduce_q.third()
    reduce_o.finish()
    sums[1].wait_recv()
    SMS[1] = SMS[0] + SMR[1]
    sums.append(links.go(SMS.at[1], SMR.at[2], to_y))
    reduce_v.last()
    sums[2].wait_recv()
    SMZ[z] = SMS[1] + SMR[2]
    sums = [links.go(SMZ.at[z], SMZ.at[z], dev(ahead[dz], x, y, c)) for dz in range(1, A)]
    reduce_k.last()
    reduce_q.last()
    for copy in sums:
        copy.wait_recv()
    r["small"][...] = jnp.sum(SMZ[...], axis=0)
    reduce_v.finish()
    reduce_k.finish()
    reduce_q.finish()
    outs = [
        pltpu.make_async_copy(r["FIN"], r["mlp_grads"], local.at[2]),
        pltpu.make_async_copy(r["FINA"], r["attn_grads"], local.at[3]),
    ]
    for copy in outs:
        copy.start()
    links.drain()
    for copy in outs + [new_copy, grad_copy]:
        copy.wait()
    for k, name in enumerate(DEBUG):
        copy = pltpu.make_async_copy(r[name], r["dbg_" + name], local.at[4])
        copy.start()
        copy.wait()


def finish_kernel(dims, slots, rows, row_grads, attn_grads, mlp_grads, small, base, base_grad,
                  out, out_grad, stats, router, gain_one, gain_two, attn_out, up_out, down_out,
                  attn_stage, up_stage, down_stage, sems):
    S, per, R, Wd, part = dims
    i = pl.program_id(0)
    s, k = i // per, i % per
    size, cap = base.shape[1], slots.shape[1]
    position = lax.broadcasted_iota(jnp.int32, (size, cap), 0) + k * size
    onehot = jnp.where(slots[pl.ds(s, 1), :] == position, 1.0, 0.0)
    hit = jnp.max(onehot, axis=-1, keepdims=True) > 0.5
    onehot = onehot.astype(bf16)
    own = aligned(s * cap, cap)
    for new, old, target in ((rows, base, out), (row_grads, base_grad, out_grad)):
        picked = dot(onehot, new[own, :], 1, 0).astype(bf16)
        target[0] = jnp.where(hit, picked, old[0])

    attn_copies = [
        pltpu.make_async_copy(attn_stage.at[g], attn_out[g], sems.at[g]) for g in range(4)
    ]
    down_copies = [
        pltpu.make_async_copy(down_stage.at[q], down_out.at[pl.ds(q * R, R)], sems.at[4 + q]) for q in range(4)
    ]
    up_copy = pltpu.make_async_copy(up_stage, up_out, sems.at[8])

    @pl.when(i == 0)
    def _():
        for g in range(4):
            attn_stage[g] = attn_grads[g].astype(f32)
            attn_copies[g].start()
        w = lax.axis_index("wide")
        gains = pltpu.roll(small[...], (small.shape[1] - w * R) % small.shape[1], 1)
        gain_one[...] = gains[0:1, :R]
        gain_two[...] = gains[1:2, :R]
        router[...] = small[2:3]
        lane = lax.broadcasted_iota(jnp.int32, (1, small.shape[1]), 1)
        counts = small[3:4]
        valid = jnp.sum(jnp.where(lane == 1, counts, 0.0), axis=1, keepdims=True)
        shifted = jnp.where(lane == 1, pltpu.roll(counts, small.shape[1] - 1, 1), counts)
        stats[...] = (shifted / valid)[:, : stats.shape[1]]

    @pl.when(i == 1)
    def _():
        for q in range(4):
            down_stage[q] = mlp_grads[1, q].astype(f32)
            down_copies[q].start()

    @pl.when(i == 2)
    def _():
        for q in range(4):
            for v in range(Wd):
                at = (v * 4 + q) * part
                up_stage[:, at : at + part] = mlp_grads[0, q, :, v * part : (v + 1) * part].astype(f32)
        up_copy.start()

    @pl.when(i == S * per - 1)
    def _():
        for copy in attn_copies + down_copies + [up_copy]:
            copy.wait()


def finish(mesh, res, slots, block_input, cotangent, R, FF):
    S, SEQ, D = block_input.shape
    Wd = mesh.shape["wide"]
    size = 256
    per, part = SEQ // size, FF // (4 * Wd)

    def kernel(slots, rows, row_grads, attn, mlp, small, base, base_grad, out, out_grad, stats, router,
               gain_one, gain_two, q, k, v, o, up, down, *scratch):
        finish_kernel((S, per, R, Wd, part), slots, rows, row_grads, attn, mlp, small, base, base_grad,
                      out, out_grad, stats, router, gain_one, gain_two, (q, k, v, o), up, down, *scratch)

    vmem, hbm = pl.BlockSpec(memory_space=pltpu.VMEM), pl.BlockSpec(memory_space=pl.ANY)
    tile = pl.BlockSpec((1, size, D), lambda i: (i // per, i % per, 0))
    shape = jax.ShapeDtypeStruct
    return pl.pallas_call(
        kernel,
        grid=(S * per,),
        out_shape=[shape(block_input.shape, bf16)] * 2
        + [shape((1, 2), f32), shape((1, D), f32), shape((1, R), f32), shape((1, R), f32)]
        + [shape((R, D), f32)] * 4
        + [shape((R, FF), f32), shape((4 * R, D), f32)],
        in_specs=[vmem] * 6 + [tile] * 2,
        out_specs=[tile] * 2 + [vmem] * 4 + [hbm] * 6,
        scratch_shapes=[
            pltpu.VMEM((4, R, D), f32),
            pltpu.VMEM((R, FF), f32),
            pltpu.VMEM((4, R, D), f32),
            pltpu.SemaphoreType.DMA((9,)),
        ],
        compiler_params=pltpu.CompilerParams(vmem_limit_bytes=60 * MIB),
        name="finish_rows",
    )(slots, res["new_rows"], res["row_grads"], res["attn_grads"].reshape(4, R, D), res["mlp_grads"],
      res["small"], block_input, cotangent)


def run_block(mesh, inputs, S, SEQ, CAP, D, R):
    Wd = mesh.shape["wide"]
    A, RB, T = Wd // 2, R // 2, S * CAP
    dims = dict(A=A, R=R, T=T, S=S, CAP=CAP, SEQ=SEQ, D=D, RB=RB)
    out_shapes = {
        "new_rows": ((T, D), bf16),
        "row_grads": ((T, D), bf16),
        "mlp_grads": ((2, 4, R, D), bf16),
        "attn_grads": ((4, 2, RB, D), bf16),
        "small": ((8, D), f32),
    }
    scratch = {
        "WA": ((4, Wd, R, D), bf16),
        "WU": ((A, 2, R, D), bf16),
        "WD": ((A, 2, R, D), bf16),
        "GP": ((Wd, 8, D), f32),
        "GN": ((8, D), f32),
        "NT": ((4, A, 2, RB, D), bf16),
        "MG": ((4, T, D), bf16),
        "ACT": ((2, A, 2, 2, RB, D), bf16),
        "DG": ((2, A, 2, 2, RB, D), bf16),
        "QKVM": ((4, T, D), bf16),
        "N1": ((T, D), bf16),
        "RT": ((T, D), bf16),
        "OG": ((T, D), bf16),
        "AO": ((T, D), f32),
        "NG": ((T, D), f32),
        "MO": ((T, D), f32),
        "PS": ((2, T, D), bf16),
        "PR": ((2, T, D), bf16),
        "YS": ((T, D), bf16),
        "YR": ((2, T, D), bf16),
        "GXR": ((2, A, R, D), bf16),
        "GZR": ((2, A - 1, R, D), bf16),
        "FIN": ((2, 4, R, D), bf16),
        "XRA": ((4, A // 2, RB, D), bf16),
        "YRA": ((4, A // 2, RB, D // 2), bf16),
        "YRB": ((4, A // 2, 2, RB, D // 2), bf16),
        "XRB": ((4, A // 2, RB, D // 2), bf16),
        "ZR": ((4, A - 1, RB, D // 2), bf16),
        "FINA": ((4, 2, RB, D), bf16),
        "GATE": ((T, 1), f32),
        "R1": ((T, 1), f32),
        "R2": ((T, 1), f32),
        "LG": ((T, 1), f32),
        "SLOT": ((S, CAP, 1), jnp.int32),
        "SEGC": ((S, CAP, LANES), f32),
        "SEGR": ((S, 16, CAP), f32),
        "STAT": ((8, CHUNK), f32),
        "SM": ((8, D), f32),
        "SMS": ((2, 8, D), f32),
        "SMR": ((3, 8, D), f32),
        "SMZ": ((A, 8, D), f32),
    }
    for name in DEBUG:
        out_shapes["dbg_" + name] = scratch[name]
    count = copy_count(A)
    semaphores = {
        "send": pltpu.SemaphoreType.DMA((count,)),
        "recv": pltpu.SemaphoreType.DMA((count,)),
        "local": pltpu.SemaphoreType.DMA((11 + Wd,)),
        "credit": pltpu.SemaphoreType.REGULAR((2,)),
    }
    in_vmem = ("gains", "router", "slots", "segments", "pad_mask")
    hbm, vmem = pl.BlockSpec(memory_space=pl.ANY), pl.BlockSpec(memory_space=pltpu.VMEM)
    names = list(inputs) + list(out_shapes) + list(scratch) + list(semaphores)
    results = pl.pallas_call(
        functools.partial(block_kernel, dims, names),
        out_shape=[jax.ShapeDtypeStruct(*v) for v in out_shapes.values()],
        in_specs=[vmem if k in in_vmem else hbm for k in inputs],
        out_specs=[vmem if k == "small" else hbm for k in out_shapes],
        scratch_shapes=[pltpu.VMEM(*v) for v in scratch.values()] + list(semaphores.values()),
        compiler_params=pltpu.CompilerParams(
            collective_id=0, has_side_effects=True, vmem_limit_bytes=64 * MIB - 65536
        ),
        name="routed_block",
    )(*inputs.values())
    return dict(zip(out_shapes, results))


def body(mesh, block_input, query_weight, key_weight, value_weight, out_weight, up_weight, down_weight,
         attn_gain, mlp_gain, router_weight, slots, segments, pad_mask, cotangent):
    S, SEQ, D = block_input.shape
    CAP = slots.shape[1]
    R, FF = up_weight.shape
    Wd = mesh.shape["wide"]
    w, n = lax.axis_index("wide"), lax.axis_index("narrow")
    part = FF // (4 * Wd)
    assert FF == 4 * D and 2 * S * CAP == D and part == R and mesh.shape["narrow"] == 4
    if part % LANES:
        up_weight = lax.dynamic_index_in_dim(up_weight.reshape(R, Wd, 4, part), n, axis=2, keepdims=False)
        up_weight = up_weight.reshape(R, D)
    shard = jnp.stack([attn_gain, mlp_gain]).astype(f32)
    gains = lax.dynamic_update_slice(jnp.zeros((8, D), f32), shard, (0, w * R))
    inputs = {
        "block_input": block_input,
        "cotangent": cotangent,
        "w_query": query_weight,
        "w_key": key_weight,
        "w_value": value_weight,
        "w_out": out_weight,
        "w_up": up_weight,
        "w_down": down_weight,
        "gains": gains,
        "router": router_weight.reshape(1, D),
        "slots": slots,
        "segments": segments,
        "pad_mask": pad_mask,
    }
    res = run_block(mesh, inputs, S, SEQ, CAP, D, R)
    outs = finish(mesh, res, slots, block_input, cotangent, R, FF)
    result = (outs[0], outs[1], *outs[6:], outs[4].reshape(R), outs[5].reshape(R), outs[3].reshape(D), outs[2].reshape(2))
    if DEBUG:
        return result, {k: res["dbg_" + k] for k in DEBUG}
    return result


def solution(mesh):
    rows, wide = P(("wide", "narrow")), P("wide")
    return jax.shard_map(
        functools.partial(body, mesh),
        mesh=mesh,
        in_specs=(rows,) + (wide,) * 8 + (P(),) + (rows,) * 4,
        out_specs=(rows, rows) + (wide,) * 8 + (P(), P()),
        check_vma=False,
    )
```

```python
import functools
import math

import jax
import jax.numpy as jnp
from jax import lax
from jax.experimental import pallas as pl
from jax.experimental.pallas import tpu as pltpu
from jax.sharding import PartitionSpec as P

HEADS = 16
HEAD_DIM = 64
EPS = 1e-06
LANES = 128
MESH = pl.DeviceIdType.MESH
f32 = jnp.float32
bf16 = jnp.bfloat16
MIB = 2**20
CHUNK = 512
DEBUG = ()


def dot(a, b, ca, cb):
    return lax.dot_general(a, b, (((ca,), (cb,)), ((), ())), preferred_element_type=f32)


def aligned(start, size):
    return pl.ds(pl.multiple_of(start, size), size)


def loop(count, step):
    def run(i, carry):
        step(i)
        return carry

    lax.fori_loop(0, count, run, 0)


class Column:
    def __init__(self, ref, lane):
        self.ref, self.lane = ref, slice(lane, lane + 1)

    def __getitem__(self, at):
        return self.ref[at[0], self.lane]

    def __setitem__(self, at, value):
        self.ref[at[0], self.lane] = value


class Links:
    def __init__(self, send, recv):
        self.send, self.recv, self.count, self.open = send, recv, 0, []

    def make(self, src, dst, device):
        i = self.count
        self.count += 1
        return pltpu.make_async_remote_copy(
            src_ref=src,
            dst_ref=dst,
            send_sem=self.send.at[i],
            recv_sem=self.recv.at[i],
            device_id=device,
            device_id_type=MESH,
        )

    def go(self, src, dst, device):
        copy = self.make(src, dst, device)
        copy.start()
        self.open.append(copy)
        return copy

    def sent(self, copy):
        copy.wait_send()
        self.open = [other for other in self.open if other is not copy]

    def sent_all(self, copies):
        for copy in copies:
            self.sent(copy)

    def drain(self):
        for copy in self.open:
            copy.wait_send()
        self.open = []


def copy_count(far):
    near = far - 1
    gather = 4 * (8 * near + 2) + 3 * (2 * near + 1)
    narrow = 2 * 6 + 2 * 4
    reduce_mlp = 2 * (far + near + 3)
    reduce_attn = 4 * (1 + 2 * far + near + 3)
    return gather + narrow + reduce_mlp + reduce_attn + 3 + near


def block_kernel(dims, names, *refs):
    r = dict(zip(names, refs))
    A, R, T, S, CAP, SEQ, D, RB = (
        dims[k] for k in ("A", "R", "T", "S", "CAP", "SEQ", "D", "RB")
    )
    Wd = 2 * A
    half, quart = D // 2, D // 4
    scale = 1.0 / math.sqrt(HEAD_DIM)
    w, n = lax.axis_index("wide"), lax.axis_index("narrow")
    z, x = w // 2, w % 2
    y, c = n // 2, n % 2
    WA, WU, WD, GP = r["WA"], r["WU"], r["WD"], r["GP"]
    NT, MG, ACT, DG = r["NT"], r["MG"], r["ACT"], r["DG"]
    QKVM, N1, RT, OG = r["QKVM"], r["N1"], r["RT"], r["OG"]
    AO, NG, MO = r["AO"], r["NG"], r["MO"]
    PS, PR, YS, YR = r["PS"], r["PR"], r["YS"], r["YR"]
    GATE, R1, R2, LG, SLOT = (Column(r["COLS"], k) for k in range(5))
    SEGR, STAT, SM = r["SEGR"], r["STAT"], r["SM"]
    local, credit = r["local"], r["credit"]
    links = Links(r["send"], r["recv"])

    def dev(zz, xx, yy, cc):
        return (zz * 2 + xx, yy * 2 + cc)

    to_x, to_y, to_c = dev(z, 1 - x, y, c), dev(z, x, 1 - y, c), dev(z, x, y, 1 - c)
    ahead = [(z + dz) % A for dz in range(A)]
    behind = [(z - dz + A) % A for dz in range(A)]

    own = [
        pltpu.make_async_copy(r["w_query"], WA.at[0, w], local.at[0]),
        pltpu.make_async_copy(r["w_key"], WA.at[1, w], local.at[1]),
        pltpu.make_async_copy(r["w_value"], WA.at[2, w], local.at[2]),
        pltpu.make_async_copy(r["w_out"], WA.at[3, w], local.at[3]),
        pltpu.make_async_copy(r["w_down"].at[aligned(n * R, R)], WD.at[z, x], local.at[5]),
        pltpu.make_async_copy(r["gains"], GP.at[w], local.at[6]),
    ]
    if r["w_up"].shape[1] == D:
        own.append(pltpu.make_async_copy(r["w_up"], WU.at[z, x], local.at[4]))
    else:
        own += [
            pltpu.make_async_copy(
                r["w_up"].at[:, aligned((v * 4 + n) * R, R)], WU.at[z, x, :, pl.ds(v * R, R)], local.at[11 + v]
            )
            for v in range(Wd)
        ]
    for copy in own:
        copy.start()
    fetches = {}

    def fetch(i, slot):
        s, k = i // (SEQ // CHUNK), i % (SEQ // CHUNK)
        return [
            pltpu.make_async_copy(
                r[name].at[s, aligned(k * CHUNK, CHUNK)], QKVM.at[2 * slot + a], local.at[7 + 2 * slot + a]
            )
            for a, name in enumerate(("block_input", "cotangent"))
        ]

    for copy in fetch(0, 0):
        copy.start()
    barrier = pltpu.get_barrier_semaphore()
    peers = [dev(ahead[dz], x, y, c) for dz in range(1, A)] + [to_x, to_y, to_c]
    for peer in peers:
        pl.semaphore_signal(barrier, inc=1, device_id=peer, device_id_type=MESH)
    pl.semaphore_wait(barrier, len(peers))
    for copy in own:
        copy.wait()

    class AttnGather:
        def __init__(self, first, count):
            self.first, self.count = first, count

        def piece(self, zz, xx, yy):
            return WA.at[pl.ds(self.first, self.count), zz * 2 + xx, :, aligned(c * half + yy * quart, quart)]

        def wide_piece(self, zz, xx):
            return WA.at[pl.ds(self.first, self.count), zz * 2 + xx, :, aligned(c * half, half)]

        def start(self):
            p, q = self.piece(z, x, y), self.wide_piece(z, x)
            self.far = {dz: links.go(p, p, dev(ahead[dz], x, y, c)) for dz in range(1, A)}
            self.x0 = links.go(q, q, to_x)
            self.x1, self.y1, self.second, self.core = {}, {}, {}, []

        def to_core(self, p):
            self.core.append(links.go(p, p, to_c))

        def relay(self, dz):
            self.far[dz].wait_recv()
            p = self.piece(behind[dz], x, y)
            self.x1[dz] = links.go(p, p, to_x)
            self.y1[dz] = links.go(p, p, to_y)
            self.to_core(p)

        def relay_own(self):
            self.x0.wait_recv()
            self.to_core(self.wide_piece(z, 1 - x))

        def relay_second(self, dz):
            self.x1[dz].wait_recv()
            p = self.piece(behind[dz], 1 - x, y)
            if dz % 2:
                self.second[dz] = links.go(p, p, to_y)
            self.to_core(p)
            self.y1[dz].wait_recv()
            p = self.piece(behind[dz], x, 1 - y)
            if not dz % 2:
                self.second[dz] = links.go(p, p, to_x)
            self.to_core(p)

        def relay_third(self, dz):
            self.second[dz].wait_recv()
            self.to_core(self.piece(behind[dz], 1 - x, 1 - y))

        def finish(self):
            for copy in self.core:
                copy.wait_recv()

    class WideGather:
        def __init__(self, at):
            self.at = at

        def start(self):
            p = self.at(z, x)
            self.far = {dz: links.go(p, p, dev(ahead[dz], x, y, c)) for dz in range(1, A)}
            self.near = []

        def start_near(self):
            p = self.at(z, x)
            self.near.append(links.go(p, p, to_x))

        def relay(self, dz):
            self.far[dz].wait_recv()
            p = self.at(behind[dz], x)
            self.near.append(links.go(p, p, to_x))

        def finish(self):
            for copy in self.near:
                copy.wait_recv()

        def release(self):
            links.sent_all(list(self.far.values()) + self.near)

    gains = WideGather(lambda zz, xx: GP.at[zz * 2 + xx])
    query, key, value, out = (AttnGather(g, 1) for g in range(4))
    attn = (query, key, value, out)
    up = WideGather(lambda zz, xx: WU.at[zz, xx])
    down = WideGather(lambda zz, xx: WD.at[zz, xx])
    gains.start()
    gains.start_near()
    for group in attn:
        group.start()
    up.start()
    down.start()

    AO[...] = jnp.zeros_like(AO)
    NG[...] = jnp.zeros_like(NG)
    SEGR[...] = jnp.zeros_like(SEGR)
    STAT[...] = jnp.zeros_like(STAT)
    eye = lax.broadcasted_iota(jnp.int32, (CAP, CAP), 0) == lax.broadcasted_iota(jnp.int32, (CAP, CAP), 1)

    def upright(row):
        return jnp.sum(jnp.where(eye, row, 0.0), axis=1, keepdims=True)

    for s in range(S):
        SLOT[pl.ds(s * CAP, CAP), :] = upright(r["slots"][s : s + 1, :].astype(f32))
    router_row = r["router"][...].astype(f32)
    router_tile = jnp.broadcast_to(router_row, (16, D)).astype(bf16)
    steps = S * (SEQ // CHUNK)

    def gather_step(i):
        slot = i % 2
        s, k = i // (SEQ // CHUNK), i % (SEQ // CHUNK)

        @pl.when(i + 1 < steps)
        def _():
            for copy in fetch(i + 1, (i + 1) % 2):
                copy.start()

        for copy in fetch(i, slot):
            copy.wait()
        position = lax.broadcasted_iota(jnp.int32, (CAP, CHUNK), 1) + k * CHUNK
        rows = aligned(s * CAP, CAP)
        onehot = jnp.where(SLOT[rows, :].astype(jnp.int32) == position, 1.0, 0.0).astype(bf16)
        tokens = QKVM[2 * slot]
        AO[rows, :] += dot(onehot, tokens, 1, 0)
        NG[rows, :] += dot(onehot, QKVM[2 * slot + 1], 1, 0)
        at = (pl.ds(s, 1), aligned(k * CHUNK, CHUNK))
        segment, mask = r["segments"][at].astype(f32), r["pad_mask"][at].astype(f32)
        line = lax.broadcasted_iota(jnp.int32, (16, CHUNK), 0)
        marks = jnp.where(line == 0, segment, jnp.where(line == 1, mask, 0.0)).astype(bf16)
        gate_logits = dot(router_tile, tokens, 1, 1)[0:1]
        STAT[0:1] += mask * jax.nn.sigmoid(gate_logits)
        STAT[1:2] += mask
        SEGR[s] += dot(marks, onehot, 1, 1)

    def gather_steps(first, last):
        loop(last - first, lambda i: gather_step(i + first))

    far = range(1, A)
    gather_steps(0, 3)
    for dz in far:
        gains.relay(dz)
    for dz in far:
        query.relay(dz)
    gather_steps(3, 5)
    for dz in far:
        key.relay(dz)
    query.relay_own()
    for dz in far:
        query.relay_second(dz)
    gather_steps(5, 7)
    for dz in far:
        value.relay(dz)
    key.relay_own()
    for dz in far:
        key.relay_second(dz)
    for dz in far:
        query.relay_third(dz)
    gather_steps(7, steps)

    step_rows = T // 4

    def gate_step(i):
        rows = aligned(i * step_rows, step_rows)
        v, g = AO[rows, :], NG[rows, :]
        gate = jax.nn.sigmoid(jnp.sum(v * router_row, axis=-1, keepdims=True))
        GATE[rows, :] = gate
        R1[rows, :] = lax.rsqrt(jnp.mean(v * v, axis=-1, keepdims=True) + EPS)
        RT[rows, :] = v.astype(bf16)
        OG[rows, :] = g.astype(bf16)
        MG[n, rows, :] = (gate * g).astype(bf16)

    for dz in far:
        out.relay(dz)
    value.relay_own()
    for dz in far:
        value.relay_second(dz)
    for dz in far:
        key.relay_third(dz)
    loop(4, gate_step)

    class RowShare:
        def __init__(self, at):
            self.at = at

        def start(self, k):
            p = self.at(n, k)
            self.core = getattr(self, "core", {})
            self.far = getattr(self, "far", {})
            self.core[k] = links.go(p, p, to_c)
            self.far[k] = links.go(p, p, to_y)

        def relay(self, k):
            self.far[k].wait_recv()
            p = self.at((1 - y) * 2 + c, k)
            self.last = getattr(self, "last", {})
            self.last[k] = links.go(p, p, to_c)

        def release(self):
            for copies in (self.core, self.far, self.last):
                links.sent_all(list(copies.values()))

    share_mg = RowShare(lambda b, k: MG.at[b, pl.ds(k * CAP, CAP)])
    share_nt = RowShare(lambda b, k: NT.at[b, pl.ds(k * (A // 2), A // 2)])
    gains.finish()
    r["GN"][...] = jnp.sum(GP[...], axis=0)

    def norm_one_step(i):
        rows = aligned(i * step_rows, step_rows)
        N1[rows, :] = (RT[rows, :].astype(f32) * R1[rows, :] * r["GN"][0:1]).astype(bf16)

    loop(4, norm_one_step)
    ordered = lax.broadcasted_iota(jnp.int32, (CAP, CAP), 0) <= lax.broadcasted_iota(jnp.int32, (CAP, CAP), 1)
    for s in range(S):
        same = upright(SEGR[s][0:1]) == SEGR[s][0:1]
        r["BIAS"][s] = jnp.where(ordered & same, 0.0, -1e30)
    out.relay_own()
    for dz in far:
        out.relay_second(dz)
    for dz in far:
        value.relay_third(dz)
    for dz in far:
        out.relay_third(dz)
    up.start_near()
    down.start_near()
    for k in range(2):
        share_mg.start(k)

    def project(g):
        def step(j):
            cols = aligned(j * half, half)
            QKVM[g, :, cols] = dot(N1[...], WA[g, :, :, cols].reshape(D, half), 1, 0).astype(bf16)

        loop(2, step)

    for g in range(3):
        attn[g].finish()
        project(g)

    lane = lax.broadcasted_iota(jnp.int32, (1, LANES), 1)
    low_lanes = lane < HEAD_DIM

    def pick(h, v):
        return jnp.where(low_lanes if h == 0 else ~low_lanes, v, jnp.zeros_like(v))

    def softmax_of(s, q, k, h):
        logits = dot(k, pick(h, q), 1, 1) + r["BIAS"][s]
        e = jnp.exp(logits - jnp.max(logits, axis=0, keepdims=True))
        return e * (1.0 / jnp.sum(e, axis=0, keepdims=True))

    group = 2

    def attend(s):
        def step(i):
            for u in range(group):
                rows, cols = pl.ds(s * CAP, CAP), aligned((i * group + u) * LANES, LANES)
                q, k, v = QKVM[0, rows, cols] * bf16(scale), QKVM[1, rows, cols], QKVM[2, rows, cols]
                o = [dot(softmax_of(s, q, k, h).astype(bf16), v, 0, 0) for h in range(2)]
                QKVM[3, rows, cols] = jnp.where(low_lanes, o[0], o[1]).astype(bf16)

        loop(D // LANES // group, step)

    def project_out(s):
        rows = pl.ds(s * CAP, CAP)

        def step(j):
            cols = aligned(j * half, half)
            AO[rows, cols] = dot(QKVM[3, rows, :], WA[3, :, :, cols].reshape(D, half), 1, 0)

        loop(2, step)

    def norm_two(k):
        def step(i):
            rows = aligned(k * CAP + i * (CAP // 2), CAP // 2)
            v = RT[rows, :].astype(f32) + AO[rows, :]
            scale_two = lax.rsqrt(jnp.mean(v * v, axis=-1, keepdims=True) + EPS)
            R2[rows, :] = scale_two
            part = (v * scale_two * r["GN"][1:2]).astype(bf16)
            NT[n, pl.ds(k * (A // 2) + i * (A // 4), A // 4)] = part.reshape(A // 4, 2, RB, D)

        loop(2, step)

    attend(0)
    out.finish()
    project_out(0)
    norm_two(0)
    share_nt.start(0)
    for dz in far:
        up.relay(dz)
    attend(1)
    project_out(1)
    norm_two(1)
    share_nt.start(1)

    tanh_k = math.sqrt(2.0 / math.pi)

    def up_unit(yy, k):
        rows = NT.at[pl.ds(yy * 2, 2), pl.ds(k * (A // 2), A // 2)]
        parts = [pl.ds(cc * (A // 2) + k * (A // 4), A // 4) for cc in range(2)]

        def step(j):
            cols = aligned(j * quart, quart)
            v = dot(rows[...].reshape(T, D), WU[:, :, :, cols].reshape(D, quart), 1, 0)
            vv = v * v
            t = jnp.tanh(v * (tanh_k + (tanh_k * 0.044715) * vv))
            act = 0.5 * v * (1.0 + t)
            slope = (0.5 + 0.5 * t) * (1.0 + v * (1.0 - t) * (tanh_k + (tanh_k * 0.134145) * vv))
            for cc in range(2):
                at = slice(cc * CAP, (cc + 1) * CAP)
                ACT[yy, parts[cc], :, :, :, cols] = act[at].astype(bf16).reshape(A // 4, 2, 2, RB, quart)
                DG[yy, parts[cc], :, :, :, cols] = slope[at].astype(bf16).reshape(A // 4, 2, 2, RB, quart)

        loop(4, step)

    def act_unit(yy):
        def step(j):
            cols = aligned(j * quart, quart)
            rows = WD[pl.ds(j * (A // 4), A // 4)].reshape(quart, D)
            v = dot(MG[pl.ds(yy * 2, 2)].reshape(2 * T, D), rows, 1, 1)
            slope = DG[yy, :, :, :, :, cols].reshape(2 * T, quart).astype(f32)
            DG[yy, :, :, :, :, cols] = (v * slope).astype(bf16).reshape(A, 2, 2, RB, quart)

        loop(4, step)

    up.finish()
    share_nt.core[0].wait_recv()
    up_unit(y, 0)
    for dz in far:
        down.relay(dz)
    share_nt.core[1].wait_recv()
    up_unit(y, 1)
    for k in range(2):
        share_mg.relay(k)
    share_nt.relay(0)
    down.finish()
    for k in range(2):
        share_mg.core[k].wait_recv()
    act_unit(y)
    share_nt.last[0].wait_recv()
    up_unit(1 - y, 0)
    share_nt.relay(1)
    for k in range(2):
        share_mg.last[k].wait_recv()
    share_nt.last[1].wait_recv()
    up_unit(1 - y, 1)
    act_unit(1 - y)

    class NarrowReduce:
        def __init__(self, lhs, part, send, k, total):
            self.lhs, self.part, self.send, self.k, self.total = lhs, part, send, k, total
            self.core, self.far = [], []

        def compute(self, q):
            yy = y if q else 1 - y
            keep = self.total if q else MO

            def step(j):
                cols = aligned(j * quart, quart)
                v = self.part(self.lhs[yy].reshape(2 * T, D), j, cols)
                PS[q, :, cols] = jnp.where(c == 0, v[T:], v[:T]).astype(bf16)
                keep[:, cols] = jnp.where(c == 0, v[:T], v[T:])

            loop(4, step)
            self.core.append(links.go(PS.at[q], PR.at[q], to_c))

        def send_far(self):
            self.core[0].wait_recv()
            for k in range(2):
                rows = pl.ds(k * CAP, CAP)
                self.send[rows, :] = (MO[rows, :] + PR[0, rows, :].astype(f32)).astype(bf16)
                self.far.append(links.go(self.send.at[rows], YR.at[self.k, rows], to_y))

        def keep_own(self):
            self.core[1].wait_recv()
            for k in range(2):
                rows = pl.ds(k * CAP, CAP)
                self.total[rows, :] = self.total[rows, :] + PR[1, rows, :].astype(f32)

    def norm_two_part(rows, j, cols):
        return dot(rows, WU[pl.ds(j * (A // 4), A // 4)].reshape(quart, D), 1, 1)

    def mlp_part(rows, j, cols):
        return dot(rows, WD[:, :, :, cols].reshape(D, quart), 1, 0)

    reduce_nt = NarrowReduce(DG, norm_two_part, YS, 0, NG)
    reduce_nt.compute(0)
    reduce_nt.compute(1)
    reduce_nt.send_far()
    reduce_nt.keep_own()
    pl.semaphore_signal(credit.at[0], inc=1, device_id=to_c, device_id_type=MESH)

    class WideReduce:
        def __init__(self, grad, k):
            self.grad, self.k = grad, k

        def landing(self, dz):
            return PR.at[0, pl.ds(dz * R, R)] if self.k else r["GXR"].at[dz]

        def compute(self, lhs, rhs):
            def step(i):
                cols = aligned(i * quart, quart)
                v = dot(lhs(cols), rhs(), 0, 0)
                self.grad[pl.ds(i * (A // 4), A // 4)] = v.astype(bf16).reshape(A // 4, 2, R, D)

            loop(4, step)

        def start(self):
            self.x, self.far = {}, {}
            for dz in list(range(1, A)) + [0]:
                self.x[dz] = links.go(self.grad.at[ahead[dz], 1 - x], self.landing(dz), to_x)

        def middle(self, *dzs):
            for dz in dzs:
                self.x[dz].wait_recv()
                p = self.grad.at[ahead[dz], x]
                p[...] = (p[...].astype(f32) + self.landing(dz)[...].astype(f32)).astype(bf16)
                if dz:
                    self.far[dz] = links.go(p, r["GZR"].at[self.k, dz - 1], dev(ahead[dz], x, y, c))

        def last(self):
            total = self.grad[z, x].astype(f32)
            for dz in range(1, A):
                self.far[dz].wait_recv()
                total = total + r["GZR"][self.k, dz - 1].astype(f32)
            r["FIN"][self.k, n] = total.astype(bf16)
            p = r["FIN"].at[self.k, n]
            self.core = [links.go(p, p, to_c)]
            self.yy = links.go(p, p, to_y)

        def finish(self):
            self.yy.wait_recv()
            p = r["FIN"].at[self.k, (1 - y) * 2 + c]
            self.core.append(links.go(p, p, to_c))
            for copy in self.core:
                copy.wait_recv()

    reduce_up, reduce_down = WideReduce(WU, 0), WideReduce(WD, 1)
    up.release()
    reduce_up.compute(lambda cols: NT[..., cols].reshape(4 * T, quart), lambda: DG[...].reshape(4 * T, D))
    reduce_up.start()
    share_nt.release()
    pl.semaphore_signal(credit.at[1], inc=1, device_id=to_c, device_id_type=MESH)

    reduce_mo = NarrowReduce(ACT, mlp_part, r["YS2"], 1, MO)
    pl.semaphore_wait(credit.at[0], 1)
    links.sent_all(reduce_nt.core)
    reduce_mo.compute(0)
    reduce_up.middle(1)
    reduce_mo.send_far()
    reduce_mo.compute(1)
    reduce_mo.keep_own()
    pl.semaphore_signal(credit.at[2], inc=1, device_id=to_x, device_id_type=MESH)
    down.release()
    reduce_down.compute(lambda cols: ACT[..., cols].reshape(4 * T, quart), lambda: MG[...].reshape(4 * T, D))
    pl.semaphore_wait(credit.at[2], 1)
    reduce_down.start()
    reduce_up.middle(2)
    links.sent_all(reduce_mo.core)
    share_mg.release()
    SM[...] = jnp.zeros_like(SM)

    def norm_two_back(s):
        def step(i):
            rows = aligned(s * CAP + i * step_rows, step_rows)
            dy = NG[rows, :] + YR[0, rows, :].astype(f32)
            v = RT[rows, :].astype(f32) + AO[rows, :]
            s2 = R2[rows, :]
            dyg = dy * r["GN"][1:2]
            mean = jnp.mean(dyg * v, axis=-1, keepdims=True)
            grad = s2 * dyg - v * (s2 * s2 * s2 * mean)
            SM[1:2] += jnp.sum(dy * (v * s2), axis=0, keepdims=True)
            NG[rows, :] = grad
            PS[0, rows, :] = (GATE[rows, :] * OG[rows, :].astype(f32) + grad).astype(bf16)

        loop(2, step)

    def mixed_back(s):
        rows = pl.ds(s * CAP, CAP)

        def step(j):
            weight = WA[3, pl.ds(j * (Wd // 2), Wd // 2)].reshape(half, D)
            MG[3, rows, aligned(j * half, half)] = dot(PS[0, rows, :], weight, 1, 1).astype(bf16)

        loop(2, step)

    def attend_back(s):
        def step(i):
            for u in range(group):
                rows, cols = pl.ds(s * CAP, CAP), aligned((i * group + u) * LANES, LANES)
                q, k, v = QKVM[0, rows, cols] * bf16(scale), QKVM[1, rows, cols], QKVM[2, rows, cols]
                dm = MG[3, rows, cols]
                dq, dk, dv = [], [], []
                for h in range(2):
                    p = softmax_of(s, q, k, h)
                    dp = dot(v, pick(h, dm), 1, 1)
                    dl = (p * (dp - jnp.sum(p * dp, axis=0, keepdims=True))).astype(bf16)
                    dq.append(dot(dl, k, 0, 0))
                    dk.append(dot(dl, q, 1, 0))
                    dv.append(dot(p.astype(bf16), dm, 1, 0))
                MG[0, rows, cols] = (jnp.where(low_lanes, dq[0], dq[1]) * scale).astype(bf16)
                MG[1, rows, cols] = jnp.where(low_lanes, dk[0], dk[1]).astype(bf16)
                MG[2, rows, cols] = jnp.where(low_lanes, dv[0], dv[1]).astype(bf16)

        loop(D // LANES // group, step)

    class AttnReduce:
        def __init__(self, buf, at, k):
            self.buf, self.at, self.k = buf, at, k

        def compute(self, lhs, rhs):
            def step(i):
                cols = aligned(i * quart, quart)
                v = dot(lhs(cols), rhs(), 0, 0)
                self.buf[self.at, pl.ds(i * (A // 4), A // 4)] = v.astype(bf16).reshape(A // 4, 2, 2, RB, D)

            loop(4, step)

        def landing(self, d):
            return PR.at[1, pl.ds((self.k * (A // 2) + d) * RB, RB)]

        def start(self):
            self.core = [links.go(self.buf.at[self.at, :, :, 1 - c], NT.at[self.k], to_c)]

        def part(self, zz, xx, cols=None):
            if cols is None:
                return self.buf.at[self.at, zz, xx, c]
            return self.buf.at[self.at, zz, xx, c, :, aligned(cols * half, half)]

        def first(self):
            self.core[0].wait_recv()

            def step(i):
                p = self.buf.at[self.at, i // 2, i % 2, c]
                p[...] = (p[...].astype(f32) + NT[self.k, i // 2, i % 2].astype(f32)).astype(bf16)

            loop(2 * A, step)
            self.one, self.two, self.far = {}, {}, {}
            for dz in range(A):
                d = (dz + 1) % A
                zz = ahead[d]
                if d < A // 2:
                    self.one[d] = links.go(self.part(zz, 1 - x), self.landing(d), to_x)
                else:
                    e = d - A // 2
                    cols = aligned((1 - y) * half, half)
                    self.one[d] = links.go(self.buf.at[self.at, zz, :, c, :, cols], r["YRB"].at[self.k, e], to_y)

        def add(self, p, q):
            p[...] = (p[...].astype(f32) + q[...].astype(f32)).astype(bf16)

        def second(self):
            for dz in range(A):
                d = (dz + 1) % A
                zz = ahead[d]
                self.one[d].wait_recv()
                if d < A // 2:
                    self.add(self.part(zz, x), self.landing(d))
                    self.two[d] = links.go(self.part(zz, x, 1 - y), r["YRA"].at[self.k, d], to_y)
                else:
                    e = d - A // 2
                    p = self.buf.at[self.at, zz, :, c, :, aligned(y * half, half)]
                    self.add(p, r["YRB"].at[self.k, e])
                    self.two[d] = links.go(self.part(zz, 1 - x, y), r["XRB"].at[self.k, e], to_x)

        def third(self):
            for dz in range(A):
                d = (dz + 1) % A
                zz = ahead[d]
                self.two[d].wait_recv()
                p = self.part(zz, x, y)
                self.add(p, r["YRA"].at[self.k, d] if d < A // 2 else r["XRB"].at[self.k, d - A // 2])
                if d:
                    self.far[d] = links.go(p, r["ZR"].at[self.k, d - 1], dev(zz, x, y, c))

        def fin(self, yy):
            return r["FINA"].at[self.k, c, :, aligned(yy * half, half)]

        def last(self):
            total = self.part(z, x, y)[...].astype(f32)
            for d in range(1, A):
                self.far[d].wait_recv()
                total = total + r["ZR"][self.k, d - 1].astype(f32)
            p = self.fin(y)
            p[...] = total.astype(bf16)
            self.core.append(links.go(p, p, to_c))
            self.yy = links.go(p, p, to_y)

        def finish(self):
            self.yy.wait_recv()
            p = self.fin(1 - y)
            self.core.append(links.go(p, p, to_c))
            for copy in self.core[1:]:
                copy.wait_recv()

    reduce_o = AttnReduce(ACT, 0, 3)
    reduce_v = AttnReduce(ACT, 1, 2)
    reduce_k = AttnReduce(DG, 0, 1)
    reduce_q = AttnReduce(DG, 1, 0)
    reduce_nt.far[0].wait_recv()
    norm_two_back(0)
    mixed_back(0)
    attend_back(0)
    reduce_up.middle(3, 0) if A == 4 else reduce_up.middle(*range(3, A), 0)
    reduce_nt.far[1].wait_recv()
    norm_two_back(1)
    mixed_back(1)
    reduce_o.compute(lambda cols: QKVM[3, :, cols], lambda: PS[0])
    pl.semaphore_wait(credit.at[1], 1)
    reduce_o.start()
    attend_back(1)
    reduce_o.first()
    reduce_down.middle(1, 2)
    for k, red in ((2, reduce_v), (1, reduce_k), (0, reduce_q)):
        red.compute(lambda cols: N1[:, cols], lambda k=k: MG[k])
        red.start()
    reduce_v.first()
    reduce_up.last()
    reduce_k.first()
    reduce_down.middle(*range(3, A), 0)
    reduce_q.first()

    def output_step(i):
        rows = aligned(i * step_rows, step_rows)
        v = RT[rows, :].astype(f32)
        g = OG[rows, :].astype(f32)
        gate = GATE[rows, :]
        branch = AO[rows, :] + MO[rows, :] + YR[1, rows, :].astype(f32)
        lg = jnp.sum(g * branch, axis=-1, keepdims=True) * gate * (1.0 - gate)
        LG[rows, :] = lg
        SM[2:3] += jnp.sum(lg * v, axis=0, keepdims=True)
        QKVM[3, rows, :] = (v + gate * branch).astype(bf16)

    for copy in reduce_mo.far:
        copy.wait_recv()
    loop(4, output_step)
    new_copy = pltpu.make_async_copy(QKVM.at[3], r["new_rows"], local.at[0])
    new_copy.start()
    reduce_o.second()

    def norm_one_grad(j):
        rows = pl.ds(j * (Wd // 4), Wd // 4)
        v = dot(MG[0], WA[0, rows].reshape(quart, D), 1, 1)
        v = v + dot(MG[1], WA[1, rows].reshape(quart, D), 1, 1)
        v = v + dot(MG[2], WA[2, rows].reshape(quart, D), 1, 1)
        MO[:, aligned(j * quart, quart)] = v

    loop(4, norm_one_grad)
    reduce_up.finish()
    reduce_v.second()
    reduce_o.third()

    def norm_one_back(i):
        rows = aligned(i * step_rows, step_rows)
        dy = MO[rows, :]
        v = RT[rows, :].astype(f32)
        s1 = R1[rows, :]
        dyg = dy * r["GN"][0:1]
        mean = jnp.mean(dyg * v, axis=-1, keepdims=True)
        SM[0:1] += jnp.sum(dy * (v * s1), axis=0, keepdims=True)
        grad = s1 * dyg - v * (s1 * s1 * s1 * mean)
        grad = OG[rows, :].astype(f32) + NG[rows, :] + grad + LG[rows, :] * router_row
        QKVM[0, rows, :] = grad.astype(bf16)

    loop(4, norm_one_back)
    grad_copy = pltpu.make_async_copy(QKVM.at[0], r["row_grads"], local.at[1])
    grad_copy.start()

    total = lambda v: jnp.sum(jnp.sum(v, axis=1, keepdims=True), axis=0, keepdims=True)
    chosen = total(jnp.sum(SEGR[...], axis=0)[1:2])
    lanes = lax.broadcasted_iota(jnp.int32, (1, D), 1)
    SM[3:4] = (
        jnp.where(lanes == 0, chosen, 0.0)
        + jnp.where(lanes == 1, total(STAT[1:2]), 0.0)
        + jnp.where(lanes == 2, total(STAT[0:1]), 0.0)
    )
    SMS, SMR, SMZ = r["SMS"], r["SMR"], r["SMZ"]
    sums = [links.go(SM, SMR.at[0], to_c)]
    reduce_k.second()
    reduce_v.third()
    reduce_down.last()
    sums[0].wait_recv()
    SMS[0] = SM[...] + SMR[0]
    sums.append(links.go(SMS.at[0], SMR.at[1], to_x))
    reduce_q.second()
    reduce_k.third()
    reduce_o.last()
    sums[1].wait_recv()
    SMS[1] = SMS[0] + SMR[1]
    sums.append(links.go(SMS.at[1], SMR.at[2], to_y))
    reduce_v.last()
    reduce_down.finish()
    reduce_q.third()
    sums[2].wait_recv()
    SMZ[z] = SMS[1] + SMR[2]
    sums = [links.go(SMZ.at[z], SMZ.at[z], dev(ahead[dz], x, y, c)) for dz in range(1, A)]
    reduce_k.last()
    reduce_o.finish()
    reduce_v.finish()
    reduce_q.last()
    for copy in sums:
        copy.wait_recv()
    r["small"][...] = jnp.sum(SMZ[...], axis=0)
    reduce_k.finish()
    reduce_q.finish()
    outs = [
        pltpu.make_async_copy(r["FIN"], r["mlp_grads"], local.at[2]),
        pltpu.make_async_copy(r["FINA"], r["attn_grads"], local.at[3]),
    ]
    for copy in outs:
        copy.start()
    links.drain()
    for copy in outs + [new_copy, grad_copy]:
        copy.wait()
    for k, name in enumerate(DEBUG):
        copy = pltpu.make_async_copy(r[name], r["dbg_" + name], local.at[4])
        copy.start()
        copy.wait()


def finish_kernel(dims, slots, rows, row_grads, attn_grads, mlp_grads, small, base, base_grad,
                  out, out_grad, stats, router, gain_one, gain_two, attn_out, up_out, down_out,
                  attn_stage, up_stage, down_stage, sems):
    S, per, R, Wd, part = dims
    i = pl.program_id(0)
    s, k = i // per, i % per
    size, cap = base.shape[1], slots.shape[1]
    position = lax.broadcasted_iota(jnp.int32, (size, cap), 0) + k * size
    onehot = jnp.where(slots[pl.ds(s, 1), :] == position, 1.0, 0.0)
    hit = jnp.max(onehot, axis=-1, keepdims=True) > 0.5
    onehot = onehot.astype(bf16)
    own = aligned(s * cap, cap)
    for new, old, target in ((rows, base, out), (row_grads, base_grad, out_grad)):
        picked = dot(onehot, new[own, :], 1, 0).astype(bf16)
        target[0] = jnp.where(hit, picked, old[0])

    attn_copies = [
        pltpu.make_async_copy(attn_stage.at[g], attn_out[g], sems.at[g]) for g in range(4)
    ]
    down_copies = [
        pltpu.make_async_copy(down_stage.at[q], down_out.at[pl.ds(q * R, R)], sems.at[4 + q]) for q in range(4)
    ]
    up_copy = pltpu.make_async_copy(up_stage, up_out, sems.at[8])

    @pl.when(i == 0)
    def _():
        for g in range(4):
            attn_stage[g] = attn_grads[g].astype(f32)
            attn_copies[g].start()
        w = lax.axis_index("wide")
        gains = pltpu.roll(small[...], (small.shape[1] - w * R) % small.shape[1], 1)
        gain_one[...] = gains[0:1, :R]
        gain_two[...] = gains[1:2, :R]
        router[...] = small[2:3]
        lane = lax.broadcasted_iota(jnp.int32, (1, small.shape[1]), 1)
        counts = small[3:4]
        valid = jnp.sum(jnp.where(lane == 1, counts, 0.0), axis=1, keepdims=True)
        shifted = jnp.where(lane == 1, pltpu.roll(counts, small.shape[1] - 1, 1), counts)
        stats[...] = (shifted / valid)[:, : stats.shape[1]]

    @pl.when(i == 1)
    def _():
        for q in range(4):
            down_stage[q] = mlp_grads[1, q].astype(f32)
            down_copies[q].start()

    @pl.when(i == 2)
    def _():
        for q in range(4):
            for v in range(Wd):
                at = (v * 4 + q) * part
                up_stage[:, at : at + part] = mlp_grads[0, q, :, v * part : (v + 1) * part].astype(f32)
        up_copy.start()

    @pl.when(i == S * per - 1)
    def _():
        for copy in attn_copies + down_copies + [up_copy]:
            copy.wait()


def finish(mesh, res, slots, block_input, cotangent, R, FF):
    S, SEQ, D = block_input.shape
    Wd = mesh.shape["wide"]
    size = 512
    per, part = SEQ // size, FF // (4 * Wd)

    def kernel(slots, rows, row_grads, attn, mlp, small, base, base_grad, out, out_grad, stats, router,
               gain_one, gain_two, q, k, v, o, up, down, *scratch):
        finish_kernel((S, per, R, Wd, part), slots, rows, row_grads, attn, mlp, small, base, base_grad,
                      out, out_grad, stats, router, gain_one, gain_two, (q, k, v, o), up, down, *scratch)

    vmem, hbm = pl.BlockSpec(memory_space=pltpu.VMEM), pl.BlockSpec(memory_space=pl.ANY)
    tile = pl.BlockSpec((1, size, D), lambda i: (i // per, i % per, 0))
    shape = jax.ShapeDtypeStruct
    return pl.pallas_call(
        kernel,
        grid=(S * per,),
        out_shape=[shape(block_input.shape, bf16)] * 2
        + [shape((1, 2), f32), shape((1, D), f32), shape((1, R), f32), shape((1, R), f32)]
        + [shape((R, D), f32)] * 4
        + [shape((R, FF), f32), shape((4 * R, D), f32)],
        in_specs=[vmem] * 6 + [tile] * 2,
        out_specs=[tile] * 2 + [vmem] * 4 + [hbm] * 6,
        scratch_shapes=[
            pltpu.VMEM((4, R, D), f32),
            pltpu.VMEM((R, FF), f32),
            pltpu.VMEM((4, R, D), f32),
            pltpu.SemaphoreType.DMA((9,)),
        ],
        compiler_params=pltpu.CompilerParams(vmem_limit_bytes=60 * MIB),
        name="finish_rows",
    )(slots, res["new_rows"], res["row_grads"], res["attn_grads"].reshape(4, R, D), res["mlp_grads"],
      res["small"], block_input, cotangent)


def run_block(mesh, inputs, S, SEQ, CAP, D, R):
    Wd = mesh.shape["wide"]
    A, RB, T = Wd // 2, R // 2, S * CAP
    dims = dict(A=A, R=R, T=T, S=S, CAP=CAP, SEQ=SEQ, D=D, RB=RB)
    out_shapes = {
        "new_rows": ((T, D), bf16),
        "row_grads": ((T, D), bf16),
        "mlp_grads": ((2, 4, R, D), bf16),
        "attn_grads": ((4, 2, RB, D), bf16),
        "small": ((8, D), f32),
    }
    scratch = {
        "WA": ((4, Wd, R, D), bf16),
        "WU": ((A, 2, R, D), bf16),
        "WD": ((A, 2, R, D), bf16),
        "GP": ((Wd, 8, D), f32),
        "GN": ((8, D), f32),
        "NT": ((4, A, 2, RB, D), bf16),
        "MG": ((4, T, D), bf16),
        "ACT": ((2, A, 2, 2, RB, D), bf16),
        "DG": ((2, A, 2, 2, RB, D), bf16),
        "QKVM": ((4, T, D), bf16),
        "N1": ((T, D), bf16),
        "RT": ((T, D), bf16),
        "OG": ((T, D), bf16),
        "AO": ((T, D), f32),
        "NG": ((T, D), f32),
        "MO": ((T, D), f32),
        "PS": ((2, T, D), bf16),
        "PR": ((2, T, D), bf16),
        "YS": ((T, D), bf16),
        "YS2": ((T, D), bf16),
        "YR": ((2, T, D), bf16),
        "GXR": ((A, R, D), bf16),
        "GZR": ((2, A - 1, R, D), bf16),
        "FIN": ((2, 4, R, D), bf16),
        "YRA": ((4, A // 2, RB, D // 2), bf16),
        "YRB": ((4, A // 2, 2, RB, D // 2), bf16),
        "XRB": ((4, A // 2, RB, D // 2), bf16),
        "ZR": ((4, A - 1, RB, D // 2), bf16),
        "FINA": ((4, 2, RB, D), bf16),
        "COLS": ((T, LANES), f32),
        "BIAS": ((S, CAP, CAP), f32),
        "SEGR": ((S, 16, CAP), f32),
        "STAT": ((8, CHUNK), f32),
        "SM": ((8, D), f32),
        "SMS": ((2, 8, D), f32),
        "SMR": ((3, 8, D), f32),
        "SMZ": ((A, 8, D), f32),
    }
    for name in DEBUG:
        out_shapes["dbg_" + name] = scratch[name]
    count = copy_count(A)
    semaphores = {
        "send": pltpu.SemaphoreType.DMA((count,)),
        "recv": pltpu.SemaphoreType.DMA((count,)),
        "local": pltpu.SemaphoreType.DMA((11 + Wd,)),
        "credit": pltpu.SemaphoreType.REGULAR((3,)),
    }
    in_vmem = ("gains", "router", "slots", "segments", "pad_mask")
    hbm, vmem = pl.BlockSpec(memory_space=pl.ANY), pl.BlockSpec(memory_space=pltpu.VMEM)
    names = list(inputs) + list(out_shapes) + list(scratch) + list(semaphores)
    results = pl.pallas_call(
        functools.partial(block_kernel, dims, names),
        out_shape=[jax.ShapeDtypeStruct(*v) for v in out_shapes.values()],
        in_specs=[vmem if k in in_vmem else hbm for k in inputs],
        out_specs=[vmem if k == "small" else hbm for k in out_shapes],
        scratch_shapes=[pltpu.VMEM(*v) for v in scratch.values()] + list(semaphores.values()),
        compiler_params=pltpu.CompilerParams(
            collective_id=0, has_side_effects=True, vmem_limit_bytes=64 * MIB - 65536
        ),
        name="routed_block",
    )(*inputs.values())
    return dict(zip(out_shapes, results))


def body(mesh, block_input, query_weight, key_weight, value_weight, out_weight, up_weight, down_weight,
         attn_gain, mlp_gain, router_weight, slots, segments, pad_mask, cotangent):
    S, SEQ, D = block_input.shape
    CAP = slots.shape[1]
    R, FF = up_weight.shape
    Wd = mesh.shape["wide"]
    w, n = lax.axis_index("wide"), lax.axis_index("narrow")
    part = FF // (4 * Wd)
    assert FF == 4 * D and S == 2 and 4 * CAP == D and part == R and mesh.shape["narrow"] == 4
    if part % LANES:
        up_weight = lax.dynamic_index_in_dim(up_weight.reshape(R, Wd, 4, part), n, axis=2, keepdims=False)
        up_weight = up_weight.reshape(R, D)
    shard = jnp.stack([attn_gain, mlp_gain]).astype(f32)
    gains = lax.dynamic_update_slice(jnp.zeros((8, D), f32), shard, (0, w * R))
    inputs = {
        "block_input": block_input,
        "cotangent": cotangent,
        "w_query": query_weight,
        "w_key": key_weight,
        "w_value": value_weight,
        "w_out": out_weight,
        "w_up": up_weight,
        "w_down": down_weight,
        "gains": gains,
        "router": router_weight.reshape(1, D),
        "slots": slots,
        "segments": segments,
        "pad_mask": pad_mask,
    }
    res = run_block(mesh, inputs, S, SEQ, CAP, D, R)
    outs = finish(mesh, res, slots, block_input, cotangent, R, FF)
    result = (outs[0], outs[1], *outs[6:], outs[4].reshape(R), outs[5].reshape(R), outs[3].reshape(D), outs[2].reshape(2))
    if DEBUG:
        return result, {k: res["dbg_" + k] for k in DEBUG}
    return result


def solution(mesh):
    rows, wide = P(("wide", "narrow")), P("wide")
    return jax.shard_map(
        functools.partial(body, mesh),
        mesh=mesh,
        in_specs=(rows,) + (wide,) * 8 + (P(),) + (rows,) * 4,
        out_specs=(rows, rows) + (wide,) * 8 + (P(), P()),
        check_vma=False,
    )
```

```python
import functools
import math

import jax
import jax.numpy as jnp
from jax import lax
from jax.experimental import pallas as pl
from jax.experimental.pallas import tpu as pltpu
from jax.sharding import PartitionSpec as P

HEADS = 16
HEAD_DIM = 64
EPS = 1e-06
LANES = 128
MESH = pl.DeviceIdType.MESH
f32 = jnp.float32
bf16 = jnp.bfloat16
MIB = 2**20
CHUNK = 512
DEBUG = ()


def dot(a, b, ca, cb):
    return lax.dot_general(a, b, (((ca,), (cb,)), ((), ())), preferred_element_type=f32)


def aligned(start, size):
    return pl.ds(pl.multiple_of(start, size), size)


def loop(count, step):
    def run(i, carry):
        step(i)
        return carry

    lax.fori_loop(0, count, run, 0)


class Column:
    def __init__(self, ref, lane):
        self.ref, self.lane = ref, slice(lane, lane + 1)

    def __getitem__(self, at):
        return self.ref[at[0], self.lane]

    def __setitem__(self, at, value):
        self.ref[at[0], self.lane] = value


class Links:
    def __init__(self, send, recv):
        self.send, self.recv, self.count, self.open = send, recv, 0, []

    def make(self, src, dst, device):
        i = self.count
        self.count += 1
        return pltpu.make_async_remote_copy(
            src_ref=src,
            dst_ref=dst,
            send_sem=self.send.at[i],
            recv_sem=self.recv.at[i],
            device_id=device,
            device_id_type=MESH,
        )

    def go(self, src, dst, device):
        copy = self.make(src, dst, device)
        copy.start()
        self.open.append(copy)
        return copy

    def sent(self, copy):
        copy.wait_send()
        self.open = [other for other in self.open if other is not copy]

    def sent_all(self, copies):
        for copy in copies:
            self.sent(copy)

    def drain(self):
        for copy in self.open:
            copy.wait_send()
        self.open = []


def copy_count(far):
    near = far - 1
    gather = 4 * (8 * near + 2) + 3 * (2 * near + 1)
    narrow = 2 * 6 + 2 * 4
    reduce_mlp = 2 * (far + near + 3)
    reduce_attn = 4 * (1 + 2 * far + near + 3)
    return gather + narrow + reduce_mlp + reduce_attn + 3 + near


def block_kernel(dims, names, *refs):
    r = dict(zip(names, refs))
    A, R, T, S, CAP, SEQ, D, RB = (
        dims[k] for k in ("A", "R", "T", "S", "CAP", "SEQ", "D", "RB")
    )
    Wd = 2 * A
    half, quart = D // 2, D // 4
    scale = 1.0 / math.sqrt(HEAD_DIM)
    w, n = lax.axis_index("wide"), lax.axis_index("narrow")
    z, x = w // 2, w % 2
    y, c = n // 2, n % 2
    WA, WU, WD, GP = r["WA"], r["WU"], r["WD"], r["GP"]
    NT, MG, ACT, DG = r["NT"], r["MG"], r["ACT"], r["DG"]
    QKVM, N1, RT, OG = r["QKVM"], r["N1"], r["RT"], r["OG"]
    AO, NG, MO = r["AO"], r["NG"], r["MO"]
    PS, PR, YS, YR = r["PS"], r["PR"], r["YS"], r["YR"]
    GATE, R1, R2, LG, SLOT = (Column(r["COLS"], k) for k in range(5))
    SEGR, STAT, SM = r["SEGR"], r["STAT"], r["SM"]
    local, credit = r["local"], r["credit"]
    links = Links(r["send"], r["recv"])

    def dev(zz, xx, yy, cc):
        return (zz * 2 + xx, yy * 2 + cc)

    to_x, to_y, to_c = dev(z, 1 - x, y, c), dev(z, x, 1 - y, c), dev(z, x, y, 1 - c)
    ahead = [(z + dz) % A for dz in range(A)]
    behind = [(z - dz + A) % A for dz in range(A)]

    own = [
        pltpu.make_async_copy(r["w_query"], WA.at[0, w], local.at[0]),
        pltpu.make_async_copy(r["w_key"], WA.at[1, w], local.at[1]),
        pltpu.make_async_copy(r["w_value"], WA.at[2, w], local.at[2]),
        pltpu.make_async_copy(r["w_out"], WA.at[3, w], local.at[3]),
        pltpu.make_async_copy(r["w_down"].at[aligned(n * R, R)], WD.at[z, x], local.at[5]),
        pltpu.make_async_copy(r["gains"], GP.at[w], local.at[6]),
    ]
    if r["w_up"].shape[1] == D:
        own.append(pltpu.make_async_copy(r["w_up"], WU.at[z, x], local.at[4]))
    else:
        own += [
            pltpu.make_async_copy(
                r["w_up"].at[:, aligned((v * 4 + n) * R, R)], WU.at[z, x, :, pl.ds(v * R, R)], local.at[11 + v]
            )
            for v in range(Wd)
        ]
    for copy in own:
        copy.start()
    fetches = {}

    def fetch(i, slot):
        s, k = i // (SEQ // CHUNK), i % (SEQ // CHUNK)
        return [
            pltpu.make_async_copy(
                r[name].at[s, aligned(k * CHUNK, CHUNK)], QKVM.at[2 * slot + a], local.at[7 + 2 * slot + a]
            )
            for a, name in enumerate(("block_input", "cotangent"))
        ]

    for copy in fetch(0, 0):
        copy.start()
    barrier = pltpu.get_barrier_semaphore()
    peers = [dev(ahead[dz], x, y, c) for dz in range(1, A)] + [to_x, to_y, to_c]
    for peer in peers:
        pl.semaphore_signal(barrier, inc=1, device_id=peer, device_id_type=MESH)
    pl.semaphore_wait(barrier, len(peers))
    for copy in own:
        copy.wait()

    class AttnGather:
        def __init__(self, first, count):
            self.first, self.count = first, count

        def piece(self, zz, xx, yy):
            return WA.at[pl.ds(self.first, self.count), zz * 2 + xx, :, aligned(c * half + yy * quart, quart)]

        def wide_piece(self, zz, xx):
            return WA.at[pl.ds(self.first, self.count), zz * 2 + xx, :, aligned(c * half, half)]

        def start(self):
            p, q = self.piece(z, x, y), self.wide_piece(z, x)
            self.far = {dz: links.go(p, p, dev(ahead[dz], x, y, c)) for dz in range(1, A)}
            self.x0 = links.go(q, q, to_x)
            self.x1, self.y1, self.second, self.core = {}, {}, {}, []

        def to_core(self, p):
            self.core.append(links.go(p, p, to_c))

        def relay(self, dz):
            self.far[dz].wait_recv()
            p = self.piece(behind[dz], x, y)
            self.x1[dz] = links.go(p, p, to_x)
            self.y1[dz] = links.go(p, p, to_y)
            self.to_core(p)

        def relay_own(self):
            self.x0.wait_recv()
            self.to_core(self.wide_piece(z, 1 - x))

        def relay_second(self, dz):
            self.x1[dz].wait_recv()
            p = self.piece(behind[dz], 1 - x, y)
            if dz % 2:
                self.second[dz] = links.go(p, p, to_y)
            self.to_core(p)
            self.y1[dz].wait_recv()
            p = self.piece(behind[dz], x, 1 - y)
            if not dz % 2:
                self.second[dz] = links.go(p, p, to_x)
            self.to_core(p)

        def relay_third(self, dz):
            self.second[dz].wait_recv()
            self.to_core(self.piece(behind[dz], 1 - x, 1 - y))

        def finish(self):
            for copy in self.core:
                copy.wait_recv()

    class WideGather:
        def __init__(self, at):
            self.at = at

        def start(self):
            p = self.at(z, x)
            self.far = {dz: links.go(p, p, dev(ahead[dz], x, y, c)) for dz in range(1, A)}
            self.near = []

        def start_near(self):
            p = self.at(z, x)
            self.near.append(links.go(p, p, to_x))

        def relay(self, dz):
            self.far[dz].wait_recv()
            p = self.at(behind[dz], x)
            self.near.append(links.go(p, p, to_x))

        def finish(self):
            for copy in self.near:
                copy.wait_recv()

        def release(self):
            links.sent_all(list(self.far.values()) + self.near)

    gains = WideGather(lambda zz, xx: GP.at[zz * 2 + xx])
    query, key, value, out = (AttnGather(g, 1) for g in range(4))
    attn = (query, key, value, out)
    up = WideGather(lambda zz, xx: WU.at[zz, xx])
    down = WideGather(lambda zz, xx: WD.at[zz, xx])
    gains.start()
    gains.start_near()
    for group in attn:
        group.start()
    up.start()
    down.start()

    AO[...] = jnp.zeros_like(AO)
    NG[...] = jnp.zeros_like(NG)
    SEGR[...] = jnp.zeros_like(SEGR)
    STAT[...] = jnp.zeros_like(STAT)
    eye = lax.broadcasted_iota(jnp.int32, (CAP, CAP), 0) == lax.broadcasted_iota(jnp.int32, (CAP, CAP), 1)

    def upright(row):
        return jnp.sum(jnp.where(eye, row, 0.0), axis=1, keepdims=True)

    for s in range(S):
        SLOT[pl.ds(s * CAP, CAP), :] = upright(r["slots"][s : s + 1, :].astype(f32))
    router_row = r["gains"][2:3]
    router_tile = jnp.broadcast_to(router_row, (16, D)).astype(bf16)
    steps = S * (SEQ // CHUNK)

    def gather_step(i):
        slot = i % 2
        s, k = i // (SEQ // CHUNK), i % (SEQ // CHUNK)

        @pl.when(i + 1 < steps)
        def _():
            for copy in fetch(i + 1, (i + 1) % 2):
                copy.start()

        for copy in fetch(i, slot):
            copy.wait()
        position = lax.broadcasted_iota(jnp.int32, (CAP, CHUNK), 1) + k * CHUNK
        rows = aligned(s * CAP, CAP)
        onehot = jnp.where(SLOT[rows, :].astype(jnp.int32) == position, 1.0, 0.0).astype(bf16)
        tokens = QKVM[2 * slot]
        AO[rows, :] += dot(onehot, tokens, 1, 0)
        NG[rows, :] += dot(onehot, QKVM[2 * slot + 1], 1, 0)
        at = (pl.ds(s, 1), aligned(k * CHUNK, CHUNK))
        segment, mask = r["segments"][at].astype(f32), r["pad_mask"][at].astype(f32)
        line = lax.broadcasted_iota(jnp.int32, (16, CHUNK), 0)
        marks = jnp.where(line == 0, segment, jnp.where(line == 1, mask, 0.0)).astype(bf16)
        gate_logits = dot(router_tile, tokens, 1, 1)[0:1]
        STAT[0:1] += mask * jax.nn.sigmoid(gate_logits)
        STAT[1:2] += mask
        SEGR[s] += dot(marks, onehot, 1, 1)

    def gather_steps(first, last):
        loop(last - first, lambda i: gather_step(i + first))

    far = range(1, A)
    gather_steps(0, 3)
    for dz in far:
        gains.relay(dz)
    for dz in far:
        query.relay(dz)
    gather_steps(3, 5)
    for dz in far:
        key.relay(dz)
    query.relay_own()
    for dz in far:
        query.relay_second(dz)
    gather_steps(5, 7)
    for dz in far:
        value.relay(dz)
    key.relay_own()
    for dz in far:
        key.relay_second(dz)
    for dz in far:
        query.relay_third(dz)
    gather_steps(7, steps)

    step_rows = T // 4

    def gate_step(i):
        rows = aligned(i * step_rows, step_rows)
        v, g = AO[rows, :], NG[rows, :]
        gate = jax.nn.sigmoid(jnp.sum(v * router_row, axis=-1, keepdims=True))
        GATE[rows, :] = gate
        R1[rows, :] = lax.rsqrt(jnp.mean(v * v, axis=-1, keepdims=True) + EPS)
        RT[rows, :] = v.astype(bf16)
        OG[rows, :] = g.astype(bf16)
        MG[n, rows, :] = (gate * g).astype(bf16)

    for dz in far:
        out.relay(dz)
    value.relay_own()
    for dz in far:
        value.relay_second(dz)
    for dz in far:
        key.relay_third(dz)
    loop(4, gate_step)

    class RowShare:
        def __init__(self, at):
            self.at = at

        def start(self, k):
            p = self.at(n, k)
            self.core = getattr(self, "core", {})
            self.far = getattr(self, "far", {})
            self.core[k] = links.go(p, p, to_c)
            self.far[k] = links.go(p, p, to_y)

        def relay(self, k):
            self.far[k].wait_recv()
            p = self.at((1 - y) * 2 + c, k)
            self.last = getattr(self, "last", {})
            self.last[k] = links.go(p, p, to_c)

        def release(self):
            for copies in (self.core, self.far, self.last):
                links.sent_all(list(copies.values()))

    share_mg = RowShare(lambda b, k: MG.at[b, pl.ds(k * CAP, CAP)])
    share_nt = RowShare(lambda b, k: NT.at[b, pl.ds(k * (A // 2), A // 2)])
    gains.finish()
    r["GN"][...] = jnp.sum(GP[...], axis=0)

    def norm_one_step(i):
        rows = aligned(i * step_rows, step_rows)
        N1[rows, :] = (RT[rows, :].astype(f32) * R1[rows, :] * r["GN"][0:1]).astype(bf16)

    loop(4, norm_one_step)
    ordered = lax.broadcasted_iota(jnp.int32, (CAP, CAP), 0) <= lax.broadcasted_iota(jnp.int32, (CAP, CAP), 1)
    for s in range(S):
        same = upright(SEGR[s][0:1]) == SEGR[s][0:1]
        r["BIAS"][s] = jnp.where(ordered & same, 0.0, -1e30)
    out.relay_own()
    for dz in far:
        out.relay_second(dz)
    for dz in far:
        value.relay_third(dz)
    for dz in far:
        out.relay_third(dz)
    up.start_near()
    down.start_near()
    for k in range(2):
        share_mg.start(k)

    def project(g):
        def step(j):
            cols = aligned(j * half, half)
            QKVM[g, :, cols] = dot(N1[...], WA[g, :, :, cols].reshape(D, half), 1, 0).astype(bf16)

        loop(2, step)

    for g in range(3):
        attn[g].finish()
        project(g)

    lane = lax.broadcasted_iota(jnp.int32, (1, LANES), 1)
    low_lanes = lane < HEAD_DIM

    def pick(h, v):
        return jnp.where(low_lanes if h == 0 else ~low_lanes, v, jnp.zeros_like(v))

    def softmax_of(s, q, k, h):
        logits = dot(k, pick(h, q), 1, 1) + r["BIAS"][s]
        e = jnp.exp(logits - jnp.max(logits, axis=0, keepdims=True))
        return e * (1.0 / jnp.sum(e, axis=0, keepdims=True))

    group = 4

    def attend(s):
        def step(i):
            for u in range(group):
                rows, cols = pl.ds(s * CAP, CAP), aligned((i * group + u) * LANES, LANES)
                q, k, v = QKVM[0, rows, cols] * bf16(scale), QKVM[1, rows, cols], QKVM[2, rows, cols]
                o = [dot(softmax_of(s, q, k, h).astype(bf16), v, 0, 0) for h in range(2)]
                QKVM[3, rows, cols] = jnp.where(low_lanes, o[0], o[1]).astype(bf16)

        loop(D // LANES // group, step)

    def project_out(s):
        rows = pl.ds(s * CAP, CAP)

        def step(j):
            cols = aligned(j * half, half)
            AO[rows, cols] = dot(QKVM[3, rows, :], WA[3, :, :, cols].reshape(D, half), 1, 0)

        loop(2, step)

    def norm_two(k):
        def step(i):
            rows = aligned(k * CAP + i * (CAP // 2), CAP // 2)
            v = RT[rows, :].astype(f32) + AO[rows, :]
            scale_two = lax.rsqrt(jnp.mean(v * v, axis=-1, keepdims=True) + EPS)
            R2[rows, :] = scale_two
            part = (v * scale_two * r["GN"][1:2]).astype(bf16)
            NT[n, pl.ds(k * (A // 2) + i * (A // 4), A // 4)] = part.reshape(A // 4, 2, RB, D)

        loop(2, step)

    attend(0)
    out.finish()
    project_out(0)
    norm_two(0)
    share_nt.start(0)
    for dz in far:
        up.relay(dz)
    attend(1)
    project_out(1)
    norm_two(1)
    share_nt.start(1)
    for dz in range(1, A - 1):
        down.relay(dz)

    tanh_k = math.sqrt(2.0 / math.pi)

    def up_unit(yy, k):
        rows = NT.at[pl.ds(yy * 2, 2), pl.ds(k * (A // 2), A // 2)]
        parts = [pl.ds(cc * (A // 2) + k * (A // 4), A // 4) for cc in range(2)]

        def step(j):
            cols = aligned(j * quart, quart)
            v = dot(rows[...].reshape(T, D), WU[:, :, :, cols].reshape(D, quart), 1, 0)
            vv = v * v
            t = jnp.tanh(v * (tanh_k + (tanh_k * 0.044715) * vv))
            act = 0.5 * v * (1.0 + t)
            slope = (0.5 + 0.5 * t) * (1.0 + v * (1.0 - t) * (tanh_k + (tanh_k * 0.134145) * vv))
            for cc in range(2):
                at = slice(cc * CAP, (cc + 1) * CAP)
                ACT[yy, parts[cc], :, :, :, cols] = act[at].astype(bf16).reshape(A // 4, 2, 2, RB, quart)
                DG[yy, parts[cc], :, :, :, cols] = slope[at].astype(bf16).reshape(A // 4, 2, 2, RB, quart)

        loop(4, step)

    def act_unit(yy):
        def step(j):
            cols = aligned(j * quart, quart)
            rows = WD[pl.ds(j * (A // 4), A // 4)].reshape(quart, D)
            v = dot(MG[pl.ds(yy * 2, 2)].reshape(2 * T, D), rows, 1, 1)
            slope = DG[yy, :, :, :, :, cols].reshape(2 * T, quart).astype(f32)
            DG[yy, :, :, :, :, cols] = (v * slope).astype(bf16).reshape(A, 2, 2, RB, quart)

        loop(4, step)

    for k in range(2):
        share_mg.relay(k)
        share_nt.core[k].wait_recv()
        share_mg.core[k].wait_recv()
    up.finish()
    up_unit(y, 0)
    down.relay(A - 1)
    up_unit(y, 1)
    share_nt.relay(0)
    share_nt.last[0].wait_recv()
    up_unit(1 - y, 0)
    for k in range(2):
        share_mg.last[k].wait_recv()
    share_nt.relay(1)
    share_nt.last[1].wait_recv()
    up_unit(1 - y, 1)
    down.finish()
    act_unit(1 - y)
    act_unit(y)

    class NarrowReduce:
        def __init__(self, lhs, part, send, k, total):
            self.lhs, self.part, self.send, self.k, self.total = lhs, part, send, k, total
            self.core, self.far = [], []

        def compute(self, q):
            yy = y if q else 1 - y
            keep = self.total if q else MO

            def step(j):
                cols = aligned(j * quart, quart)
                v = self.part(self.lhs[yy].reshape(2 * T, D), j, cols)
                PS[q, :, cols] = jnp.where(c == 0, v[T:], v[:T]).astype(bf16)
                keep[:, cols] = jnp.where(c == 0, v[:T], v[T:])

            loop(4, step)
            self.core.append(links.go(PS.at[q], PR.at[q], to_c))

        def send_far(self):
            self.core[0].wait_recv()
            for k in range(2):
                rows = pl.ds(k * CAP, CAP)
                self.send[rows, :] = (MO[rows, :] + PR[0, rows, :].astype(f32)).astype(bf16)
                self.far.append(links.go(self.send.at[rows], YR.at[self.k, rows], to_y))

        def keep_own(self):
            self.core[1].wait_recv()
            for k in range(2):
                rows = pl.ds(k * CAP, CAP)
                self.total[rows, :] = self.total[rows, :] + PR[1, rows, :].astype(f32)

    def norm_two_part(rows, j, cols):
        return dot(rows, WU[pl.ds(j * (A // 4), A // 4)].reshape(quart, D), 1, 1)

    def mlp_part(rows, j, cols):
        return dot(rows, WD[:, :, :, cols].reshape(D, quart), 1, 0)

    reduce_nt = NarrowReduce(DG, norm_two_part, YS, 0, NG)
    reduce_nt.compute(0)
    reduce_nt.compute(1)
    reduce_nt.send_far()
    reduce_nt.keep_own()
    pl.semaphore_signal(credit.at[0], inc=1, device_id=to_c, device_id_type=MESH)

    class WideReduce:
        def __init__(self, grad, k):
            self.grad, self.k = grad, k

        def landing(self, dz):
            return PR.at[0, pl.ds(dz * R, R)] if self.k else r["GXR"].at[dz]

        def compute(self, lhs, rhs):
            def step(i):
                cols = aligned(i * quart, quart)
                v = dot(lhs(cols), rhs(), 0, 0)
                self.grad[pl.ds(i * (A // 4), A // 4)] = v.astype(bf16).reshape(A // 4, 2, R, D)

            loop(4, step)

        def start(self):
            self.x, self.far = {}, {}
            for dz in list(range(1, A)) + [0]:
                self.x[dz] = links.go(self.grad.at[ahead[dz], 1 - x], self.landing(dz), to_x)

        def middle(self, *dzs):
            for dz in dzs:
                self.x[dz].wait_recv()
                p = self.grad.at[ahead[dz], x]
                p[...] = (p[...].astype(f32) + self.landing(dz)[...].astype(f32)).astype(bf16)
                if dz:
                    self.far[dz] = links.go(p, r["GZR"].at[self.k, dz - 1], dev(ahead[dz], x, y, c))

        def last(self):
            total = self.grad[z, x].astype(f32)
            for dz in range(1, A):
                self.far[dz].wait_recv()
                total = total + r["GZR"][self.k, dz - 1].astype(f32)
            r["FIN"][self.k, n] = total.astype(bf16)
            p = r["FIN"].at[self.k, n]
            self.core = [links.go(p, p, to_c)]
            self.yy = links.go(p, p, to_y)

        def finish(self):
            self.yy.wait_recv()
            p = r["FIN"].at[self.k, (1 - y) * 2 + c]
            self.core.append(links.go(p, p, to_c))
            for copy in self.core:
                copy.wait_recv()

    reduce_up, reduce_down = WideReduce(WU, 0), WideReduce(WD, 1)
    up.release()
    reduce_up.compute(lambda cols: NT[..., cols].reshape(4 * T, quart), lambda: DG[...].reshape(4 * T, D))
    reduce_up.start()
    share_nt.release()
    pl.semaphore_signal(credit.at[1], inc=1, device_id=to_c, device_id_type=MESH)

    reduce_mo = NarrowReduce(ACT, mlp_part, r["YS2"], 1, MO)
    pl.semaphore_wait(credit.at[0], 1)
    links.sent_all(reduce_nt.core)
    reduce_mo.compute(0)
    reduce_up.middle(1)
    reduce_mo.send_far()
    reduce_mo.compute(1)
    reduce_mo.keep_own()
    pl.semaphore_signal(credit.at[2], inc=1, device_id=to_x, device_id_type=MESH)
    down.release()
    reduce_down.compute(lambda cols: ACT[..., cols].reshape(4 * T, quart), lambda: MG[...].reshape(4 * T, D))
    pl.semaphore_wait(credit.at[2], 1)
    reduce_down.start()
    reduce_up.middle(2)
    links.sent_all(reduce_mo.core)
    share_mg.release()
    SM[...] = jnp.zeros_like(SM)

    def norm_two_back(s):
        def step(i):
            rows = aligned(s * CAP + i * step_rows, step_rows)
            dy = NG[rows, :] + YR[0, rows, :].astype(f32)
            v = RT[rows, :].astype(f32) + AO[rows, :]
            s2 = R2[rows, :]
            dyg = dy * r["GN"][1:2]
            mean = jnp.mean(dyg * v, axis=-1, keepdims=True)
            grad = s2 * dyg - v * (s2 * s2 * s2 * mean)
            SM[1:2] += jnp.sum(dy * (v * s2), axis=0, keepdims=True)
            NG[rows, :] = grad
            PS[0, rows, :] = (GATE[rows, :] * OG[rows, :].astype(f32) + grad).astype(bf16)

        loop(2, step)

    def mixed_back(s):
        rows = pl.ds(s * CAP, CAP)

        def step(j):
            weight = WA[3, pl.ds(j * (Wd // 2), Wd // 2)].reshape(half, D)
            MG[3, rows, aligned(j * half, half)] = dot(PS[0, rows, :], weight, 1, 1).astype(bf16)

        loop(2, step)

    def attend_back(s):
        def step(i):
            for u in range(group):
                rows, cols = pl.ds(s * CAP, CAP), aligned((i * group + u) * LANES, LANES)
                q, k, v = QKVM[0, rows, cols] * bf16(scale), QKVM[1, rows, cols], QKVM[2, rows, cols]
                dm = MG[3, rows, cols]
                k_t = k.T
                dq, dk, dv = [], [], []
                for h in range(2):
                    p = softmax_of(s, q, k, h)
                    dp = dot(v, pick(h, dm), 1, 1)
                    dl = (p * (dp - jnp.sum(p * dp, axis=0, keepdims=True))).astype(bf16)
                    dq.append(dot(k_t[h * HEAD_DIM : (h + 1) * HEAD_DIM], dl, 1, 0))
                    dk.append(dot(dl, q, 1, 0))
                    dv.append(dot(p.astype(bf16), dm, 1, 0))
                MG[0, rows, cols] = (jnp.concatenate(dq, axis=0) * scale).astype(bf16).T
                MG[1, rows, cols] = jnp.where(low_lanes, dk[0], dk[1]).astype(bf16)
                MG[2, rows, cols] = jnp.where(low_lanes, dv[0], dv[1]).astype(bf16)

        loop(D // LANES // group, step)

    x_first = A - A // 4

    class AttnReduce:
        def __init__(self, buf, at, k):
            self.buf, self.at, self.k = buf, at, k

        def compute(self, lhs, rhs):
            def step(i):
                cols = aligned(i * quart, quart)
                v = dot(lhs(cols), rhs(), 0, 0)
                self.buf[self.at, pl.ds(i * (A // 4), A // 4)] = v.astype(bf16).reshape(A // 4, 2, 2, RB, D)

            loop(4, step)

        def landing(self, d):
            if d < A // 2:
                return PR.at[1, pl.ds((self.k * (A // 2) + d) * RB, RB)]
            return r["XRA"].at[self.k, d - A // 2]

        def start(self):
            self.core = [links.go(self.buf.at[self.at, :, :, 1 - c], NT.at[self.k], to_c)]

        def part(self, zz, xx, cols=None):
            if cols is None:
                return self.buf.at[self.at, zz, xx, c]
            return self.buf.at[self.at, zz, xx, c, :, aligned(cols * half, half)]

        def first(self):
            self.core[0].wait_recv()

            def step(i):
                p = self.buf.at[self.at, i // 2, i % 2, c]
                p[...] = (p[...].astype(f32) + NT[self.k, i // 2, i % 2].astype(f32)).astype(bf16)

            loop(2 * A, step)
            self.one, self.two, self.far = {}, {}, {}
            for dz in range(A):
                d = (dz + 1) % A
                zz = ahead[d]
                if d < x_first:
                    self.one[d] = links.go(self.part(zz, 1 - x), self.landing(d), to_x)
                else:
                    e = d - x_first
                    cols = aligned((1 - y) * half, half)
                    self.one[d] = links.go(self.buf.at[self.at, zz, :, c, :, cols], r["YRB"].at[self.k, e], to_y)

        def add(self, p, q):
            p[...] = (p[...].astype(f32) + q[...].astype(f32)).astype(bf16)

        def second(self):
            for dz in range(A):
                d = (dz + 1) % A
                zz = ahead[d]
                self.one[d].wait_recv()
                if d < x_first:
                    self.add(self.part(zz, x), self.landing(d))
                    self.two[d] = links.go(self.part(zz, x, 1 - y), r["YRA"].at[self.k, d], to_y)
                else:
                    e = d - x_first
                    p = self.buf.at[self.at, zz, :, c, :, aligned(y * half, half)]
                    self.add(p, r["YRB"].at[self.k, e])
                    self.two[d] = links.go(self.part(zz, 1 - x, y), r["XRB"].at[self.k, e], to_x)

        def third(self):
            for dz in range(A):
                d = (dz + 1) % A
                zz = ahead[d]
                self.two[d].wait_recv()
                p = self.part(zz, x, y)
                self.add(p, r["YRA"].at[self.k, d] if d < x_first else r["XRB"].at[self.k, d - x_first])
                if d:
                    self.far[d] = links.go(p, r["ZR"].at[self.k, d - 1], dev(zz, x, y, c))

        def fin(self, yy):
            return r["FINA"].at[self.k, c, :, aligned(yy * half, half)]

        def last(self):
            total = self.part(z, x, y)[...].astype(f32)
            for d in range(1, A):
                self.far[d].wait_recv()
                total = total + r["ZR"][self.k, d - 1].astype(f32)
            p = self.fin(y)
            p[...] = total.astype(bf16)
            self.core.append(links.go(p, p, to_c))
            self.yy = links.go(p, p, to_y)

        def finish(self):
            self.yy.wait_recv()
            p = self.fin(1 - y)
            self.core.append(links.go(p, p, to_c))
            for copy in self.core[1:]:
                copy.wait_recv()

    reduce_o = AttnReduce(ACT, 0, 3)
    reduce_v = AttnReduce(ACT, 1, 2)
    reduce_k = AttnReduce(DG, 0, 1)
    reduce_q = AttnReduce(DG, 1, 0)
    reduce_nt.far[0].wait_recv()
    norm_two_back(0)
    mixed_back(0)
    attend_back(0)
    reduce_up.middle(3, 0) if A == 4 else reduce_up.middle(*range(3, A), 0)
    reduce_nt.far[1].wait_recv()
    norm_two_back(1)
    mixed_back(1)
    reduce_o.compute(lambda cols: QKVM[3, :, cols], lambda: PS[0])
    pl.semaphore_wait(credit.at[1], 1)
    reduce_o.start()
    attend_back(1)
    reduce_o.first()
    reduce_down.middle(1, 2)
    for k, red in ((2, reduce_v), (1, reduce_k), (0, reduce_q)):
        red.compute(lambda cols: N1[:, cols], lambda k=k: MG[k])
        red.start()
    reduce_v.first()
    reduce_up.last()
    reduce_k.first()
    reduce_down.middle(*range(3, A), 0)
    reduce_q.first()

    def output_step(i):
        rows = aligned(i * step_rows, step_rows)
        v = RT[rows, :].astype(f32)
        g = OG[rows, :].astype(f32)
        gate = GATE[rows, :]
        branch = AO[rows, :] + MO[rows, :] + YR[1, rows, :].astype(f32)
        lg = jnp.sum(g * branch, axis=-1, keepdims=True) * gate * (1.0 - gate)
        LG[rows, :] = lg
        SM[2:3] += jnp.sum(lg * v, axis=0, keepdims=True)
        QKVM[3, rows, :] = (v + gate * branch).astype(bf16)

    for copy in reduce_mo.far:
        copy.wait_recv()
    loop(4, output_step)
    new_copy = pltpu.make_async_copy(QKVM.at[3], r["new_rows"], local.at[0])
    new_copy.start()
    reduce_o.second()

    def norm_one_grad(j):
        rows = pl.ds(j * (Wd // 4), Wd // 4)
        v = dot(MG[0], WA[0, rows].reshape(quart, D), 1, 1)
        v = v + dot(MG[1], WA[1, rows].reshape(quart, D), 1, 1)
        v = v + dot(MG[2], WA[2, rows].reshape(quart, D), 1, 1)
        MO[:, aligned(j * quart, quart)] = v

    loop(4, norm_one_grad)
    reduce_up.finish()
    reduce_v.second()
    reduce_o.third()

    def norm_one_back(i):
        rows = aligned(i * step_rows, step_rows)
        dy = MO[rows, :]
        v = RT[rows, :].astype(f32)
        s1 = R1[rows, :]
        dyg = dy * r["GN"][0:1]
        mean = jnp.mean(dyg * v, axis=-1, keepdims=True)
        SM[0:1] += jnp.sum(dy * (v * s1), axis=0, keepdims=True)
        grad = s1 * dyg - v * (s1 * s1 * s1 * mean)
        grad = OG[rows, :].astype(f32) + NG[rows, :] + grad + LG[rows, :] * router_row
        QKVM[0, rows, :] = grad.astype(bf16)

    loop(4, norm_one_back)
    grad_copy = pltpu.make_async_copy(QKVM.at[0], r["row_grads"], local.at[1])
    grad_copy.start()

    total = lambda v: jnp.sum(jnp.sum(v, axis=1, keepdims=True), axis=0, keepdims=True)
    chosen = total(jnp.sum(SEGR[...], axis=0)[1:2])
    lanes = lax.broadcasted_iota(jnp.int32, (1, D), 1)
    SM[3:4] = (
        jnp.where(lanes == 0, chosen, 0.0)
        + jnp.where(lanes == 1, total(STAT[1:2]), 0.0)
        + jnp.where(lanes == 2, total(STAT[0:1]), 0.0)
    )
    SMS, SMR, SMZ = r["SMS"], r["SMR"], r["SMZ"]
    sums = [links.go(SM, SMR.at[0], to_c)]
    reduce_k.second()
    reduce_v.third()
    reduce_down.last()
    sums[0].wait_recv()
    SMS[0] = SM[...] + SMR[0]
    sums.append(links.go(SMS.at[0], SMR.at[1], to_x))
    reduce_q.second()
    reduce_k.third()
    reduce_o.last()
    sums[1].wait_recv()
    SMS[1] = SMS[0] + SMR[1]
    sums.append(links.go(SMS.at[1], SMR.at[2], to_y))
    reduce_v.last()
    reduce_down.finish()
    reduce_q.third()
    sums[2].wait_recv()
    SMZ[z] = SMS[1] + SMR[2]
    sums = [links.go(SMZ.at[z], SMZ.at[z], dev(ahead[dz], x, y, c)) for dz in range(1, A)]
    reduce_k.last()
    reduce_o.finish()
    reduce_v.finish()
    reduce_q.last()
    for copy in sums:
        copy.wait_recv()
    r["small"][...] = jnp.sum(SMZ[...], axis=0)
    reduce_k.finish()
    reduce_q.finish()
    outs = [
        pltpu.make_async_copy(r["FIN"], r["mlp_grads"], local.at[2]),
        pltpu.make_async_copy(r["FINA"], r["attn_grads"], local.at[3]),
    ]
    for copy in outs:
        copy.start()
    links.drain()
    for copy in outs + [new_copy, grad_copy]:
        copy.wait()
    for k, name in enumerate(DEBUG):
        copy = pltpu.make_async_copy(r[name], r["dbg_" + name], local.at[4])
        copy.start()
        copy.wait()


def finish_kernel(dims, slots, rows, row_grads, attn_grads, mlp_grads, small, base, base_grad,
                  out, out_grad, stats, router, gain_one, gain_two, attn_out, up_out, down_out,
                  attn_stage, up_stage, down_stage, sems):
    S, per, R, Wd, part = dims
    i = pl.program_id(0)
    s, k = i // per, i % per
    size, cap = base.shape[1], slots.shape[1]
    position = lax.broadcasted_iota(jnp.int32, (size, cap), 0) + k * size
    onehot = jnp.where(slots[pl.ds(s, 1), :] == position, 1.0, 0.0)
    hit = jnp.max(onehot, axis=-1, keepdims=True) > 0.5
    onehot = onehot.astype(bf16)
    own = aligned(s * cap, cap)
    for new, old, target in ((rows, base, out), (row_grads, base_grad, out_grad)):
        picked = dot(onehot, new[own, :], 1, 0).astype(bf16)
        target[0] = jnp.where(hit, picked, old[0])

    attn_copies = [
        pltpu.make_async_copy(attn_stage.at[g], attn_out[g], sems.at[g]) for g in range(4)
    ]
    down_copies = [
        pltpu.make_async_copy(down_stage.at[q], down_out.at[pl.ds(q * R, R)], sems.at[4 + q]) for q in range(4)
    ]
    up_copy = pltpu.make_async_copy(up_stage, up_out, sems.at[8])

    @pl.when(i == 0)
    def _():
        for g in range(4):
            attn_stage[g] = attn_grads[g].astype(f32)
            attn_copies[g].start()
        w = lax.axis_index("wide")
        gains = pltpu.roll(small[...], (small.shape[1] - w * R) % small.shape[1], 1)
        gain_one[...] = gains[0:1, :R]
        gain_two[...] = gains[1:2, :R]
        router[...] = small[2:3]
        lane = lax.broadcasted_iota(jnp.int32, (1, small.shape[1]), 1)
        counts = small[3:4]
        valid = jnp.sum(jnp.where(lane == 1, counts, 0.0), axis=1, keepdims=True)
        shifted = jnp.where(lane == 1, pltpu.roll(counts, small.shape[1] - 1, 1), counts)
        stats[...] = (shifted / valid)[:, : stats.shape[1]]

    @pl.when(i == 1)
    def _():
        for q in range(4):
            down_stage[q] = mlp_grads[1, q].astype(f32)
            down_copies[q].start()

    @pl.when(i == 2)
    def _():
        for q in range(4):
            for v in range(Wd):
                at = (v * 4 + q) * part
                up_stage[:, at : at + part] = mlp_grads[0, q, :, v * part : (v + 1) * part].astype(f32)
        up_copy.start()

    @pl.when(i == S * per - 1)
    def _():
        for copy in attn_copies + down_copies + [up_copy]:
            copy.wait()


def finish(mesh, res, slots, block_input, cotangent, R, FF):
    S, SEQ, D = block_input.shape
    Wd = mesh.shape["wide"]
    size = 1024
    per, part = SEQ // size, FF // (4 * Wd)

    def kernel(slots, rows, row_grads, attn, mlp, small, base, base_grad, out, out_grad, stats, router,
               gain_one, gain_two, q, k, v, o, up, down, *scratch):
        finish_kernel((S, per, R, Wd, part), slots, rows, row_grads, attn, mlp, small, base, base_grad,
                      out, out_grad, stats, router, gain_one, gain_two, (q, k, v, o), up, down, *scratch)

    vmem, hbm = pl.BlockSpec(memory_space=pltpu.VMEM), pl.BlockSpec(memory_space=pl.ANY)
    tile = pl.BlockSpec((1, size, D), lambda i: (i // per, i % per, 0))
    shape = jax.ShapeDtypeStruct
    return pl.pallas_call(
        kernel,
        grid=(S * per,),
        out_shape=[shape(block_input.shape, bf16)] * 2
        + [shape((1, 2), f32), shape((1, D), f32), shape((1, R), f32), shape((1, R), f32)]
        + [shape((R, D), f32)] * 4
        + [shape((R, FF), f32), shape((4 * R, D), f32)],
        in_specs=[vmem] * 6 + [tile] * 2,
        out_specs=[tile] * 2 + [vmem] * 4 + [hbm] * 6,
        scratch_shapes=[
            pltpu.VMEM((4, R, D), f32),
            pltpu.VMEM((R, FF), f32),
            pltpu.VMEM((4, R, D), f32),
            pltpu.SemaphoreType.DMA((9,)),
        ],
        compiler_params=pltpu.CompilerParams(vmem_limit_bytes=60 * MIB),
        name="finish_rows",
    )(slots, res["new_rows"], res["row_grads"], res["attn_grads"].reshape(4, R, D), res["mlp_grads"],
      res["small"], block_input, cotangent)


def run_block(mesh, inputs, S, SEQ, CAP, D, R):
    Wd = mesh.shape["wide"]
    A, RB, T = Wd // 2, R // 2, S * CAP
    dims = dict(A=A, R=R, T=T, S=S, CAP=CAP, SEQ=SEQ, D=D, RB=RB)
    out_shapes = {
        "new_rows": ((T, D), bf16),
        "row_grads": ((T, D), bf16),
        "mlp_grads": ((2, 4, R, D), bf16),
        "attn_grads": ((4, 2, RB, D), bf16),
        "small": ((8, D), f32),
    }
    scratch = {
        "WA": ((4, Wd, R, D), bf16),
        "WU": ((A, 2, R, D), bf16),
        "WD": ((A, 2, R, D), bf16),
        "GP": ((Wd, 8, D), f32),
        "GN": ((8, D), f32),
        "NT": ((4, A, 2, RB, D), bf16),
        "MG": ((4, T, D), bf16),
        "ACT": ((2, A, 2, 2, RB, D), bf16),
        "DG": ((2, A, 2, 2, RB, D), bf16),
        "QKVM": ((4, T, D), bf16),
        "N1": ((T, D), bf16),
        "RT": ((T, D), bf16),
        "OG": ((T, D), bf16),
        "AO": ((T, D), f32),
        "NG": ((T, D), f32),
        "MO": ((T, D), f32),
        "PS": ((2, T, D), bf16),
        "PR": ((2, T, D), bf16),
        "YS": ((T, D), bf16),
        "YS2": ((T, D), bf16),
        "YR": ((2, T, D), bf16),
        "GXR": ((A, R, D), bf16),
        "GZR": ((2, A - 1, R, D), bf16),
        "FIN": ((2, 4, R, D), bf16),
        "XRA": ((4, A // 4, RB, D), bf16),
        "YRA": ((4, A - A // 4, RB, D // 2), bf16),
        "YRB": ((4, A // 4, 2, RB, D // 2), bf16),
        "XRB": ((4, A // 4, RB, D // 2), bf16),
        "ZR": ((4, A - 1, RB, D // 2), bf16),
        "FINA": ((4, 2, RB, D), bf16),
        "COLS": ((T, LANES), f32),
        "BIAS": ((S, CAP, CAP), f32),
        "SEGR": ((S, 16, CAP), f32),
        "STAT": ((8, CHUNK), f32),
        "SM": ((8, D), f32),
        "SMS": ((2, 8, D), f32),
        "SMR": ((3, 8, D), f32),
        "SMZ": ((A, 8, D), f32),
    }
    for name in DEBUG:
        out_shapes["dbg_" + name] = scratch[name]
    count = copy_count(A)
    semaphores = {
        "send": pltpu.SemaphoreType.DMA((count,)),
        "recv": pltpu.SemaphoreType.DMA((count,)),
        "local": pltpu.SemaphoreType.DMA((11 + Wd,)),
        "credit": pltpu.SemaphoreType.REGULAR((3,)),
    }
    in_vmem = ("gains", "slots", "segments", "pad_mask")
    hbm, vmem = pl.BlockSpec(memory_space=pl.ANY), pl.BlockSpec(memory_space=pltpu.VMEM)
    names = list(inputs) + list(out_shapes) + list(scratch) + list(semaphores)
    results = pl.pallas_call(
        functools.partial(block_kernel, dims, names),
        out_shape=[jax.ShapeDtypeStruct(*v) for v in out_shapes.values()],
        in_specs=[vmem if k in in_vmem else hbm for k in inputs],
        out_specs=[vmem if k == "small" else hbm for k in out_shapes],
        scratch_shapes=[pltpu.VMEM(*v) for v in scratch.values()] + list(semaphores.values()),
        compiler_params=pltpu.CompilerParams(
            collective_id=0, has_side_effects=True, vmem_limit_bytes=64 * MIB - 65536
        ),
        name="routed_block",
    )(*inputs.values())
    return dict(zip(out_shapes, results))


def body(mesh, block_input, query_weight, key_weight, value_weight, out_weight, up_weight, down_weight,
         attn_gain, mlp_gain, router_weight, slots, segments, pad_mask, cotangent):
    S, SEQ, D = block_input.shape
    CAP = slots.shape[1]
    R, FF = up_weight.shape
    Wd = mesh.shape["wide"]
    w, n = lax.axis_index("wide"), lax.axis_index("narrow")
    part = FF // (4 * Wd)
    assert FF == 4 * D and S == 2 and 4 * CAP == D and part == R and mesh.shape["narrow"] == 4
    if part % LANES:
        up_weight = lax.dynamic_index_in_dim(up_weight.reshape(R, Wd, 4, part), n, axis=2, keepdims=False)
        up_weight = up_weight.reshape(R, D)
    shard = jnp.stack([attn_gain, mlp_gain]).astype(f32)
    line = lax.broadcasted_iota(jnp.int32, (8, D), 0)
    gains = jnp.where(line == 2, router_weight.astype(f32)[None], 0.0)
    gains = lax.dynamic_update_slice(gains, shard, (0, w * R))
    inputs = {
        "block_input": block_input,
        "cotangent": cotangent,
        "w_query": query_weight,
        "w_key": key_weight,
        "w_value": value_weight,
        "w_out": out_weight,
        "w_up": up_weight,
        "w_down": down_weight,
        "gains": gains,
        "slots": slots,
        "segments": segments,
        "pad_mask": pad_mask,
    }
    res = run_block(mesh, inputs, S, SEQ, CAP, D, R)
    outs = finish(mesh, res, slots, block_input, cotangent, R, FF)
    result = (outs[0], outs[1], *outs[6:], outs[4].reshape(R), outs[5].reshape(R), outs[3].reshape(D), outs[2].reshape(2))
    if DEBUG:
        return result, {k: res["dbg_" + k] for k in DEBUG}
    return result


def solution(mesh):
    rows, wide = P(("wide", "narrow")), P("wide")
    return jax.shard_map(
        functools.partial(body, mesh),
        mesh=mesh,
        in_specs=(rows,) + (wide,) * 8 + (P(),) + (rows,) * 4,
        out_specs=(rows, rows) + (wide,) * 8 + (P(), P()),
        check_vma=False,
    )
```

```python
import functools
import math

import jax
import jax.numpy as jnp
from jax import lax
from jax.experimental import pallas as pl
from jax.experimental.pallas import tpu as pltpu
from jax.sharding import PartitionSpec as P

HEADS = 16
HEAD_DIM = 64
EPS = 1e-06
LANES = 128
MESH = pl.DeviceIdType.MESH
f32 = jnp.float32
bf16 = jnp.bfloat16
MIB = 2**20
CHUNK = 512
DEBUG = ()


def dot(a, b, ca, cb):
    return lax.dot_general(a, b, (((ca,), (cb,)), ((), ())), preferred_element_type=f32)


def aligned(start, size):
    return pl.ds(pl.multiple_of(start, size), size)


def loop(count, step):
    def run(i, carry):
        step(i)
        return carry

    lax.fori_loop(0, count, run, 0)


class Column:
    def __init__(self, ref, lane):
        self.ref, self.lane = ref, slice(lane, lane + 1)

    def __getitem__(self, at):
        return self.ref[at[0], self.lane]

    def __setitem__(self, at, value):
        self.ref[at[0], self.lane] = value


class Links:
    def __init__(self, send, recv):
        self.send, self.recv, self.count, self.open = send, recv, 0, []

    def make(self, src, dst, device):
        i = self.count
        self.count += 1
        return pltpu.make_async_remote_copy(
            src_ref=src,
            dst_ref=dst,
            send_sem=self.send.at[i],
            recv_sem=self.recv.at[i],
            device_id=device,
            device_id_type=MESH,
        )

    def go(self, src, dst, device):
        copy = self.make(src, dst, device)
        copy.start()
        self.open.append(copy)
        return copy

    def sent(self, copy):
        copy.wait_send()
        self.open = [other for other in self.open if other is not copy]

    def sent_all(self, copies):
        for copy in copies:
            self.sent(copy)

    def drain(self):
        for copy in self.open:
            copy.wait_send()
        self.open = []


def copy_count(far):
    near = far - 1
    gather = 4 * (8 * near + 2) + 5 * (2 * near + 1)
    narrow = 2 * 6 + 2 * 4
    reduce_mlp = 2 * (far + near + 3)
    reduce_attn = 4 * (1 + 2 * far + near + 3)
    return gather + narrow + reduce_mlp + reduce_attn + 3 + near


def block_kernel(dims, names, *refs):
    r = dict(zip(names, refs))
    A, R, T, S, CAP, SEQ, D, RB = (
        dims[k] for k in ("A", "R", "T", "S", "CAP", "SEQ", "D", "RB")
    )
    Wd = 2 * A
    half, quart = D // 2, D // 4
    scale = 1.0 / math.sqrt(HEAD_DIM)
    w, n = lax.axis_index("wide"), lax.axis_index("narrow")
    z, x = w // 2, w % 2
    y, c = n // 2, n % 2
    WA, WU, WD, GP = r["WA"], r["WU"], r["WD"], r["GP"]
    NT, MG, ACT, DG = r["NT"], r["MG"], r["ACT"], r["DG"]
    QKVM, N1, RT, OG = r["QKVM"], r["N1"], r["RT"], r["OG"]
    AO, NG, MO = r["AO"], r["NG"], r["MO"]
    PS, PR, YS, YR = r["PS"], r["PR"], r["YS"], r["YR"]
    GATE, R1, R2, LG, SLOT = (Column(r["COLS"], k) for k in range(5))
    SEGR, STAT, SM = r["SEGR"], r["STAT"], r["SM"]
    local, credit = r["local"], r["credit"]
    links = Links(r["send"], r["recv"])

    def dev(zz, xx, yy, cc):
        return (zz * 2 + xx, yy * 2 + cc)

    to_x, to_y, to_c = dev(z, 1 - x, y, c), dev(z, x, 1 - y, c), dev(z, x, y, 1 - c)
    ahead = [(z + dz) % A for dz in range(A)]
    behind = [(z - dz + A) % A for dz in range(A)]

    own = [
        pltpu.make_async_copy(r["w_query"], WA.at[0, w], local.at[0]),
        pltpu.make_async_copy(r["w_key"], WA.at[1, w], local.at[1]),
        pltpu.make_async_copy(r["w_value"], WA.at[2, w], local.at[2]),
        pltpu.make_async_copy(r["w_out"], WA.at[3, w], local.at[3]),
        pltpu.make_async_copy(r["w_down"].at[aligned(n * R, R)], WD.at[z, x], local.at[5]),
        pltpu.make_async_copy(r["gains"], GP.at[w], local.at[6]),
    ]
    if r["w_up"].shape[1] == D:
        own.append(pltpu.make_async_copy(r["w_up"], WU.at[z, x], local.at[4]))
    else:
        own += [
            pltpu.make_async_copy(
                r["w_up"].at[:, aligned((v * 4 + n) * R, R)], WU.at[z, x, :, pl.ds(v * R, R)], local.at[11 + v]
            )
            for v in range(Wd)
        ]
    for copy in own:
        copy.start()
    fetches = {}

    def fetch(i, slot):
        s, k = i // (SEQ // CHUNK), i % (SEQ // CHUNK)
        return [
            pltpu.make_async_copy(
                r[name].at[s, aligned(k * CHUNK, CHUNK)], QKVM.at[2 * slot + a], local.at[7 + 2 * slot + a]
            )
            for a, name in enumerate(("block_input", "cotangent"))
        ]

    for copy in fetch(0, 0):
        copy.start()
    barrier = pltpu.get_barrier_semaphore()
    peers = [dev(ahead[dz], x, y, c) for dz in range(1, A)] + [to_x, to_y, to_c]
    for peer in peers:
        pl.semaphore_signal(barrier, inc=1, device_id=peer, device_id_type=MESH)
    pl.semaphore_wait(barrier, len(peers))
    for copy in own:
        copy.wait()

    class AttnGather:
        def __init__(self, first, count):
            self.first, self.count = first, count

        def piece(self, zz, xx, yy):
            return WA.at[pl.ds(self.first, self.count), zz * 2 + xx, :, aligned(c * half + yy * quart, quart)]

        def wide_piece(self, zz, xx):
            return WA.at[pl.ds(self.first, self.count), zz * 2 + xx, :, aligned(c * half, half)]

        def start(self):
            p, q = self.piece(z, x, y), self.wide_piece(z, x)
            self.far = {dz: links.go(p, p, dev(ahead[dz], x, y, c)) for dz in range(1, A)}
            self.x0 = links.go(q, q, to_x)
            self.x1, self.y1, self.second, self.core = {}, {}, {}, []

        def to_core(self, p):
            self.core.append(links.go(p, p, to_c))

        def relay(self, dz):
            self.far[dz].wait_recv()
            p = self.piece(behind[dz], x, y)
            self.x1[dz] = links.go(p, p, to_x)
            self.y1[dz] = links.go(p, p, to_y)
            self.to_core(p)

        def relay_own(self):
            self.x0.wait_recv()
            self.to_core(self.wide_piece(z, 1 - x))

        def relay_second(self, dz):
            self.x1[dz].wait_recv()
            p = self.piece(behind[dz], 1 - x, y)
            if dz % 2:
                self.second[dz] = links.go(p, p, to_y)
            self.to_core(p)
            self.y1[dz].wait_recv()
            p = self.piece(behind[dz], x, 1 - y)
            if not dz % 2:
                self.second[dz] = links.go(p, p, to_x)
            self.to_core(p)

        def relay_third(self, dz):
            self.second[dz].wait_recv()
            self.to_core(self.piece(behind[dz], 1 - x, 1 - y))

        def finish(self):
            for copy in self.core:
                copy.wait_recv()

    class WideGather:
        def __init__(self, at):
            self.at = at

        def start(self):
            p = self.at(z, x)
            self.far = {dz: links.go(p, p, dev(ahead[dz], x, y, c)) for dz in range(1, A)}
            self.near = []

        def start_near(self):
            p = self.at(z, x)
            self.near.append(links.go(p, p, to_x))

        def relay(self, dz):
            self.far[dz].wait_recv()
            p = self.at(behind[dz], x)
            self.near.append(links.go(p, p, to_x))

        def finish(self):
            for copy in self.near:
                copy.wait_recv()

        def release(self):
            links.sent_all(list(self.far.values()) + self.near)

    gains = WideGather(lambda zz, xx: GP.at[zz * 2 + xx])
    query, key, value, out = (AttnGather(g, 1) for g in range(4))
    attn = (query, key, value, out)
    up, down = (
        [WideGather(lambda zz, xx, ref=ref, h=h: ref.at[zz, xx, pl.ds(h * RB, RB)]) for h in range(2)]
        for ref in (WU, WD)
    )
    gains.start()
    gains.start_near()
    for group in attn:
        group.start()
    for part in up + down:
        part.start()

    AO[...] = jnp.zeros_like(AO)
    NG[...] = jnp.zeros_like(NG)
    SEGR[...] = jnp.zeros_like(SEGR)
    STAT[...] = jnp.zeros_like(STAT)
    eye = lax.broadcasted_iota(jnp.int32, (CAP, CAP), 0) == lax.broadcasted_iota(jnp.int32, (CAP, CAP), 1)

    def upright(row):
        return jnp.sum(jnp.where(eye, row, 0.0), axis=1, keepdims=True)

    for s in range(S):
        SLOT[pl.ds(s * CAP, CAP), :] = upright(r["slots"][s : s + 1, :].astype(f32))
    router_row = r["gains"][2:3]
    router_tile = jnp.broadcast_to(router_row, (16, D)).astype(bf16)
    steps = S * (SEQ // CHUNK)

    def gather_step(i):
        slot = i % 2
        s, k = i // (SEQ // CHUNK), i % (SEQ // CHUNK)

        @pl.when(i + 1 < steps)
        def _():
            for copy in fetch(i + 1, (i + 1) % 2):
                copy.start()

        for copy in fetch(i, slot):
            copy.wait()
        position = lax.broadcasted_iota(jnp.int32, (CAP, CHUNK), 1) + k * CHUNK
        rows = aligned(s * CAP, CAP)
        onehot = jnp.where(SLOT[rows, :].astype(jnp.int32) == position, 1.0, 0.0).astype(bf16)
        tokens = QKVM[2 * slot]
        AO[rows, :] += dot(onehot, tokens, 1, 0)
        NG[rows, :] += dot(onehot, QKVM[2 * slot + 1], 1, 0)
        at = (pl.ds(s, 1), aligned(k * CHUNK, CHUNK))
        segment, mask = r["segments"][at].astype(f32), r["pad_mask"][at].astype(f32)
        line = lax.broadcasted_iota(jnp.int32, (16, CHUNK), 0)
        marks = jnp.where(line == 0, segment, jnp.where(line == 1, mask, 0.0)).astype(bf16)
        gate_logits = dot(router_tile, tokens, 1, 1)[0:1]
        STAT[0:1] += mask * jax.nn.sigmoid(gate_logits)
        STAT[1:2] += mask
        SEGR[s] += dot(marks, onehot, 1, 1)

    def gather_steps(first, last):
        loop(last - first, lambda i: gather_step(i + first))

    far = range(1, A)
    gather_steps(0, 3)
    for dz in far:
        gains.relay(dz)
    for dz in far:
        query.relay(dz)
    gather_steps(3, 5)
    for dz in far:
        key.relay(dz)
    query.relay_own()
    for dz in far:
        query.relay_second(dz)
    gather_steps(5, 7)
    for dz in far:
        value.relay(dz)
    key.relay_own()
    for dz in far:
        key.relay_second(dz)
    for dz in far:
        query.relay_third(dz)
    gather_steps(7, steps)

    step_rows = T // 4

    def gate_step(i):
        rows = aligned(i * step_rows, step_rows)
        v, g = AO[rows, :], NG[rows, :]
        gate = jax.nn.sigmoid(jnp.sum(v * router_row, axis=-1, keepdims=True))
        GATE[rows, :] = gate
        R1[rows, :] = lax.rsqrt(jnp.mean(v * v, axis=-1, keepdims=True) + EPS)
        RT[rows, :] = v.astype(bf16)
        OG[rows, :] = g.astype(bf16)
        MG[n, rows, :] = (gate * g).astype(bf16)

    for dz in far:
        out.relay(dz)
    value.relay_own()
    for dz in far:
        value.relay_second(dz)
    for dz in far:
        key.relay_third(dz)
    loop(4, gate_step)

    class RowShare:
        def __init__(self, at):
            self.at = at

        def start(self, k):
            p = self.at(n, k)
            self.core = getattr(self, "core", {})
            self.far = getattr(self, "far", {})
            self.core[k] = links.go(p, p, to_c)
            self.far[k] = links.go(p, p, to_y)

        def relay(self, k):
            self.far[k].wait_recv()
            p = self.at((1 - y) * 2 + c, k)
            self.last = getattr(self, "last", {})
            self.last[k] = links.go(p, p, to_c)

        def release(self):
            for copies in (self.core, self.far, self.last):
                links.sent_all(list(copies.values()))

    share_mg = RowShare(lambda b, k: MG.at[b, pl.ds(k * CAP, CAP)])
    share_nt = RowShare(lambda b, k: NT.at[b, pl.ds(k * (A // 2), A // 2)])
    gains.finish()
    r["GN"][...] = jnp.sum(GP[...], axis=0)

    def norm_one_step(i):
        rows = aligned(i * step_rows, step_rows)
        N1[rows, :] = (RT[rows, :].astype(f32) * R1[rows, :] * r["GN"][0:1]).astype(bf16)

    loop(4, norm_one_step)
    ordered = lax.broadcasted_iota(jnp.int32, (CAP, CAP), 0) <= lax.broadcasted_iota(jnp.int32, (CAP, CAP), 1)
    for s in range(S):
        same = upright(SEGR[s][0:1]) == SEGR[s][0:1]
        r["BIAS"][s] = jnp.where(ordered & same, 0.0, -1e30)
    out.relay_own()
    for dz in far:
        out.relay_second(dz)
    for dz in far:
        value.relay_third(dz)
    for dz in far:
        out.relay_third(dz)
    for part in up + down:
        part.start_near()
    for k in range(2):
        share_mg.start(k)

    def project(g):
        def step(j):
            cols = aligned(j * half, half)
            QKVM[g, :, cols] = dot(N1[...], WA[g, :, :, cols].reshape(D, half), 1, 0).astype(bf16)

        loop(2, step)

    for g in range(3):
        attn[g].finish()
        project(g)

    lane = lax.broadcasted_iota(jnp.int32, (1, LANES), 1)
    low_lanes = lane < HEAD_DIM

    def pick(h, v):
        return jnp.where(low_lanes if h == 0 else ~low_lanes, v, jnp.zeros_like(v))

    def softmax_of(s, q, k, h):
        logits = dot(k, pick(h, q), 1, 1) + r["BIAS"][s]
        e = jnp.exp(logits - jnp.max(logits, axis=0, keepdims=True))
        return e * (1.0 / jnp.sum(e, axis=0, keepdims=True))

    group = 4

    def attend(s):
        def step(i):
            for u in range(group):
                rows, cols = pl.ds(s * CAP, CAP), aligned((i * group + u) * LANES, LANES)
                q, k, v = QKVM[0, rows, cols] * bf16(scale), QKVM[1, rows, cols], QKVM[2, rows, cols]
                o = [dot(softmax_of(s, q, k, h).astype(bf16), v, 0, 0) for h in range(2)]
                QKVM[3, rows, cols] = jnp.where(low_lanes, o[0], o[1]).astype(bf16)

        loop(D // LANES // group, step)

    def project_out(s):
        rows = pl.ds(s * CAP, CAP)

        def step(j):
            cols = aligned(j * half, half)
            AO[rows, cols] = dot(QKVM[3, rows, :], WA[3, :, :, cols].reshape(D, half), 1, 0)

        loop(2, step)

    def norm_two(k):
        def step(i):
            rows = aligned(k * CAP + i * (CAP // 2), CAP // 2)
            v = RT[rows, :].astype(f32) + AO[rows, :]
            scale_two = lax.rsqrt(jnp.mean(v * v, axis=-1, keepdims=True) + EPS)
            R2[rows, :] = scale_two
            part = (v * scale_two * r["GN"][1:2]).astype(bf16)
            NT[n, pl.ds(k * (A // 2) + i * (A // 4), A // 4)] = part.reshape(A // 4, 2, RB, D)

        loop(2, step)

    attend(0)
    out.finish()
    project_out(0)
    norm_two(0)
    share_nt.start(0)
    for part in up:
        for dz in far:
            part.relay(dz)
    attend(1)
    project_out(1)
    norm_two(1)
    share_nt.start(1)
    for dz in far:
        down[0].relay(dz)

    tanh_k = math.sqrt(2.0 / math.pi)

    def up_unit(yy, k):
        rows = NT.at[pl.ds(yy * 2, 2), pl.ds(k * (A // 2), A // 2)]
        parts = [pl.ds(cc * (A // 2) + k * (A // 4), A // 4) for cc in range(2)]

        def step(j):
            cols = aligned(j * quart, quart)
            v = dot(rows[...].reshape(T, D), WU[:, :, :, cols].reshape(D, quart), 1, 0)
            vv = v * v
            t = jnp.tanh(v * (tanh_k + (tanh_k * 0.044715) * vv))
            act = 0.5 * v * (1.0 + t)
            slope = (0.5 + 0.5 * t) * (1.0 + v * (1.0 - t) * (tanh_k + (tanh_k * 0.134145) * vv))
            for cc in range(2):
                at = slice(cc * CAP, (cc + 1) * CAP)
                ACT[yy, parts[cc], :, :, :, cols] = act[at].astype(bf16).reshape(A // 4, 2, 2, RB, quart)
                DG[yy, parts[cc], :, :, :, cols] = slope[at].astype(bf16).reshape(A // 4, 2, 2, RB, quart)

        loop(4, step)

    def act_unit(yy):
        def step(j):
            cols = aligned(j * quart, quart)
            rows = WD[pl.ds(j * (A // 4), A // 4)].reshape(quart, D)
            v = dot(MG[pl.ds(yy * 2, 2)].reshape(2 * T, D), rows, 1, 1)
            slope = DG[yy, :, :, :, :, cols].reshape(2 * T, quart).astype(f32)
            DG[yy, :, :, :, :, cols] = (v * slope).astype(bf16).reshape(A, 2, 2, RB, quart)

        loop(4, step)

    for k in range(2):
        share_mg.relay(k)
        share_nt.core[k].wait_recv()
        share_mg.core[k].wait_recv()
    for part in up:
        part.finish()
    up_unit(y, 0)
    for dz in far:
        down[1].relay(dz)
    up_unit(y, 1)
    share_nt.relay(0)
    share_nt.last[0].wait_recv()
    up_unit(1 - y, 0)
    for k in range(2):
        share_mg.last[k].wait_recv()
    share_nt.relay(1)
    share_nt.last[1].wait_recv()
    up_unit(1 - y, 1)
    for part in down:
        part.finish()
    act_unit(1 - y)
    act_unit(y)

    class NarrowReduce:
        def __init__(self, lhs, part, send, k, total):
            self.lhs, self.part, self.send, self.k, self.total = lhs, part, send, k, total
            self.core, self.far = [], []

        def compute(self, q):
            yy = y if q else 1 - y
            keep = self.total if q else MO

            def step(j):
                cols = aligned(j * quart, quart)
                v = self.part(self.lhs[yy].reshape(2 * T, D), j, cols)
                PS[q, :, cols] = jnp.where(c == 0, v[T:], v[:T]).astype(bf16)
                keep[:, cols] = jnp.where(c == 0, v[:T], v[T:])

            loop(4, step)
            self.core.append(links.go(PS.at[q], PR.at[q], to_c))

        def send_far(self):
            self.core[0].wait_recv()
            for k in range(2):
                rows = pl.ds(k * CAP, CAP)
                self.send[rows, :] = (MO[rows, :] + PR[0, rows, :].astype(f32)).astype(bf16)
                self.far.append(links.go(self.send.at[rows], YR.at[self.k, rows], to_y))

        def keep_own(self):
            self.core[1].wait_recv()
            for k in range(2):
                rows = pl.ds(k * CAP, CAP)
                self.total[rows, :] = self.total[rows, :] + PR[1, rows, :].astype(f32)

    def norm_two_part(rows, j, cols):
        return dot(rows, WU[pl.ds(j * (A // 4), A // 4)].reshape(quart, D), 1, 1)

    def mlp_part(rows, j, cols):
        return dot(rows, WD[:, :, :, cols].reshape(D, quart), 1, 0)

    reduce_nt = NarrowReduce(DG, norm_two_part, YS, 0, NG)
    reduce_nt.compute(0)
    reduce_nt.compute(1)
    reduce_nt.send_far()
    reduce_nt.keep_own()
    pl.semaphore_signal(credit.at[0], inc=1, device_id=to_c, device_id_type=MESH)

    class WideReduce:
        def __init__(self, grad, k):
            self.grad, self.k = grad, k

        def landing(self, dz):
            return PR.at[0, pl.ds(dz * R, R)] if self.k else r["GXR"].at[dz]

        def compute(self, lhs, rhs):
            def step(i):
                cols = aligned(i * quart, quart)
                v = dot(lhs(cols), rhs(), 0, 0)
                self.grad[pl.ds(i * (A // 4), A // 4)] = v.astype(bf16).reshape(A // 4, 2, R, D)

            loop(4, step)

        def start(self):
            self.x, self.far = {}, {}
            for dz in list(range(1, A)) + [0]:
                self.x[dz] = links.go(self.grad.at[ahead[dz], 1 - x], self.landing(dz), to_x)

        def middle(self, *dzs):
            for dz in dzs:
                self.x[dz].wait_recv()
                p = self.grad.at[ahead[dz], x]
                p[...] = (p[...].astype(f32) + self.landing(dz)[...].astype(f32)).astype(bf16)
                if dz:
                    self.far[dz] = links.go(p, r["GZR"].at[self.k, dz - 1], dev(ahead[dz], x, y, c))

        def last(self):
            total = self.grad[z, x].astype(f32)
            for dz in range(1, A):
                self.far[dz].wait_recv()
                total = total + r["GZR"][self.k, dz - 1].astype(f32)
            r["FIN"][self.k, n] = total.astype(bf16)
            p = r["FIN"].at[self.k, n]
            self.core = [links.go(p, p, to_c)]
            self.yy = links.go(p, p, to_y)

        def finish(self):
            self.yy.wait_recv()
            p = r["FIN"].at[self.k, (1 - y) * 2 + c]
            self.core.append(links.go(p, p, to_c))
            for copy in self.core:
                copy.wait_recv()

    reduce_up, reduce_down = WideReduce(WU, 0), WideReduce(WD, 1)
    for part in up:
        part.release()
    reduce_up.compute(lambda cols: NT[..., cols].reshape(4 * T, quart), lambda: DG[...].reshape(4 * T, D))
    reduce_up.start()
    share_nt.release()
    pl.semaphore_signal(credit.at[1], inc=1, device_id=to_c, device_id_type=MESH)

    reduce_mo = NarrowReduce(ACT, mlp_part, r["YS2"], 1, MO)
    pl.semaphore_wait(credit.at[0], 1)
    links.sent_all(reduce_nt.core)
    reduce_mo.compute(0)
    reduce_up.middle(1)
    reduce_mo.send_far()
    reduce_mo.compute(1)
    reduce_mo.keep_own()
    pl.semaphore_signal(credit.at[2], inc=1, device_id=to_x, device_id_type=MESH)
    for part in down:
        part.release()
    reduce_down.compute(lambda cols: ACT[..., cols].reshape(4 * T, quart), lambda: MG[...].reshape(4 * T, D))
    pl.semaphore_wait(credit.at[2], 1)
    reduce_down.start()
    reduce_up.middle(2)
    links.sent_all(reduce_mo.core)
    share_mg.release()
    SM[...] = jnp.zeros_like(SM)

    def norm_two_back(s):
        def step(i):
            rows = aligned(s * CAP + i * step_rows, step_rows)
            dy = NG[rows, :] + YR[0, rows, :].astype(f32)
            v = RT[rows, :].astype(f32) + AO[rows, :]
            s2 = R2[rows, :]
            dyg = dy * r["GN"][1:2]
            mean = jnp.mean(dyg * v, axis=-1, keepdims=True)
            grad = s2 * dyg - v * (s2 * s2 * s2 * mean)
            SM[1:2] += jnp.sum(dy * (v * s2), axis=0, keepdims=True)
            NG[rows, :] = grad
            PS[0, rows, :] = (GATE[rows, :] * OG[rows, :].astype(f32) + grad).astype(bf16)

        loop(2, step)

    def mixed_back(s):
        rows = pl.ds(s * CAP, CAP)

        def step(j):
            weight = WA[3, pl.ds(j * (Wd // 2), Wd // 2)].reshape(half, D)
            MG[3, rows, aligned(j * half, half)] = dot(PS[0, rows, :], weight, 1, 1).astype(bf16)

        loop(2, step)

    def attend_back(s):
        def step(i):
            for u in range(group):
                rows, cols = pl.ds(s * CAP, CAP), aligned((i * group + u) * LANES, LANES)
                q, k, v = QKVM[0, rows, cols] * bf16(scale), QKVM[1, rows, cols], QKVM[2, rows, cols]
                dm = MG[3, rows, cols]
                k_t = k.T
                dq, dk, dv = [], [], []
                for h in range(2):
                    p = softmax_of(s, q, k, h)
                    dp = dot(v, pick(h, dm), 1, 1)
                    dl = (p * (dp - jnp.sum(p * dp, axis=0, keepdims=True))).astype(bf16)
                    dq.append(dot(k_t[h * HEAD_DIM : (h + 1) * HEAD_DIM], dl, 1, 0))
                    dk.append(dot(dl, q, 1, 0))
                    dv.append(dot(p.astype(bf16), dm, 1, 0))
                MG[0, rows, cols] = (jnp.concatenate(dq, axis=0) * scale).astype(bf16).T
                MG[1, rows, cols] = jnp.where(low_lanes, dk[0], dk[1]).astype(bf16)
                MG[2, rows, cols] = jnp.where(low_lanes, dv[0], dv[1]).astype(bf16)

        loop(D // LANES // group, step)

    x_first = A // 2

    class AttnReduce:
        def __init__(self, buf, at, k):
            self.buf, self.at, self.k = buf, at, k

        def compute(self, lhs, rhs):
            def step(i):
                cols = aligned(i * quart, quart)
                v = dot(lhs(cols), rhs(), 0, 0)
                self.buf[self.at, pl.ds(i * (A // 4), A // 4)] = v.astype(bf16).reshape(A // 4, 2, 2, RB, D)

            loop(4, step)

        def landing(self, d):
            return PR.at[1, pl.ds((self.k * (A // 2) + d) * RB, RB)]

        def start(self):
            self.core = [links.go(self.buf.at[self.at, :, :, 1 - c], NT.at[self.k], to_c)]

        def part(self, zz, xx, cols=None):
            if cols is None:
                return self.buf.at[self.at, zz, xx, c]
            return self.buf.at[self.at, zz, xx, c, :, aligned(cols * half, half)]

        def first(self):
            self.core[0].wait_recv()

            def step(i):
                p = self.buf.at[self.at, i // 2, i % 2, c]
                p[...] = (p[...].astype(f32) + NT[self.k, i // 2, i % 2].astype(f32)).astype(bf16)

            loop(2 * A, step)
            self.one, self.two, self.far = {}, {}, {}
            for dz in range(A):
                d = (dz + 1) % A
                zz = ahead[d]
                if d < x_first:
                    self.one[d] = links.go(self.part(zz, 1 - x), self.landing(d), to_x)
                else:
                    e = d - x_first
                    cols = aligned((1 - y) * half, half)
                    self.one[d] = links.go(self.buf.at[self.at, zz, :, c, :, cols], r["YRB"].at[self.k, e], to_y)

        def add(self, p, q):
            p[...] = (p[...].astype(f32) + q[...].astype(f32)).astype(bf16)

        def second(self):
            for dz in range(A):
                d = (dz + 1) % A
                zz = ahead[d]
                self.one[d].wait_recv()
                if d < x_first:
                    self.add(self.part(zz, x), self.landing(d))
                    self.two[d] = links.go(self.part(zz, x, 1 - y), r["YRA"].at[self.k, d], to_y)
                else:
                    e = d - x_first
                    p = self.buf.at[self.at, zz, :, c, :, aligned(y * half, half)]
                    self.add(p, r["YRB"].at[self.k, e])
                    self.two[d] = links.go(self.part(zz, 1 - x, y), r["XRB"].at[self.k, e], to_x)

        def third(self):
            for dz in range(A):
                d = (dz + 1) % A
                zz = ahead[d]
                self.two[d].wait_recv()
                p = self.part(zz, x, y)
                self.add(p, r["YRA"].at[self.k, d] if d < x_first else r["XRB"].at[self.k, d - x_first])
                if d:
                    self.far[d] = links.go(p, r["ZR"].at[self.k, d - 1], dev(zz, x, y, c))

        def fin(self, yy):
            return r["FINA"].at[self.k, c, :, aligned(yy * half, half)]

        def last(self):
            total = self.part(z, x, y)[...].astype(f32)
            for d in range(1, A):
                self.far[d].wait_recv()
                total = total + r["ZR"][self.k, d - 1].astype(f32)
            p = self.fin(y)
            p[...] = total.astype(bf16)
            self.core.append(links.go(p, p, to_c))
            self.yy = links.go(p, p, to_y)

        def finish(self):
            self.yy.wait_recv()
            p = self.fin(1 - y)
            self.core.append(links.go(p, p, to_c))
            for copy in self.core[1:]:
                copy.wait_recv()

    reduce_o = AttnReduce(ACT, 0, 3)
    reduce_v = AttnReduce(ACT, 1, 2)
    reduce_k = AttnReduce(DG, 0, 1)
    reduce_q = AttnReduce(DG, 1, 0)
    reduce_nt.far[0].wait_recv()
    norm_two_back(0)
    mixed_back(0)
    attend_back(0)
    reduce_up.middle(3, 0) if A == 4 else reduce_up.middle(*range(3, A), 0)
    reduce_nt.far[1].wait_recv()
    norm_two_back(1)
    mixed_back(1)
    reduce_o.compute(lambda cols: QKVM[3, :, cols], lambda: PS[0])
    pl.semaphore_wait(credit.at[1], 1)
    reduce_o.start()
    attend_back(1)
    reduce_o.first()
    reduce_down.middle(1, 2)
    for k, red in ((2, reduce_v), (1, reduce_k), (0, reduce_q)):
        red.compute(lambda cols: N1[:, cols], lambda k=k: MG[k])
        red.start()
    reduce_v.first()
    reduce_up.last()
    reduce_k.first()
    reduce_down.middle(*range(3, A), 0)
    reduce_q.first()

    def output_step(i):
        rows = aligned(i * step_rows, step_rows)
        v = RT[rows, :].astype(f32)
        g = OG[rows, :].astype(f32)
        gate = GATE[rows, :]
        branch = AO[rows, :] + MO[rows, :] + YR[1, rows, :].astype(f32)
        lg = jnp.sum(g * branch, axis=-1, keepdims=True) * gate * (1.0 - gate)
        LG[rows, :] = lg
        SM[2:3] += jnp.sum(lg * v, axis=0, keepdims=True)
        QKVM[3, rows, :] = (v + gate * branch).astype(bf16)

    for copy in reduce_mo.far:
        copy.wait_recv()
    loop(4, output_step)
    new_copy = pltpu.make_async_copy(QKVM.at[3], r["new_rows"], local.at[0])
    new_copy.start()
    reduce_o.second()

    def norm_one_grad(j):
        rows = pl.ds(j * (Wd // 4), Wd // 4)
        v = dot(MG[0], WA[0, rows].reshape(quart, D), 1, 1)
        v = v + dot(MG[1], WA[1, rows].reshape(quart, D), 1, 1)
        v = v + dot(MG[2], WA[2, rows].reshape(quart, D), 1, 1)
        MO[:, aligned(j * quart, quart)] = v

    loop(4, norm_one_grad)
    reduce_up.finish()
    reduce_v.second()
    reduce_o.third()

    def norm_one_back(i):
        rows = aligned(i * step_rows, step_rows)
        dy = MO[rows, :]
        v = RT[rows, :].astype(f32)
        s1 = R1[rows, :]
        dyg = dy * r["GN"][0:1]
        mean = jnp.mean(dyg * v, axis=-1, keepdims=True)
        SM[0:1] += jnp.sum(dy * (v * s1), axis=0, keepdims=True)
        grad = s1 * dyg - v * (s1 * s1 * s1 * mean)
        grad = OG[rows, :].astype(f32) + NG[rows, :] + grad + LG[rows, :] * router_row
        QKVM[0, rows, :] = grad.astype(bf16)

    loop(4, norm_one_back)
    grad_copy = pltpu.make_async_copy(QKVM.at[0], r["row_grads"], local.at[1])
    grad_copy.start()

    total = lambda v: jnp.sum(jnp.sum(v, axis=1, keepdims=True), axis=0, keepdims=True)
    chosen = total(jnp.sum(SEGR[...], axis=0)[1:2])
    lanes = lax.broadcasted_iota(jnp.int32, (1, D), 1)
    SM[3:4] = (
        jnp.where(lanes == 0, chosen, 0.0)
        + jnp.where(lanes == 1, total(STAT[1:2]), 0.0)
        + jnp.where(lanes == 2, total(STAT[0:1]), 0.0)
    )
    SMS, SMR, SMZ = r["SMS"], r["SMR"], r["SMZ"]
    sums = [links.go(SM, SMR.at[0], to_c)]
    reduce_k.second()
    reduce_v.third()
    reduce_down.last()
    sums[0].wait_recv()
    SMS[0] = SM[...] + SMR[0]
    sums.append(links.go(SMS.at[0], SMR.at[1], to_x))
    reduce_q.second()
    reduce_k.third()
    reduce_o.last()
    sums[1].wait_recv()
    SMS[1] = SMS[0] + SMR[1]
    sums.append(links.go(SMS.at[1], SMR.at[2], to_y))
    reduce_v.last()
    reduce_down.finish()
    reduce_q.third()
    sums[2].wait_recv()
    SMZ[z] = SMS[1] + SMR[2]
    sums = [links.go(SMZ.at[z], SMZ.at[z], dev(ahead[dz], x, y, c)) for dz in range(1, A)]
    reduce_k.last()
    reduce_o.finish()
    reduce_v.finish()
    reduce_q.last()
    for copy in sums:
        copy.wait_recv()
    r["small"][...] = jnp.sum(SMZ[...], axis=0)
    reduce_k.finish()
    reduce_q.finish()
    outs = [
        pltpu.make_async_copy(r["FIN"], r["mlp_grads"], local.at[2]),
        pltpu.make_async_copy(r["FINA"], r["attn_grads"], local.at[3]),
    ]
    for copy in outs:
        copy.start()
    links.drain()
    for copy in outs + [new_copy, grad_copy]:
        copy.wait()
    for k, name in enumerate(DEBUG):
        copy = pltpu.make_async_copy(r[name], r["dbg_" + name], local.at[4])
        copy.start()
        copy.wait()


def finish_kernel(dims, slots, rows, row_grads, attn_grads, mlp_grads, small, base, base_grad,
                  out, out_grad, stats, router, gain_one, gain_two, attn_out, up_out, down_out,
                  attn_stage, up_stage, down_stage, sems):
    S, per, R, Wd, part = dims
    i = pl.program_id(0)
    s, k = i // per, i % per
    size, cap = base.shape[1], slots.shape[1]
    position = lax.broadcasted_iota(jnp.int32, (size, cap), 0) + k * size
    onehot = jnp.where(slots[pl.ds(s, 1), :] == position, 1.0, 0.0)
    hit = jnp.max(onehot, axis=-1, keepdims=True) > 0.5
    onehot = onehot.astype(bf16)
    own = aligned(s * cap, cap)
    for new, old, target in ((rows, base, out), (row_grads, base_grad, out_grad)):
        picked = dot(onehot, new[own, :], 1, 0).astype(bf16)
        target[0] = jnp.where(hit, picked, old[0])

    attn_copies = [
        pltpu.make_async_copy(attn_stage.at[g], attn_out[g], sems.at[g]) for g in range(4)
    ]
    down_copies = [
        pltpu.make_async_copy(down_stage.at[q], down_out.at[pl.ds(q * R, R)], sems.at[4 + q]) for q in range(4)
    ]
    up_copy = pltpu.make_async_copy(up_stage, up_out, sems.at[8])

    @pl.when(i == 0)
    def _():
        for g in range(4):
            attn_stage[g] = attn_grads[g].astype(f32)
            attn_copies[g].start()
        w = lax.axis_index("wide")
        gains = pltpu.roll(small[...], (small.shape[1] - w * R) % small.shape[1], 1)
        gain_one[...] = gains[0:1, :R]
        gain_two[...] = gains[1:2, :R]
        router[...] = small[2:3]
        lane = lax.broadcasted_iota(jnp.int32, (1, small.shape[1]), 1)
        counts = small[3:4]
        valid = jnp.sum(jnp.where(lane == 1, counts, 0.0), axis=1, keepdims=True)
        shifted = jnp.where(lane == 1, pltpu.roll(counts, small.shape[1] - 1, 1), counts)
        stats[...] = (shifted / valid)[:, : stats.shape[1]]

    @pl.when(i == 1)
    def _():
        for q in range(4):
            down_stage[q] = mlp_grads[1, q].astype(f32)
            down_copies[q].start()

    @pl.when(i == 2)
    def _():
        for q in range(4):
            for v in range(Wd):
                at = (v * 4 + q) * part
                up_stage[:, at : at + part] = mlp_grads[0, q, :, v * part : (v + 1) * part].astype(f32)
        up_copy.start()

    @pl.when(i == S * per - 1)
    def _():
        for copy in attn_copies + down_copies + [up_copy]:
            copy.wait()


def finish(mesh, res, slots, block_input, cotangent, R, FF):
    S, SEQ, D = block_input.shape
    Wd = mesh.shape["wide"]
    size = 1024
    per, part = SEQ // size, FF // (4 * Wd)

    def kernel(slots, rows, row_grads, attn, mlp, small, base, base_grad, out, out_grad, stats, router,
               gain_one, gain_two, q, k, v, o, up, down, *scratch):
        finish_kernel((S, per, R, Wd, part), slots, rows, row_grads, attn, mlp, small, base, base_grad,
                      out, out_grad, stats, router, gain_one, gain_two, (q, k, v, o), up, down, *scratch)

    vmem, hbm = pl.BlockSpec(memory_space=pltpu.VMEM), pl.BlockSpec(memory_space=pl.ANY)
    tile = pl.BlockSpec((1, size, D), lambda i: (i // per, i % per, 0))
    shape = jax.ShapeDtypeStruct
    return pl.pallas_call(
        kernel,
        grid=(S * per,),
        out_shape=[shape(block_input.shape, bf16)] * 2
        + [shape((1, 2), f32), shape((1, D), f32), shape((1, R), f32), shape((1, R), f32)]
        + [shape((R, D), f32)] * 4
        + [shape((R, FF), f32), shape((4 * R, D), f32)],
        in_specs=[vmem] * 6 + [tile] * 2,
        out_specs=[tile] * 2 + [vmem] * 4 + [hbm] * 6,
        scratch_shapes=[
            pltpu.VMEM((4, R, D), f32),
            pltpu.VMEM((R, FF), f32),
            pltpu.VMEM((4, R, D), f32),
            pltpu.SemaphoreType.DMA((9,)),
        ],
        compiler_params=pltpu.CompilerParams(vmem_limit_bytes=60 * MIB),
        name="finish_rows",
    )(slots, res["new_rows"], res["row_grads"], res["attn_grads"].reshape(4, R, D), res["mlp_grads"],
      res["small"], block_input, cotangent)


def run_block(mesh, inputs, S, SEQ, CAP, D, R):
    Wd = mesh.shape["wide"]
    A, RB, T = Wd // 2, R // 2, S * CAP
    dims = dict(A=A, R=R, T=T, S=S, CAP=CAP, SEQ=SEQ, D=D, RB=RB)
    out_shapes = {
        "new_rows": ((T, D), bf16),
        "row_grads": ((T, D), bf16),
        "mlp_grads": ((2, 4, R, D), bf16),
        "attn_grads": ((4, 2, RB, D), bf16),
        "small": ((8, D), f32),
    }
    scratch = {
        "WA": ((4, Wd, R, D), bf16),
        "WU": ((A, 2, R, D), bf16),
        "WD": ((A, 2, R, D), bf16),
        "GP": ((Wd, 8, D), f32),
        "GN": ((8, D), f32),
        "NT": ((4, A, 2, RB, D), bf16),
        "MG": ((4, T, D), bf16),
        "ACT": ((2, A, 2, 2, RB, D), bf16),
        "DG": ((2, A, 2, 2, RB, D), bf16),
        "QKVM": ((4, T, D), bf16),
        "N1": ((T, D), bf16),
        "RT": ((T, D), bf16),
        "OG": ((T, D), bf16),
        "AO": ((T, D), f32),
        "NG": ((T, D), f32),
        "MO": ((T, D), f32),
        "PS": ((2, T, D), bf16),
        "PR": ((2, T, D), bf16),
        "YS": ((T, D), bf16),
        "YS2": ((T, D), bf16),
        "YR": ((2, T, D), bf16),
        "GXR": ((A, R, D), bf16),
        "GZR": ((2, A - 1, R, D), bf16),
        "FIN": ((2, 4, R, D), bf16),
        "YRA": ((4, A // 2, RB, D // 2), bf16),
        "YRB": ((4, A // 2, 2, RB, D // 2), bf16),
        "XRB": ((4, A // 2, RB, D // 2), bf16),
        "ZR": ((4, A - 1, RB, D // 2), bf16),
        "FINA": ((4, 2, RB, D), bf16),
        "COLS": ((T, LANES), f32),
        "BIAS": ((S, CAP, CAP), f32),
        "SEGR": ((S, 16, CAP), f32),
        "STAT": ((8, CHUNK), f32),
        "SM": ((8, D), f32),
        "SMS": ((2, 8, D), f32),
        "SMR": ((3, 8, D), f32),
        "SMZ": ((A, 8, D), f32),
    }
    for name in DEBUG:
        out_shapes["dbg_" + name] = scratch[name]
    count = copy_count(A)
    semaphores = {
        "send": pltpu.SemaphoreType.DMA((count,)),
        "recv": pltpu.SemaphoreType.DMA((count,)),
        "local": pltpu.SemaphoreType.DMA((11 + Wd,)),
        "credit": pltpu.SemaphoreType.REGULAR((3,)),
    }
    in_vmem = ("gains", "slots", "segments", "pad_mask")
    hbm, vmem = pl.BlockSpec(memory_space=pl.ANY), pl.BlockSpec(memory_space=pltpu.VMEM)
    names = list(inputs) + list(out_shapes) + list(scratch) + list(semaphores)
    results = pl.pallas_call(
        functools.partial(block_kernel, dims, names),
        out_shape=[jax.ShapeDtypeStruct(*v) for v in out_shapes.values()],
        in_specs=[vmem if k in in_vmem else hbm for k in inputs],
        out_specs=[vmem if k == "small" else hbm for k in out_shapes],
        scratch_shapes=[pltpu.VMEM(*v) for v in scratch.values()] + list(semaphores.values()),
        compiler_params=pltpu.CompilerParams(
            collective_id=0, has_side_effects=True, vmem_limit_bytes=64 * MIB - 65536
        ),
        name="routed_block",
    )(*inputs.values())
    return dict(zip(out_shapes, results))


def body(mesh, block_input, query_weight, key_weight, value_weight, out_weight, up_weight, down_weight,
         attn_gain, mlp_gain, router_weight, slots, segments, pad_mask, cotangent):
    S, SEQ, D = block_input.shape
    CAP = slots.shape[1]
    R, FF = up_weight.shape
    Wd = mesh.shape["wide"]
    w, n = lax.axis_index("wide"), lax.axis_index("narrow")
    part = FF // (4 * Wd)
    assert FF == 4 * D and S == 2 and 4 * CAP == D and part == R and mesh.shape["narrow"] == 4
    if part % LANES:
        up_weight = lax.dynamic_index_in_dim(up_weight.reshape(R, Wd, 4, part), n, axis=2, keepdims=False)
        up_weight = up_weight.reshape(R, D)
    shard = jnp.stack([attn_gain, mlp_gain]).astype(f32)
    line = lax.broadcasted_iota(jnp.int32, (8, D), 0)
    gains = jnp.where(line == 2, router_weight.astype(f32)[None], 0.0)
    gains = lax.dynamic_update_slice(gains, shard, (0, w * R))
    inputs = {
        "block_input": block_input,
        "cotangent": cotangent,
        "w_query": query_weight,
        "w_key": key_weight,
        "w_value": value_weight,
        "w_out": out_weight,
        "w_up": up_weight,
        "w_down": down_weight,
        "gains": gains,
        "slots": slots,
        "segments": segments,
        "pad_mask": pad_mask,
    }
    res = run_block(mesh, inputs, S, SEQ, CAP, D, R)
    outs = finish(mesh, res, slots, block_input, cotangent, R, FF)
    result = (outs[0], outs[1], *outs[6:], outs[4].reshape(R), outs[5].reshape(R), outs[3].reshape(D), outs[2].reshape(2))
    if DEBUG:
        return result, {k: res["dbg_" + k] for k in DEBUG}
    return result


def solution(mesh):
    rows, wide = P(("wide", "narrow")), P("wide")
    return jax.shard_map(
        functools.partial(body, mesh),
        mesh=mesh,
        in_specs=(rows,) + (wide,) * 8 + (P(),) + (rows,) * 4,
        out_specs=(rows, rows) + (wide,) * 8 + (P(), P()),
        check_vma=False,
    )
```

```python
import functools
import math

import jax
import jax.numpy as jnp
from jax import lax
from jax.experimental import pallas as pl
from jax.experimental.pallas import tpu as pltpu
from jax.sharding import PartitionSpec as P

HEADS = 16
HEAD_DIM = 64
EPS = 1e-06
LANES = 128
MESH = pl.DeviceIdType.MESH
f32 = jnp.float32
bf16 = jnp.bfloat16
MIB = 2**20
CHUNK = 512
DEBUG = ()


def dot(a, b, ca, cb):
    return lax.dot_general(a, b, (((ca,), (cb,)), ((), ())), preferred_element_type=f32)


def aligned(start, size):
    return pl.ds(pl.multiple_of(start, size), size)


def loop(count, step):
    def run(i, carry):
        step(i)
        return carry

    lax.fori_loop(0, count, run, 0)


class Column:
    def __init__(self, ref, lane):
        self.ref, self.lane = ref, slice(lane, lane + 1)

    def __getitem__(self, at):
        return self.ref[at[0], self.lane]

    def __setitem__(self, at, value):
        self.ref[at[0], self.lane] = value


class Links:
    def __init__(self, send, recv):
        self.send, self.recv, self.count, self.open = send, recv, 0, []

    def make(self, src, dst, device):
        i = self.count
        self.count += 1
        return pltpu.make_async_remote_copy(
            src_ref=src,
            dst_ref=dst,
            send_sem=self.send.at[i],
            recv_sem=self.recv.at[i],
            device_id=device,
            device_id_type=MESH,
        )

    def go(self, src, dst, device):
        copy = self.make(src, dst, device)
        copy.start()
        self.open.append(copy)
        return copy

    def sent(self, copy):
        copy.wait_send()
        self.open = [other for other in self.open if other is not copy]

    def sent_all(self, copies):
        for copy in copies:
            self.sent(copy)

    def drain(self):
        for copy in self.open:
            copy.wait_send()
        self.open = []


def copy_count(far):
    near = far - 1
    gather = 4 * (8 * near + 2) + 7 * (2 * near + 1)
    narrow = 2 * 6 + 2 * 4
    reduce_mlp = 2 * (far + near + 3)
    reduce_attn = 4 * (1 + 2 * far + near + 3)
    return gather + narrow + reduce_mlp + reduce_attn + 3 + near


def block_kernel(dims, names, *refs):
    r = dict(zip(names, refs))
    A, R, T, S, CAP, SEQ, D, RB = (
        dims[k] for k in ("A", "R", "T", "S", "CAP", "SEQ", "D", "RB")
    )
    Wd = 2 * A
    half, quart = D // 2, D // 4
    scale = 1.0 / math.sqrt(HEAD_DIM)
    w, n = lax.axis_index("wide"), lax.axis_index("narrow")
    z, x = w // 2, w % 2
    y, c = n // 2, n % 2
    WA, WU, WD, GP = r["WA"], r["WU"], r["WD"], r["GP"]
    NT, MG, ACT, DG = r["NT"], r["MG"], r["ACT"], r["DG"]
    QKVM, N1, RT, OG = r["QKVM"], r["N1"], r["RT"], r["OG"]
    AO, NG, MO = r["AO"], r["NG"], r["MO"]
    PS, PR, YS, YR = r["PS"], r["PR"], r["YS"], r["YR"]
    GATE, R1, R2, LG, SLOT = (Column(r["COLS"], k) for k in range(5))
    SEGR, STAT, SM = r["SEGR"], r["STAT"], r["SM"]
    local, credit = r["local"], r["credit"]
    links = Links(r["send"], r["recv"])

    def dev(zz, xx, yy, cc):
        return (zz * 2 + xx, yy * 2 + cc)

    to_x, to_y, to_c = dev(z, 1 - x, y, c), dev(z, x, 1 - y, c), dev(z, x, y, 1 - c)
    ahead = [(z + dz) % A for dz in range(A)]
    behind = [(z - dz + A) % A for dz in range(A)]

    own = [
        pltpu.make_async_copy(r["w_query"], WA.at[0, w], local.at[0]),
        pltpu.make_async_copy(r["w_key"], WA.at[1, w], local.at[1]),
        pltpu.make_async_copy(r["w_value"], WA.at[2, w], local.at[2]),
        pltpu.make_async_copy(r["w_out"], WA.at[3, w], local.at[3]),
        pltpu.make_async_copy(r["w_down"].at[aligned(n * R, R)], WD.at[z, x], local.at[5]),
        pltpu.make_async_copy(r["gains"], GP.at[w], local.at[6]),
    ]
    if r["w_up"].shape[1] == D:
        own.append(pltpu.make_async_copy(r["w_up"], WU.at[z, x], local.at[4]))
    else:
        own += [
            pltpu.make_async_copy(
                r["w_up"].at[:, aligned((v * 4 + n) * R, R)], WU.at[z, x, :, pl.ds(v * R, R)], local.at[11 + v]
            )
            for v in range(Wd)
        ]
    for copy in own:
        copy.start()
    fetches = {}

    def fetch(i, slot):
        s, k = i // (SEQ // CHUNK), i % (SEQ // CHUNK)
        return [
            pltpu.make_async_copy(
                r[name].at[s, aligned(k * CHUNK, CHUNK)], QKVM.at[2 * slot + a], local.at[7 + 2 * slot + a]
            )
            for a, name in enumerate(("block_input", "cotangent"))
        ]

    for copy in fetch(0, 0):
        copy.start()
    barrier = pltpu.get_barrier_semaphore()
    peers = [dev(ahead[dz], x, y, c) for dz in range(1, A)] + [to_x, to_y, to_c]
    for peer in peers:
        pl.semaphore_signal(barrier, inc=1, device_id=peer, device_id_type=MESH)
    pl.semaphore_wait(barrier, len(peers))
    for copy in own:
        copy.wait()

    class AttnGather:
        def __init__(self, first, count):
            self.first, self.count = first, count

        def piece(self, zz, xx, yy):
            return WA.at[pl.ds(self.first, self.count), zz * 2 + xx, :, aligned(c * half + yy * quart, quart)]

        def wide_piece(self, zz, xx):
            return WA.at[pl.ds(self.first, self.count), zz * 2 + xx, :, aligned(c * half, half)]

        def start(self):
            p, q = self.piece(z, x, y), self.wide_piece(z, x)
            self.far = {dz: links.go(p, p, dev(ahead[dz], x, y, c)) for dz in range(1, A)}
            self.x0 = links.go(q, q, to_x)
            self.x1, self.y1, self.second, self.core = {}, {}, {}, []

        def to_core(self, p):
            self.core.append(links.go(p, p, to_c))

        def relay(self, dz):
            self.far[dz].wait_recv()
            p = self.piece(behind[dz], x, y)
            self.x1[dz] = links.go(p, p, to_x)
            self.y1[dz] = links.go(p, p, to_y)
            self.to_core(p)

        def relay_own(self):
            self.x0.wait_recv()
            self.to_core(self.wide_piece(z, 1 - x))

        def relay_second(self, dz):
            self.x1[dz].wait_recv()
            p = self.piece(behind[dz], 1 - x, y)
            if dz % 2:
                self.second[dz] = links.go(p, p, to_y)
            self.to_core(p)
            self.y1[dz].wait_recv()
            p = self.piece(behind[dz], x, 1 - y)
            if not dz % 2:
                self.second[dz] = links.go(p, p, to_x)
            self.to_core(p)

        def relay_third(self, dz):
            self.second[dz].wait_recv()
            self.to_core(self.piece(behind[dz], 1 - x, 1 - y))

        def finish(self):
            for copy in self.core:
                copy.wait_recv()

    class WideGather:
        def __init__(self, at):
            self.at = at

        def start(self):
            p = self.at(z, x)
            self.far = {dz: links.go(p, p, dev(ahead[dz], x, y, c)) for dz in range(1, A)}
            self.near = []

        def start_near(self):
            p = self.at(z, x)
            self.near.append(links.go(p, p, to_x))

        def relay(self, dz):
            self.far[dz].wait_recv()
            p = self.at(behind[dz], x)
            self.near.append(links.go(p, p, to_x))

        def finish(self):
            for copy in self.near:
                copy.wait_recv()

        def release(self):
            links.sent_all(list(self.far.values()) + self.near)

    gains = WideGather(lambda zz, xx: GP.at[zz * 2 + xx])
    query, key, value, out = (AttnGather(g, 1) for g in range(4))
    attn = (query, key, value, out)
    def in_parts(ref, count):
        size = R // count
        return [
            WideGather(lambda zz, xx, h=h: ref.at[zz, xx, pl.ds(h * size, size)]) for h in range(count)
        ]

    up, down = in_parts(WU, 2), in_parts(WD, 4 if R % 64 == 0 else 2)
    gains.start()
    gains.start_near()
    for group in attn:
        group.start()
    for part in up + down:
        part.start()

    AO[...] = jnp.zeros_like(AO)
    NG[...] = jnp.zeros_like(NG)
    SEGR[...] = jnp.zeros_like(SEGR)
    STAT[...] = jnp.zeros_like(STAT)
    eye = lax.broadcasted_iota(jnp.int32, (CAP, CAP), 0) == lax.broadcasted_iota(jnp.int32, (CAP, CAP), 1)

    def upright(row):
        return jnp.sum(jnp.where(eye, row, 0.0), axis=1, keepdims=True)

    for s in range(S):
        SLOT[pl.ds(s * CAP, CAP), :] = upright(r["slots"][s : s + 1, :].astype(f32))
    router_row = r["gains"][2:3]
    router_tile = jnp.broadcast_to(router_row, (16, D)).astype(bf16)
    steps = S * (SEQ // CHUNK)

    def gather_step(i):
        slot = i % 2
        s, k = i // (SEQ // CHUNK), i % (SEQ // CHUNK)

        @pl.when(i + 1 < steps)
        def _():
            for copy in fetch(i + 1, (i + 1) % 2):
                copy.start()

        for copy in fetch(i, slot):
            copy.wait()
        position = lax.broadcasted_iota(jnp.int32, (CAP, CHUNK), 1) + k * CHUNK
        rows = aligned(s * CAP, CAP)
        onehot = jnp.where(SLOT[rows, :].astype(jnp.int32) == position, 1.0, 0.0).astype(bf16)
        tokens = QKVM[2 * slot]
        AO[rows, :] += dot(onehot, tokens, 1, 0)
        NG[rows, :] += dot(onehot, QKVM[2 * slot + 1], 1, 0)
        at = (pl.ds(s, 1), aligned(k * CHUNK, CHUNK))
        segment, mask = r["segments"][at].astype(f32), r["pad_mask"][at].astype(f32)
        line = lax.broadcasted_iota(jnp.int32, (16, CHUNK), 0)
        marks = jnp.where(line == 0, segment, jnp.where(line == 1, mask, 0.0)).astype(bf16)
        gate_logits = dot(router_tile, tokens, 1, 1)[0:1]
        STAT[0:1] += mask * jax.nn.sigmoid(gate_logits)
        STAT[1:2] += mask
        SEGR[s] += dot(marks, onehot, 1, 1)

    def gather_steps(first, last):
        loop(last - first, lambda i: gather_step(i + first))

    far = range(1, A)
    gather_steps(0, 3)
    for dz in far:
        gains.relay(dz)
    for dz in far:
        query.relay(dz)
    gather_steps(3, 5)
    for dz in far:
        key.relay(dz)
    query.relay_own()
    for dz in far:
        query.relay_second(dz)
    gather_steps(5, 7)
    for dz in far:
        value.relay(dz)
    key.relay_own()
    for dz in far:
        key.relay_second(dz)
    for dz in far:
        query.relay_third(dz)
    gather_steps(7, steps)

    step_rows = T // 4

    def gate_step(i):
        rows = aligned(i * step_rows, step_rows)
        v, g = AO[rows, :], NG[rows, :]
        gate = jax.nn.sigmoid(jnp.sum(v * router_row, axis=-1, keepdims=True))
        GATE[rows, :] = gate
        R1[rows, :] = lax.rsqrt(jnp.mean(v * v, axis=-1, keepdims=True) + EPS)
        RT[rows, :] = v.astype(bf16)
        OG[rows, :] = g.astype(bf16)
        MG[n, rows, :] = (gate * g).astype(bf16)

    for dz in far:
        out.relay(dz)
    value.relay_own()
    for dz in far:
        value.relay_second(dz)
    for dz in far:
        key.relay_third(dz)
    loop(4, gate_step)

    class RowShare:
        def __init__(self, at):
            self.at = at

        def start(self, k):
            p = self.at(n, k)
            self.core = getattr(self, "core", {})
            self.far = getattr(self, "far", {})
            self.core[k] = links.go(p, p, to_c)
            self.far[k] = links.go(p, p, to_y)

        def relay(self, k):
            self.far[k].wait_recv()
            p = self.at((1 - y) * 2 + c, k)
            self.last = getattr(self, "last", {})
            self.last[k] = links.go(p, p, to_c)

        def release(self):
            for copies in (self.core, self.far, self.last):
                links.sent_all(list(copies.values()))

    share_mg = RowShare(lambda b, k: MG.at[b, pl.ds(k * CAP, CAP)])
    share_nt = RowShare(lambda b, k: NT.at[b, pl.ds(k * (A // 2), A // 2)])
    gains.finish()
    r["GN"][...] = jnp.sum(GP[...], axis=0)

    def norm_one_step(i):
        rows = aligned(i * step_rows, step_rows)
        N1[rows, :] = (RT[rows, :].astype(f32) * R1[rows, :] * r["GN"][0:1]).astype(bf16)

    loop(4, norm_one_step)
    ordered = lax.broadcasted_iota(jnp.int32, (CAP, CAP), 0) <= lax.broadcasted_iota(jnp.int32, (CAP, CAP), 1)
    for s in range(S):
        same = upright(SEGR[s][0:1]) == SEGR[s][0:1]
        r["BIAS"][s] = jnp.where(ordered & same, 0.0, -1e30)
    out.relay_own()
    for dz in far:
        out.relay_second(dz)
    for dz in far:
        value.relay_third(dz)
    for dz in far:
        out.relay_third(dz)
    for part in up + down:
        part.start_near()
    for k in range(2):
        share_mg.start(k)

    def project(g):
        def step(j):
            cols = aligned(j * half, half)
            QKVM[g, :, cols] = dot(N1[...], WA[g, :, :, cols].reshape(D, half), 1, 0).astype(bf16)

        loop(2, step)

    for g in range(3):
        attn[g].finish()
        project(g)

    lane = lax.broadcasted_iota(jnp.int32, (1, LANES), 1)
    low_lanes = lane < HEAD_DIM

    def pick(h, v):
        return jnp.where(low_lanes if h == 0 else ~low_lanes, v, jnp.zeros_like(v))

    def softmax_of(s, q, k, h):
        logits = dot(k, pick(h, q), 1, 1) + r["BIAS"][s]
        e = jnp.exp(logits - jnp.max(logits, axis=0, keepdims=True))
        return e * (1.0 / jnp.sum(e, axis=0, keepdims=True))

    group = 4

    def attend(s):
        def step(i):
            for u in range(group):
                rows, cols = pl.ds(s * CAP, CAP), aligned((i * group + u) * LANES, LANES)
                q, k, v = QKVM[0, rows, cols] * bf16(scale), QKVM[1, rows, cols], QKVM[2, rows, cols]
                o = [dot(softmax_of(s, q, k, h).astype(bf16), v, 0, 0) for h in range(2)]
                QKVM[3, rows, cols] = jnp.where(low_lanes, o[0], o[1]).astype(bf16)

        loop(D // LANES // group, step)

    def project_out(s):
        rows = pl.ds(s * CAP, CAP)

        def step(j):
            cols = aligned(j * half, half)
            AO[rows, cols] = dot(QKVM[3, rows, :], WA[3, :, :, cols].reshape(D, half), 1, 0)

        loop(2, step)

    def norm_two(k):
        def step(i):
            rows = aligned(k * CAP + i * (CAP // 2), CAP // 2)
            v = RT[rows, :].astype(f32) + AO[rows, :]
            scale_two = lax.rsqrt(jnp.mean(v * v, axis=-1, keepdims=True) + EPS)
            R2[rows, :] = scale_two
            part = (v * scale_two * r["GN"][1:2]).astype(bf16)
            NT[n, pl.ds(k * (A // 2) + i * (A // 4), A // 4)] = part.reshape(A // 4, 2, RB, D)

        loop(2, step)

    attend(0)
    out.finish()
    project_out(0)
    norm_two(0)
    share_nt.start(0)
    for part in up:
        for dz in far:
            part.relay(dz)
    attend(1)
    project_out(1)
    norm_two(1)
    share_nt.start(1)
    for part in down[: len(down) // 2]:
        for dz in far:
            part.relay(dz)

    tanh_k = math.sqrt(2.0 / math.pi)

    def up_unit(yy, k):
        rows = NT.at[pl.ds(yy * 2, 2), pl.ds(k * (A // 2), A // 2)]
        parts = [pl.ds(cc * (A // 2) + k * (A // 4), A // 4) for cc in range(2)]

        def step(j):
            cols = aligned(j * quart, quart)
            v = dot(rows[...].reshape(T, D), WU[:, :, :, cols].reshape(D, quart), 1, 0)
            vv = v * v
            t = jnp.tanh(v * (tanh_k + (tanh_k * 0.044715) * vv))
            act = 0.5 * v * (1.0 + t)
            slope = (0.5 + 0.5 * t) * (1.0 + v * (1.0 - t) * (tanh_k + (tanh_k * 0.134145) * vv))
            for cc in range(2):
                at = slice(cc * CAP, (cc + 1) * CAP)
                ACT[yy, parts[cc], :, :, :, cols] = act[at].astype(bf16).reshape(A // 4, 2, 2, RB, quart)
                DG[yy, parts[cc], :, :, :, cols] = slope[at].astype(bf16).reshape(A // 4, 2, 2, RB, quart)

        loop(4, step)

    def act_unit(yy):
        def step(j):
            cols = aligned(j * quart, quart)
            rows = WD[pl.ds(j * (A // 4), A // 4)].reshape(quart, D)
            v = dot(MG[pl.ds(yy * 2, 2)].reshape(2 * T, D), rows, 1, 1)
            slope = DG[yy, :, :, :, :, cols].reshape(2 * T, quart).astype(f32)
            DG[yy, :, :, :, :, cols] = (v * slope).astype(bf16).reshape(A, 2, 2, RB, quart)

        loop(4, step)

    for k in range(2):
        share_mg.relay(k)
        share_nt.core[k].wait_recv()
        share_mg.core[k].wait_recv()
    for part in up:
        part.finish()
    up_unit(y, 0)
    for part in down[len(down) // 2 :]:
        for dz in far:
            part.relay(dz)
    up_unit(y, 1)
    share_nt.relay(0)
    share_nt.last[0].wait_recv()
    up_unit(1 - y, 0)
    for k in range(2):
        share_mg.last[k].wait_recv()
    share_nt.relay(1)
    share_nt.last[1].wait_recv()
    up_unit(1 - y, 1)
    for part in down:
        part.finish()
    act_unit(1 - y)
    act_unit(y)

    class NarrowReduce:
        def __init__(self, lhs, part, send, k, total):
            self.lhs, self.part, self.send, self.k, self.total = lhs, part, send, k, total
            self.core, self.far = [], []

        def compute(self, q):
            yy = y if q else 1 - y
            keep = self.total if q else MO

            def step(j):
                cols = aligned(j * quart, quart)
                v = self.part(self.lhs[yy].reshape(2 * T, D), j, cols)
                PS[q, :, cols] = jnp.where(c == 0, v[T:], v[:T]).astype(bf16)
                keep[:, cols] = jnp.where(c == 0, v[:T], v[T:])

            loop(4, step)
            self.core.append(links.go(PS.at[q], PR.at[q], to_c))

        def send_far(self):
            self.core[0].wait_recv()
            for k in range(2):
                rows = pl.ds(k * CAP, CAP)
                self.send[rows, :] = (MO[rows, :] + PR[0, rows, :].astype(f32)).astype(bf16)
                self.far.append(links.go(self.send.at[rows], YR.at[self.k, rows], to_y))

        def keep_own(self):
            self.core[1].wait_recv()
            for k in range(2):
                rows = pl.ds(k * CAP, CAP)
                self.total[rows, :] = self.total[rows, :] + PR[1, rows, :].astype(f32)

    def norm_two_part(rows, j, cols):
        return dot(rows, WU[pl.ds(j * (A // 4), A // 4)].reshape(quart, D), 1, 1)

    def mlp_part(rows, j, cols):
        return dot(rows, WD[:, :, :, cols].reshape(D, quart), 1, 0)

    reduce_nt = NarrowReduce(DG, norm_two_part, YS, 0, NG)
    reduce_nt.compute(0)
    reduce_nt.compute(1)
    reduce_nt.send_far()
    reduce_nt.keep_own()
    pl.semaphore_signal(credit.at[0], inc=1, device_id=to_c, device_id_type=MESH)

    class WideReduce:
        def __init__(self, grad, k):
            self.grad, self.k = grad, k

        def landing(self, dz):
            return PR.at[0, pl.ds(dz * R, R)] if self.k else r["GXR"].at[dz]

        def compute(self, lhs, rhs):
            def step(i):
                cols = aligned(i * quart, quart)
                v = dot(lhs(cols), rhs(), 0, 0)
                self.grad[pl.ds(i * (A // 4), A // 4)] = v.astype(bf16).reshape(A // 4, 2, R, D)

            loop(4, step)

        def start(self):
            self.x, self.far = {}, {}
            for dz in list(range(1, A)) + [0]:
                self.x[dz] = links.go(self.grad.at[ahead[dz], 1 - x], self.landing(dz), to_x)

        def middle(self, *dzs):
            for dz in dzs:
                self.x[dz].wait_recv()
                p = self.grad.at[ahead[dz], x]
                p[...] = (p[...].astype(f32) + self.landing(dz)[...].astype(f32)).astype(bf16)
                if dz:
                    self.far[dz] = links.go(p, r["GZR"].at[self.k, dz - 1], dev(ahead[dz], x, y, c))

        def last(self):
            total = self.grad[z, x].astype(f32)
            for dz in range(1, A):
                self.far[dz].wait_recv()
                total = total + r["GZR"][self.k, dz - 1].astype(f32)
            r["FIN"][self.k, n] = total.astype(bf16)
            p = r["FIN"].at[self.k, n]
            self.core = [links.go(p, p, to_c)]
            self.yy = links.go(p, p, to_y)

        def finish(self):
            self.yy.wait_recv()
            p = r["FIN"].at[self.k, (1 - y) * 2 + c]
            self.core.append(links.go(p, p, to_c))
            for copy in self.core:
                copy.wait_recv()

    reduce_up, reduce_down = WideReduce(WU, 0), WideReduce(WD, 1)
    for part in up:
        part.release()
    reduce_up.compute(lambda cols: NT[..., cols].reshape(4 * T, quart), lambda: DG[...].reshape(4 * T, D))
    reduce_up.start()
    share_nt.release()
    pl.semaphore_signal(credit.at[1], inc=1, device_id=to_c, device_id_type=MESH)

    reduce_mo = NarrowReduce(ACT, mlp_part, r["YS2"], 1, MO)
    pl.semaphore_wait(credit.at[0], 1)
    links.sent_all(reduce_nt.core)
    reduce_mo.compute(0)
    reduce_up.middle(1)
    reduce_mo.send_far()
    reduce_mo.compute(1)
    reduce_mo.keep_own()
    pl.semaphore_signal(credit.at[2], inc=1, device_id=to_x, device_id_type=MESH)
    for part in down:
        part.release()
    reduce_down.compute(lambda cols: ACT[..., cols].reshape(4 * T, quart), lambda: MG[...].reshape(4 * T, D))
    pl.semaphore_wait(credit.at[2], 1)
    reduce_down.start()
    reduce_up.middle(2)
    links.sent_all(reduce_mo.core)
    share_mg.release()
    SM[...] = jnp.zeros_like(SM)

    def norm_two_back(s):
        def step(i):
            rows = aligned(s * CAP + i * step_rows, step_rows)
            dy = NG[rows, :] + YR[0, rows, :].astype(f32)
            v = RT[rows, :].astype(f32) + AO[rows, :]
            s2 = R2[rows, :]
            dyg = dy * r["GN"][1:2]
            mean = jnp.mean(dyg * v, axis=-1, keepdims=True)
            grad = s2 * dyg - v * (s2 * s2 * s2 * mean)
            SM[1:2] += jnp.sum(dy * (v * s2), axis=0, keepdims=True)
            NG[rows, :] = grad
            PS[0, rows, :] = (GATE[rows, :] * OG[rows, :].astype(f32) + grad).astype(bf16)

        loop(2, step)

    def mixed_back(s):
        rows = pl.ds(s * CAP, CAP)

        def step(j):
            weight = WA[3, pl.ds(j * (Wd // 2), Wd // 2)].reshape(half, D)
            MG[3, rows, aligned(j * half, half)] = dot(PS[0, rows, :], weight, 1, 1).astype(bf16)

        loop(2, step)

    def attend_back(s):
        def step(i):
            for u in range(group):
                rows, cols = pl.ds(s * CAP, CAP), aligned((i * group + u) * LANES, LANES)
                q, k, v = QKVM[0, rows, cols] * bf16(scale), QKVM[1, rows, cols], QKVM[2, rows, cols]
                dm = MG[3, rows, cols]
                k_t = k.T
                dq, dk, dv = [], [], []
                for h in range(2):
                    p = softmax_of(s, q, k, h)
                    dp = dot(v, pick(h, dm), 1, 1)
                    dl = (p * (dp - jnp.sum(p * dp, axis=0, keepdims=True))).astype(bf16)
                    dq.append(dot(k_t[h * HEAD_DIM : (h + 1) * HEAD_DIM], dl, 1, 0))
                    dk.append(dot(dl, q, 1, 0))
                    dv.append(dot(p.astype(bf16), dm, 1, 0))
                MG[0, rows, cols] = (jnp.concatenate(dq, axis=0) * scale).astype(bf16).T
                MG[1, rows, cols] = jnp.where(low_lanes, dk[0], dk[1]).astype(bf16)
                MG[2, rows, cols] = jnp.where(low_lanes, dv[0], dv[1]).astype(bf16)

        loop(D // LANES // group, step)

    x_first = A // 2

    class AttnReduce:
        def __init__(self, buf, at, k):
            self.buf, self.at, self.k = buf, at, k

        def compute(self, lhs, rhs):
            def step(i):
                cols = aligned(i * quart, quart)
                v = dot(lhs(cols), rhs(), 0, 0)
                self.buf[self.at, pl.ds(i * (A // 4), A // 4)] = v.astype(bf16).reshape(A // 4, 2, 2, RB, D)

            loop(4, step)

        def landing(self, d):
            return PR.at[1, pl.ds((self.k * (A // 2) + d) * RB, RB)]

        def start(self):
            self.core = [links.go(self.buf.at[self.at, :, :, 1 - c], NT.at[self.k], to_c)]

        def part(self, zz, xx, cols=None):
            if cols is None:
                return self.buf.at[self.at, zz, xx, c]
            return self.buf.at[self.at, zz, xx, c, :, aligned(cols * half, half)]

        def first(self):
            self.core[0].wait_recv()

            def step(i):
                p = self.buf.at[self.at, i // 2, i % 2, c]
                p[...] = (p[...].astype(f32) + NT[self.k, i // 2, i % 2].astype(f32)).astype(bf16)

            loop(2 * A, step)
            self.one, self.two, self.far = {}, {}, {}
            for dz in range(A):
                d = (dz + 1) % A
                zz = ahead[d]
                if d < x_first:
                    self.one[d] = links.go(self.part(zz, 1 - x), self.landing(d), to_x)
                else:
                    e = d - x_first
                    cols = aligned((1 - y) * half, half)
                    self.one[d] = links.go(self.buf.at[self.at, zz, :, c, :, cols], r["YRB"].at[self.k, e], to_y)

        def add(self, p, q):
            p[...] = (p[...].astype(f32) + q[...].astype(f32)).astype(bf16)

        def second(self):
            for dz in range(A):
                d = (dz + 1) % A
                zz = ahead[d]
                self.one[d].wait_recv()
                if d < x_first:
                    self.add(self.part(zz, x), self.landing(d))
                    self.two[d] = links.go(self.part(zz, x, 1 - y), r["YRA"].at[self.k, d], to_y)
                else:
                    e = d - x_first
                    p = self.buf.at[self.at, zz, :, c, :, aligned(y * half, half)]
                    self.add(p, r["YRB"].at[self.k, e])
                    self.two[d] = links.go(self.part(zz, 1 - x, y), r["XRB"].at[self.k, e], to_x)

        def third(self):
            for dz in range(A):
                d = (dz + 1) % A
                zz = ahead[d]
                self.two[d].wait_recv()
                p = self.part(zz, x, y)
                self.add(p, r["YRA"].at[self.k, d] if d < x_first else r["XRB"].at[self.k, d - x_first])
                if d:
                    self.far[d] = links.go(p, r["ZR"].at[self.k, d - 1], dev(zz, x, y, c))

        def fin(self, yy):
            return r["FINA"].at[self.k, c, :, aligned(yy * half, half)]

        def last(self):
            total = self.part(z, x, y)[...].astype(f32)
            for d in range(1, A):
                self.far[d].wait_recv()
                total = total + r["ZR"][self.k, d - 1].astype(f32)
            p = self.fin(y)
            p[...] = total.astype(bf16)
            self.core.append(links.go(p, p, to_c))
            self.yy = links.go(p, p, to_y)

        def finish(self):
            self.yy.wait_recv()
            p = self.fin(1 - y)
            self.core.append(links.go(p, p, to_c))
            for copy in self.core[1:]:
                copy.wait_recv()

    reduce_o = AttnReduce(ACT, 0, 3)
    reduce_v = AttnReduce(ACT, 1, 2)
    reduce_k = AttnReduce(DG, 0, 1)
    reduce_q = AttnReduce(DG, 1, 0)
    reduce_nt.far[0].wait_recv()
    norm_two_back(0)
    mixed_back(0)
    attend_back(0)
    reduce_up.middle(3, 0) if A == 4 else reduce_up.middle(*range(3, A), 0)
    reduce_nt.far[1].wait_recv()
    norm_two_back(1)
    mixed_back(1)
    reduce_o.compute(lambda cols: QKVM[3, :, cols], lambda: PS[0])
    pl.semaphore_wait(credit.at[1], 1)
    reduce_o.start()
    attend_back(1)
    reduce_o.first()
    reduce_down.middle(1, 2)
    for k, red in ((2, reduce_v), (1, reduce_k), (0, reduce_q)):
        red.compute(lambda cols: N1[:, cols], lambda k=k: MG[k])
        red.start()
    reduce_v.first()
    reduce_up.last()
    reduce_k.first()
    reduce_down.middle(*range(3, A), 0)
    reduce_q.first()

    def output_step(i):
        rows = aligned(i * step_rows, step_rows)
        v = RT[rows, :].astype(f32)
        g = OG[rows, :].astype(f32)
        gate = GATE[rows, :]
        branch = AO[rows, :] + MO[rows, :] + YR[1, rows, :].astype(f32)
        lg = jnp.sum(g * branch, axis=-1, keepdims=True) * gate * (1.0 - gate)
        LG[rows, :] = lg
        SM[2:3] += jnp.sum(lg * v, axis=0, keepdims=True)
        QKVM[3, rows, :] = (v + gate * branch).astype(bf16)

    for copy in reduce_mo.far:
        copy.wait_recv()
    loop(4, output_step)
    new_copy = pltpu.make_async_copy(QKVM.at[3], r["new_rows"], local.at[0])
    new_copy.start()
    reduce_o.second()

    def norm_one_grad(j):
        rows = pl.ds(j * (Wd // 4), Wd // 4)
        v = dot(MG[0], WA[0, rows].reshape(quart, D), 1, 1)
        v = v + dot(MG[1], WA[1, rows].reshape(quart, D), 1, 1)
        v = v + dot(MG[2], WA[2, rows].reshape(quart, D), 1, 1)
        MO[:, aligned(j * quart, quart)] = v

    loop(4, norm_one_grad)
    reduce_up.finish()
    reduce_v.second()
    reduce_o.third()

    def norm_one_back(i):
        rows = aligned(i * step_rows, step_rows)
        dy = MO[rows, :]
        v = RT[rows, :].astype(f32)
        s1 = R1[rows, :]
        dyg = dy * r["GN"][0:1]
        mean = jnp.mean(dyg * v, axis=-1, keepdims=True)
        SM[0:1] += jnp.sum(dy * (v * s1), axis=0, keepdims=True)
        grad = s1 * dyg - v * (s1 * s1 * s1 * mean)
        grad = OG[rows, :].astype(f32) + NG[rows, :] + grad + LG[rows, :] * router_row
        QKVM[0, rows, :] = grad.astype(bf16)

    loop(4, norm_one_back)
    grad_copy = pltpu.make_async_copy(QKVM.at[0], r["row_grads"], local.at[1])
    grad_copy.start()

    total = lambda v: jnp.sum(jnp.sum(v, axis=1, keepdims=True), axis=0, keepdims=True)
    chosen = total(jnp.sum(SEGR[...], axis=0)[1:2])
    lanes = lax.broadcasted_iota(jnp.int32, (1, D), 1)
    SM[3:4] = (
        jnp.where(lanes == 0, chosen, 0.0)
        + jnp.where(lanes == 1, total(STAT[1:2]), 0.0)
        + jnp.where(lanes == 2, total(STAT[0:1]), 0.0)
    )
    SMS, SMR, SMZ = r["SMS"], r["SMR"], r["SMZ"]
    sums = [links.go(SM, SMR.at[0], to_c)]
    reduce_k.second()
    reduce_v.third()
    reduce_down.last()
    sums[0].wait_recv()
    SMS[0] = SM[...] + SMR[0]
    sums.append(links.go(SMS.at[0], SMR.at[1], to_x))
    reduce_q.second()
    reduce_k.third()
    reduce_o.last()
    sums[1].wait_recv()
    SMS[1] = SMS[0] + SMR[1]
    sums.append(links.go(SMS.at[1], SMR.at[2], to_y))
    reduce_v.last()
    reduce_down.finish()
    reduce_q.third()
    sums[2].wait_recv()
    SMZ[z] = SMS[1] + SMR[2]
    sums = [links.go(SMZ.at[z], SMZ.at[z], dev(ahead[dz], x, y, c)) for dz in range(1, A)]
    reduce_k.last()
    reduce_o.finish()
    reduce_v.finish()
    reduce_q.last()
    for copy in sums:
        copy.wait_recv()
    r["small"][...] = jnp.sum(SMZ[...], axis=0)
    reduce_k.finish()
    reduce_q.finish()
    outs = [
        pltpu.make_async_copy(r["FIN"], r["mlp_grads"], local.at[2]),
        pltpu.make_async_copy(r["FINA"], r["attn_grads"], local.at[3]),
    ]
    for copy in outs:
        copy.start()
    links.drain()
    for copy in outs + [new_copy, grad_copy]:
        copy.wait()
    for k, name in enumerate(DEBUG):
        copy = pltpu.make_async_copy(r[name], r["dbg_" + name], local.at[4])
        copy.start()
        copy.wait()


def finish_kernel(dims, slots, rows, row_grads, attn_grads, mlp_grads, small, base, base_grad,
                  out, out_grad, stats, router, gain_one, gain_two, attn_out, up_out, down_out,
                  attn_stage, up_stage, down_stage, sems):
    S, per, R, Wd, part = dims
    i = pl.program_id(0)
    s, k = i // per, i % per
    size, cap = base.shape[1], slots.shape[1]
    position = lax.broadcasted_iota(jnp.int32, (size, cap), 0) + k * size
    onehot = jnp.where(slots[pl.ds(s, 1), :] == position, 1.0, 0.0)
    hit = jnp.max(onehot, axis=-1, keepdims=True) > 0.5
    onehot = onehot.astype(bf16)
    own = aligned(s * cap, cap)
    for new, old, target in ((rows, base, out), (row_grads, base_grad, out_grad)):
        picked = dot(onehot, new[own, :], 1, 0).astype(bf16)
        target[0] = jnp.where(hit, picked, old[0])

    attn_copies = [
        pltpu.make_async_copy(attn_stage.at[g], attn_out[g], sems.at[g]) for g in range(4)
    ]
    down_copies = [
        pltpu.make_async_copy(down_stage.at[q], down_out.at[pl.ds(q * R, R)], sems.at[4 + q]) for q in range(4)
    ]
    up_copy = pltpu.make_async_copy(up_stage, up_out, sems.at[8])

    @pl.when(i == 0)
    def _():
        for g in range(4):
            attn_stage[g] = attn_grads[g].astype(f32)
            attn_copies[g].start()
        w = lax.axis_index("wide")
        gains = pltpu.roll(small[...], (small.shape[1] - w * R) % small.shape[1], 1)
        gain_one[...] = gains[0:1, :R]
        gain_two[...] = gains[1:2, :R]
        router[...] = small[2:3]
        lane = lax.broadcasted_iota(jnp.int32, (1, small.shape[1]), 1)
        counts = small[3:4]
        valid = jnp.sum(jnp.where(lane == 1, counts, 0.0), axis=1, keepdims=True)
        shifted = jnp.where(lane == 1, pltpu.roll(counts, small.shape[1] - 1, 1), counts)
        stats[...] = (shifted / valid)[:, : stats.shape[1]]

    @pl.when(i == 1)
    def _():
        for q in range(4):
            down_stage[q] = mlp_grads[1, q].astype(f32)
            down_copies[q].start()

    @pl.when(i == 2)
    def _():
        for q in range(4):
            for v in range(Wd):
                at = (v * 4 + q) * part
                up_stage[:, at : at + part] = mlp_grads[0, q, :, v * part : (v + 1) * part].astype(f32)
        up_copy.start()

    @pl.when(i == S * per - 1)
    def _():
        for copy in attn_copies + down_copies + [up_copy]:
            copy.wait()


def finish(mesh, res, slots, block_input, cotangent, R, FF):
    S, SEQ, D = block_input.shape
    Wd = mesh.shape["wide"]
    size = 1024
    per, part = SEQ // size, FF // (4 * Wd)

    def kernel(slots, rows, row_grads, attn, mlp, small, base, base_grad, out, out_grad, stats, router,
               gain_one, gain_two, q, k, v, o, up, down, *scratch):
        finish_kernel((S, per, R, Wd, part), slots, rows, row_grads, attn, mlp, small, base, base_grad,
                      out, out_grad, stats, router, gain_one, gain_two, (q, k, v, o), up, down, *scratch)

    vmem, hbm = pl.BlockSpec(memory_space=pltpu.VMEM), pl.BlockSpec(memory_space=pl.ANY)
    tile = pl.BlockSpec((1, size, D), lambda i: (i // per, i % per, 0))
    shape = jax.ShapeDtypeStruct
    return pl.pallas_call(
        kernel,
        grid=(S * per,),
        out_shape=[shape(block_input.shape, bf16)] * 2
        + [shape((1, 2), f32), shape((1, D), f32), shape((1, R), f32), shape((1, R), f32)]
        + [shape((R, D), f32)] * 4
        + [shape((R, FF), f32), shape((4 * R, D), f32)],
        in_specs=[vmem] * 6 + [tile] * 2,
        out_specs=[tile] * 2 + [vmem] * 4 + [hbm] * 6,
        scratch_shapes=[
            pltpu.VMEM((4, R, D), f32),
            pltpu.VMEM((R, FF), f32),
            pltpu.VMEM((4, R, D), f32),
            pltpu.SemaphoreType.DMA((9,)),
        ],
        compiler_params=pltpu.CompilerParams(vmem_limit_bytes=60 * MIB),
        name="finish_rows",
    )(slots, res["new_rows"], res["row_grads"], res["attn_grads"].reshape(4, R, D), res["mlp_grads"],
      res["small"], block_input, cotangent)


def run_block(mesh, inputs, S, SEQ, CAP, D, R):
    Wd = mesh.shape["wide"]
    A, RB, T = Wd // 2, R // 2, S * CAP
    dims = dict(A=A, R=R, T=T, S=S, CAP=CAP, SEQ=SEQ, D=D, RB=RB)
    out_shapes = {
        "new_rows": ((T, D), bf16),
        "row_grads": ((T, D), bf16),
        "mlp_grads": ((2, 4, R, D), bf16),
        "attn_grads": ((4, 2, RB, D), bf16),
        "small": ((8, D), f32),
    }
    scratch = {
        "WA": ((4, Wd, R, D), bf16),
        "WU": ((A, 2, R, D), bf16),
        "WD": ((A, 2, R, D), bf16),
        "GP": ((Wd, 8, D), f32),
        "GN": ((8, D), f32),
        "NT": ((4, A, 2, RB, D), bf16),
        "MG": ((4, T, D), bf16),
        "ACT": ((2, A, 2, 2, RB, D), bf16),
        "DG": ((2, A, 2, 2, RB, D), bf16),
        "QKVM": ((4, T, D), bf16),
        "N1": ((T, D), bf16),
        "RT": ((T, D), bf16),
        "OG": ((T, D), bf16),
        "AO": ((T, D), f32),
        "NG": ((T, D), f32),
        "MO": ((T, D), f32),
        "PS": ((2, T, D), bf16),
        "PR": ((2, T, D), bf16),
        "YS": ((T, D), bf16),
        "YS2": ((T, D), bf16),
        "YR": ((2, T, D), bf16),
        "GXR": ((A, R, D), bf16),
        "GZR": ((2, A - 1, R, D), bf16),
        "FIN": ((2, 4, R, D), bf16),
        "YRA": ((4, A // 2, RB, D // 2), bf16),
        "YRB": ((4, A // 2, 2, RB, D // 2), bf16),
        "XRB": ((4, A // 2, RB, D // 2), bf16),
        "ZR": ((4, A - 1, RB, D // 2), bf16),
        "FINA": ((4, 2, RB, D), bf16),
        "COLS": ((T, LANES), f32),
        "BIAS": ((S, CAP, CAP), f32),
        "SEGR": ((S, 16, CAP), f32),
        "STAT": ((8, CHUNK), f32),
        "SM": ((8, D), f32),
        "SMS": ((2, 8, D), f32),
        "SMR": ((3, 8, D), f32),
        "SMZ": ((A, 8, D), f32),
    }
    for name in DEBUG:
        out_shapes["dbg_" + name] = scratch[name]
    count = copy_count(A)
    semaphores = {
        "send": pltpu.SemaphoreType.DMA((count,)),
        "recv": pltpu.SemaphoreType.DMA((count,)),
        "local": pltpu.SemaphoreType.DMA((11 + Wd,)),
        "credit": pltpu.SemaphoreType.REGULAR((3,)),
    }
    in_vmem = ("gains", "slots", "segments", "pad_mask")
    hbm, vmem = pl.BlockSpec(memory_space=pl.ANY), pl.BlockSpec(memory_space=pltpu.VMEM)
    names = list(inputs) + list(out_shapes) + list(scratch) + list(semaphores)
    results = pl.pallas_call(
        functools.partial(block_kernel, dims, names),
        out_shape=[jax.ShapeDtypeStruct(*v) for v in out_shapes.values()],
        in_specs=[vmem if k in in_vmem else hbm for k in inputs],
        out_specs=[vmem if k == "small" else hbm for k in out_shapes],
        scratch_shapes=[pltpu.VMEM(*v) for v in scratch.values()] + list(semaphores.values()),
        compiler_params=pltpu.CompilerParams(
            collective_id=0, has_side_effects=True, vmem_limit_bytes=64 * MIB - 65536
        ),
        name="routed_block",
    )(*inputs.values())
    return dict(zip(out_shapes, results))


def body(mesh, block_input, query_weight, key_weight, value_weight, out_weight, up_weight, down_weight,
         attn_gain, mlp_gain, router_weight, slots, segments, pad_mask, cotangent):
    S, SEQ, D = block_input.shape
    CAP = slots.shape[1]
    R, FF = up_weight.shape
    Wd = mesh.shape["wide"]
    w, n = lax.axis_index("wide"), lax.axis_index("narrow")
    part = FF // (4 * Wd)
    assert FF == 4 * D and S == 2 and 4 * CAP == D and part == R and mesh.shape["narrow"] == 4
    if part % LANES:
        up_weight = lax.dynamic_index_in_dim(up_weight.reshape(R, Wd, 4, part), n, axis=2, keepdims=False)
        up_weight = up_weight.reshape(R, D)
    shard = jnp.stack([attn_gain, mlp_gain]).astype(f32)
    line = lax.broadcasted_iota(jnp.int32, (8, D), 0)
    gains = jnp.where(line == 2, router_weight.astype(f32)[None], 0.0)
    gains = lax.dynamic_update_slice(gains, shard, (0, w * R))
    inputs = {
        "block_input": block_input,
        "cotangent": cotangent,
        "w_query": query_weight,
        "w_key": key_weight,
        "w_value": value_weight,
        "w_out": out_weight,
        "w_up": up_weight,
        "w_down": down_weight,
        "gains": gains,
        "slots": slots,
        "segments": segments,
        "pad_mask": pad_mask,
    }
    res = run_block(mesh, inputs, S, SEQ, CAP, D, R)
    outs = finish(mesh, res, slots, block_input, cotangent, R, FF)
    result = (outs[0], outs[1], *outs[6:], outs[4].reshape(R), outs[5].reshape(R), outs[3].reshape(D), outs[2].reshape(2))
    if DEBUG:
        return result, {k: res["dbg_" + k] for k in DEBUG}
    return result


def solution(mesh):
    rows, wide = P(("wide", "narrow")), P("wide")
    return jax.shard_map(
        functools.partial(body, mesh),
        mesh=mesh,
        in_specs=(rows,) + (wide,) * 8 + (P(),) + (rows,) * 4,
        out_specs=(rows, rows) + (wide,) * 8 + (P(), P()),
        check_vma=False,
    )
```

```python
import functools
import math

import jax
import jax.numpy as jnp
from jax import lax
from jax.experimental import pallas as pl
from jax.experimental.pallas import tpu as pltpu
from jax.sharding import PartitionSpec as P

HEADS = 16
HEAD_DIM = 64
EPS = 1e-06
LANES = 128
MESH = pl.DeviceIdType.MESH
f32 = jnp.float32
bf16 = jnp.bfloat16
MIB = 2**20
CHUNK = 512
DEBUG = ()


def dot(a, b, ca, cb):
    return lax.dot_general(a, b, (((ca,), (cb,)), ((), ())), preferred_element_type=f32)


def aligned(start, size):
    return pl.ds(pl.multiple_of(start, size), size)


def loop(count, step):
    def run(i, carry):
        step(i)
        return carry

    lax.fori_loop(0, count, run, 0)


class Column:
    def __init__(self, ref, lane):
        self.ref, self.lane = ref, slice(lane, lane + 1)

    def __getitem__(self, at):
        return self.ref[at[0], self.lane]

    def __setitem__(self, at, value):
        self.ref[at[0], self.lane] = value


class Links:
    def __init__(self, send, recv):
        self.send, self.recv, self.count, self.open = send, recv, 0, []

    def make(self, src, dst, device):
        i = self.count
        self.count += 1
        return pltpu.make_async_remote_copy(
            src_ref=src,
            dst_ref=dst,
            send_sem=self.send.at[i],
            recv_sem=self.recv.at[i],
            device_id=device,
            device_id_type=MESH,
        )

    def go(self, src, dst, device):
        copy = self.make(src, dst, device)
        copy.start()
        self.open.append(copy)
        return copy

    def sent(self, copy):
        copy.wait_send()
        self.open = [other for other in self.open if other is not copy]

    def sent_all(self, copies):
        for copy in copies:
            self.sent(copy)

    def drain(self):
        for copy in self.open:
            copy.wait_send()
        self.open = []


def copy_count(far):
    near = far - 1
    gather = 4 * (8 * near + 2) + 5 * (2 * near + 1)
    narrow = 2 * 6 + 2 * 4
    reduce_mlp = 2 * (far + near + 3)
    reduce_attn = 4 * (1 + 2 * far + near + 3)
    return gather + narrow + reduce_mlp + reduce_attn + 3 + near


def block_kernel(dims, names, *refs):
    r = dict(zip(names, refs))
    A, R, T, S, CAP, SEQ, D, RB = (
        dims[k] for k in ("A", "R", "T", "S", "CAP", "SEQ", "D", "RB")
    )
    Wd = 2 * A
    half, quart = D // 2, D // 4
    scale = 1.0 / math.sqrt(HEAD_DIM)
    w, n = lax.axis_index("wide"), lax.axis_index("narrow")
    z, x = w // 2, w % 2
    y, c = n // 2, n % 2
    WA, WU, WD, GP = r["WA"], r["WU"], r["WD"], r["GP"]
    NT, MG, ACT, DG = r["NT"], r["MG"], r["ACT"], r["DG"]
    QKVM, N1, RT, OG = r["QKVM"], r["N1"], r["RT"], r["OG"]
    AO, NG, MO = r["AO"], r["NG"], r["MO"]
    PS, PR, YS, YR = r["PS"], r["PR"], r["YS"], r["YR"]
    GATE, R1, R2, LG, SLOT = (Column(r["COLS"], k) for k in range(5))
    SEGR, STAT, SM = r["SEGR"], r["STAT"], r["SM"]
    local, credit = r["local"], r["credit"]
    links = Links(r["send"], r["recv"])

    def dev(zz, xx, yy, cc):
        return (zz * 2 + xx, yy * 2 + cc)

    to_x, to_y, to_c = dev(z, 1 - x, y, c), dev(z, x, 1 - y, c), dev(z, x, y, 1 - c)
    ahead = [(z + dz) % A for dz in range(A)]
    behind = [(z - dz + A) % A for dz in range(A)]

    own = [
        pltpu.make_async_copy(r["w_query"], WA.at[0, w], local.at[0]),
        pltpu.make_async_copy(r["w_key"], WA.at[1, w], local.at[1]),
        pltpu.make_async_copy(r["w_value"], WA.at[2, w], local.at[2]),
        pltpu.make_async_copy(r["w_out"], WA.at[3, w], local.at[3]),
        pltpu.make_async_copy(r["w_down"].at[aligned(n * R, R)], WD.at[z, x], local.at[5]),
        pltpu.make_async_copy(r["gains"], GP.at[w], local.at[6]),
    ]
    if r["w_up"].shape[1] == D:
        own.append(pltpu.make_async_copy(r["w_up"], WU.at[z, x], local.at[4]))
    else:
        own += [
            pltpu.make_async_copy(
                r["w_up"].at[:, aligned((v * 4 + n) * R, R)], WU.at[z, x, :, pl.ds(v * R, R)], local.at[11 + v]
            )
            for v in range(Wd)
        ]
    for copy in own:
        copy.start()
    fetches = {}

    def fetch(i, slot):
        s, k = i // (SEQ // CHUNK), i % (SEQ // CHUNK)
        return [
            pltpu.make_async_copy(
                r[name].at[s, aligned(k * CHUNK, CHUNK)], QKVM.at[2 * slot + a], local.at[7 + 2 * slot + a]
            )
            for a, name in enumerate(("block_input", "cotangent"))
        ]

    for copy in fetch(0, 0):
        copy.start()
    barrier = pltpu.get_barrier_semaphore()
    peers = [dev(ahead[dz], x, y, c) for dz in range(1, A)] + [to_x, to_y, to_c]
    for peer in peers:
        pl.semaphore_signal(barrier, inc=1, device_id=peer, device_id_type=MESH)
    pl.semaphore_wait(barrier, len(peers))
    for copy in own:
        copy.wait()

    class AttnGather:
        def __init__(self, first, count):
            self.first, self.count = first, count

        def piece(self, zz, xx, yy):
            return WA.at[pl.ds(self.first, self.count), zz * 2 + xx, :, aligned(c * half + yy * quart, quart)]

        def wide_piece(self, zz, xx):
            return WA.at[pl.ds(self.first, self.count), zz * 2 + xx, :, aligned(c * half, half)]

        def start(self):
            p, q = self.piece(z, x, y), self.wide_piece(z, x)
            self.far = {dz: links.go(p, p, dev(ahead[dz], x, y, c)) for dz in range(1, A)}
            self.x0 = links.go(q, q, to_x)
            self.x1, self.y1, self.second, self.core = {}, {}, {}, []

        def to_core(self, p):
            self.core.append(links.go(p, p, to_c))

        def relay(self, dz):
            self.far[dz].wait_recv()
            p = self.piece(behind[dz], x, y)
            self.x1[dz] = links.go(p, p, to_x)
            self.y1[dz] = links.go(p, p, to_y)
            self.to_core(p)

        def relay_own(self):
            self.x0.wait_recv()
            self.to_core(self.wide_piece(z, 1 - x))

        def relay_second(self, dz):
            self.x1[dz].wait_recv()
            p = self.piece(behind[dz], 1 - x, y)
            if dz % 2:
                self.second[dz] = links.go(p, p, to_y)
            self.to_core(p)
            self.y1[dz].wait_recv()
            p = self.piece(behind[dz], x, 1 - y)
            if not dz % 2:
                self.second[dz] = links.go(p, p, to_x)
            self.to_core(p)

        def relay_third(self, dz):
            self.second[dz].wait_recv()
            self.to_core(self.piece(behind[dz], 1 - x, 1 - y))

        def finish(self):
            for copy in self.core:
                copy.wait_recv()

    class WideGather:
        def __init__(self, at):
            self.at = at

        def start(self):
            p = self.at(z, x)
            self.far = {dz: links.go(p, p, dev(ahead[dz], x, y, c)) for dz in range(1, A)}
            self.near = []

        def start_near(self):
            p = self.at(z, x)
            self.near.append(links.go(p, p, to_x))

        def relay(self, dz):
            self.far[dz].wait_recv()
            p = self.at(behind[dz], x)
            self.near.append(links.go(p, p, to_x))

        def finish(self):
            for copy in self.near:
                copy.wait_recv()

        def release(self):
            links.sent_all(list(self.far.values()) + self.near)

    gains = WideGather(lambda zz, xx: GP.at[zz * 2 + xx])
    query, key, value, out = (AttnGather(g, 1) for g in range(4))
    attn = (query, key, value, out)
    up, down = (
        [WideGather(lambda zz, xx, ref=ref, h=h: ref.at[zz, xx, pl.ds(h * RB, RB)]) for h in range(2)]
        for ref in (WU, WD)
    )
    gains.start()
    gains.start_near()
    for group in attn:
        group.start()
    for part in up + down:
        part.start()

    AO[...] = jnp.zeros_like(AO)
    NG[...] = jnp.zeros_like(NG)
    SEGR[...] = jnp.zeros_like(SEGR)
    STAT[...] = jnp.zeros_like(STAT)
    eye = lax.broadcasted_iota(jnp.int32, (CAP, CAP), 0) == lax.broadcasted_iota(jnp.int32, (CAP, CAP), 1)

    def upright(row):
        return jnp.sum(jnp.where(eye, row, 0.0), axis=1, keepdims=True)

    for s in range(S):
        SLOT[pl.ds(s * CAP, CAP), :] = upright(r["slots"][s : s + 1, :].astype(f32))
    router_row = r["gains"][2:3]
    router_tile = jnp.broadcast_to(router_row, (16, D)).astype(bf16)
    steps = S * (SEQ // CHUNK)

    def gather_step(i):
        slot = i % 2
        s, k = i // (SEQ // CHUNK), i % (SEQ // CHUNK)

        @pl.when(i + 1 < steps)
        def _():
            for copy in fetch(i + 1, (i + 1) % 2):
                copy.start()

        for copy in fetch(i, slot):
            copy.wait()
        position = lax.broadcasted_iota(jnp.int32, (CAP, CHUNK), 1) + k * CHUNK
        rows = aligned(s * CAP, CAP)
        onehot = jnp.where(SLOT[rows, :].astype(jnp.int32) == position, 1.0, 0.0).astype(bf16)
        tokens = QKVM[2 * slot]
        AO[rows, :] += dot(onehot, tokens, 1, 0)
        NG[rows, :] += dot(onehot, QKVM[2 * slot + 1], 1, 0)
        at = (pl.ds(s, 1), aligned(k * CHUNK, CHUNK))
        segment, mask = r["segments"][at].astype(f32), r["pad_mask"][at].astype(f32)
        line = lax.broadcasted_iota(jnp.int32, (16, CHUNK), 0)
        marks = jnp.where(line == 0, segment, jnp.where(line == 1, mask, 0.0)).astype(bf16)
        gate_logits = dot(router_tile, tokens, 1, 1)[0:1]
        STAT[0:1] += mask * jax.nn.sigmoid(gate_logits)
        STAT[1:2] += mask
        SEGR[s] += dot(marks, onehot, 1, 1)

    def gather_steps(first, last):
        loop(last - first, lambda i: gather_step(i + first))

    far = range(1, A)
    gather_steps(0, 3)
    for dz in far:
        gains.relay(dz)
    for dz in far:
        query.relay(dz)
    gather_steps(3, 5)
    for dz in far:
        key.relay(dz)
    query.relay_own()
    for dz in far:
        query.relay_second(dz)
    gather_steps(5, 7)
    for dz in far:
        value.relay(dz)
    key.relay_own()
    for dz in far:
        key.relay_second(dz)
    for dz in far:
        query.relay_third(dz)
    gather_steps(7, steps)

    step_rows = T // 4

    def gate_step(i):
        rows = aligned(i * step_rows, step_rows)
        v, g = AO[rows, :], NG[rows, :]
        gate = jax.nn.sigmoid(jnp.sum(v * router_row, axis=-1, keepdims=True))
        GATE[rows, :] = gate
        R1[rows, :] = lax.rsqrt(jnp.mean(v * v, axis=-1, keepdims=True) + EPS)
        RT[rows, :] = v.astype(bf16)
        OG[rows, :] = g.astype(bf16)
        MG[n, rows, :] = (gate * g).astype(bf16)

    for dz in far:
        out.relay(dz)
    value.relay_own()
    for dz in far:
        value.relay_second(dz)
    for dz in far:
        key.relay_third(dz)
    loop(4, gate_step)

    class RowShare:
        def __init__(self, at):
            self.at = at

        def start(self, k):
            p = self.at(n, k)
            self.core = getattr(self, "core", {})
            self.far = getattr(self, "far", {})
            self.core[k] = links.go(p, p, to_c)
            self.far[k] = links.go(p, p, to_y)

        def relay(self, k):
            self.far[k].wait_recv()
            p = self.at((1 - y) * 2 + c, k)
            self.last = getattr(self, "last", {})
            self.last[k] = links.go(p, p, to_c)

        def release(self):
            for copies in (self.core, self.far, self.last):
                links.sent_all(list(copies.values()))

    share_mg = RowShare(lambda b, k: MG.at[b, pl.ds(k * CAP, CAP)])
    share_nt = RowShare(lambda b, k: NT.at[b, pl.ds(k * (A // 2), A // 2)])
    gains.finish()
    r["GN"][...] = jnp.sum(GP[...], axis=0)

    def norm_one_step(i):
        rows = aligned(i * step_rows, step_rows)
        N1[rows, :] = (RT[rows, :].astype(f32) * R1[rows, :] * r["GN"][0:1]).astype(bf16)

    loop(4, norm_one_step)
    ordered = lax.broadcasted_iota(jnp.int32, (CAP, CAP), 0) <= lax.broadcasted_iota(jnp.int32, (CAP, CAP), 1)
    for s in range(S):
        same = upright(SEGR[s][0:1]) == SEGR[s][0:1]
        r["BIAS"][s] = jnp.where(ordered & same, 0.0, -1e30)
    out.relay_own()
    for dz in far:
        out.relay_second(dz)
    for dz in far:
        value.relay_third(dz)
    for dz in far:
        out.relay_third(dz)
    for part in up + down:
        part.start_near()
    for k in range(2):
        share_mg.start(k)

    def project(g):
        def step(j):
            cols = aligned(j * half, half)
            QKVM[g, :, cols] = dot(N1[...], WA[g, :, :, cols].reshape(D, half), 1, 0).astype(bf16)

        loop(2, step)

    for g in range(3):
        attn[g].finish()
        project(g)

    lane = lax.broadcasted_iota(jnp.int32, (1, LANES), 1)
    low_lanes = lane < HEAD_DIM

    def pick(h, v):
        return jnp.where(low_lanes if h == 0 else ~low_lanes, v, jnp.zeros_like(v))

    def softmax_of(s, q, k, h):
        logits = dot(k, pick(h, q), 1, 1) + r["BIAS"][s]
        e = jnp.exp(logits - jnp.max(logits, axis=0, keepdims=True))
        return e * (1.0 / jnp.sum(e, axis=0, keepdims=True))

    group = 4

    def attend(s):
        def step(i):
            for u in range(group):
                rows, cols = pl.ds(s * CAP, CAP), aligned((i * group + u) * LANES, LANES)
                q, k, v = QKVM[0, rows, cols] * bf16(scale), QKVM[1, rows, cols], QKVM[2, rows, cols]
                o = [dot(softmax_of(s, q, k, h).astype(bf16), v, 0, 0) for h in range(2)]
                QKVM[3, rows, cols] = jnp.where(low_lanes, o[0], o[1]).astype(bf16)

        loop(D // LANES // group, step)

    def project_out(s):
        rows = pl.ds(s * CAP, CAP)

        def step(j):
            cols = aligned(j * half, half)
            AO[rows, cols] = dot(QKVM[3, rows, :], WA[3, :, :, cols].reshape(D, half), 1, 0)

        loop(2, step)

    def norm_two(k):
        def step(i):
            rows = aligned(k * CAP + i * (CAP // 2), CAP // 2)
            v = RT[rows, :].astype(f32) + AO[rows, :]
            scale_two = lax.rsqrt(jnp.mean(v * v, axis=-1, keepdims=True) + EPS)
            R2[rows, :] = scale_two
            part = (v * scale_two * r["GN"][1:2]).astype(bf16)
            NT[n, pl.ds(k * (A // 2) + i * (A // 4), A // 4)] = part.reshape(A // 4, 2, RB, D)

        loop(2, step)

    attend(0)
    out.finish()
    project_out(0)
    norm_two(0)
    share_nt.start(0)
    for part in up:
        for dz in far:
            part.relay(dz)
    attend(1)
    project_out(1)
    norm_two(1)
    share_nt.start(1)
    for dz in far:
        down[0].relay(dz)

    tanh_k = math.sqrt(2.0 / math.pi)

    def up_unit(yy, k):
        rows = NT.at[pl.ds(yy * 2, 2), pl.ds(k * (A // 2), A // 2)]
        parts = [pl.ds(cc * (A // 2) + k * (A // 4), A // 4) for cc in range(2)]

        def step(j):
            cols = aligned(j * quart, quart)
            v = dot(rows[...].reshape(T, D), WU[:, :, :, cols].reshape(D, quart), 1, 0)
            vv = v * v
            t = jnp.tanh(v * (tanh_k + (tanh_k * 0.044715) * vv))
            act = 0.5 * v * (1.0 + t)
            slope = (0.5 + 0.5 * t) * (1.0 + v * (1.0 - t) * (tanh_k + (tanh_k * 0.134145) * vv))
            for cc in range(2):
                at = slice(cc * CAP, (cc + 1) * CAP)
                ACT[yy, parts[cc], :, :, :, cols] = act[at].astype(bf16).reshape(A // 4, 2, 2, RB, quart)
                DG[yy, parts[cc], :, :, :, cols] = slope[at].astype(bf16).reshape(A // 4, 2, 2, RB, quart)

        loop(4, step)

    def act_unit(yy):
        def step(j):
            cols = aligned(j * quart, quart)
            rows = WD[pl.ds(j * (A // 4), A // 4)].reshape(quart, D)
            v = dot(MG[pl.ds(yy * 2, 2)].reshape(2 * T, D), rows, 1, 1)
            slope = DG[yy, :, :, :, :, cols].reshape(2 * T, quart).astype(f32)
            DG[yy, :, :, :, :, cols] = (v * slope).astype(bf16).reshape(A, 2, 2, RB, quart)

        loop(4, step)

    for k in range(2):
        share_mg.relay(k)
        share_nt.core[k].wait_recv()
        share_mg.core[k].wait_recv()
    for part in up:
        part.finish()
    up_unit(y, 0)
    for dz in far:
        down[1].relay(dz)
    up_unit(y, 1)
    share_nt.relay(0)
    share_nt.last[0].wait_recv()
    up_unit(1 - y, 0)
    for k in range(2):
        share_mg.last[k].wait_recv()
    share_nt.relay(1)
    share_nt.last[1].wait_recv()
    up_unit(1 - y, 1)
    for part in down:
        part.finish()
    act_unit(1 - y)
    act_unit(y)

    class NarrowReduce:
        def __init__(self, lhs, part, send, k, total):
            self.lhs, self.part, self.send, self.k, self.total = lhs, part, send, k, total
            self.core, self.far = [], []

        def compute(self, q):
            yy = y if q else 1 - y
            keep = self.total if q else MO

            def step(j):
                cols = aligned(j * quart, quart)
                v = self.part(self.lhs[yy].reshape(2 * T, D), j, cols)
                PS[q, :, cols] = jnp.where(c == 0, v[T:], v[:T]).astype(bf16)
                keep[:, cols] = jnp.where(c == 0, v[:T], v[T:])

            loop(4, step)
            self.core.append(links.go(PS.at[q], PR.at[q], to_c))

        def send_far(self):
            self.core[0].wait_recv()
            for k in range(2):
                rows = pl.ds(k * CAP, CAP)
                self.send[rows, :] = (MO[rows, :] + PR[0, rows, :].astype(f32)).astype(bf16)
                self.far.append(links.go(self.send.at[rows], YR.at[self.k, rows], to_y))

        def keep_own(self):
            self.core[1].wait_recv()
            for k in range(2):
                rows = pl.ds(k * CAP, CAP)
                self.total[rows, :] = self.total[rows, :] + PR[1, rows, :].astype(f32)

    def norm_two_part(rows, j, cols):
        return dot(rows, WU[pl.ds(j * (A // 4), A // 4)].reshape(quart, D), 1, 1)

    def mlp_part(rows, j, cols):
        return dot(rows, WD[:, :, :, cols].reshape(D, quart), 1, 0)

    reduce_nt = NarrowReduce(DG, norm_two_part, YS, 0, NG)
    reduce_nt.compute(0)
    reduce_nt.compute(1)
    reduce_nt.send_far()
    reduce_nt.keep_own()
    pl.semaphore_signal(credit.at[0], inc=1, device_id=to_c, device_id_type=MESH)

    class WideReduce:
        def __init__(self, grad, k):
            self.grad, self.k = grad, k

        def landing(self, dz):
            return PR.at[0, pl.ds(dz * R, R)] if self.k else r["GXR"].at[dz]

        def send(self, dz):
            self.x[dz] = links.go(self.grad.at[ahead[dz], 1 - x], self.landing(dz), to_x)

        def start(self, lhs, rhs):
            self.x, self.far = {}, {}
            order = list(range(1, A)) + [0]

            def step(i):
                cols = aligned(i * quart, quart)
                v = dot(lhs(cols), rhs(), 0, 0)
                self.grad[pl.ds(i * (A // 4), A // 4)] = v.astype(bf16).reshape(A // 4, 2, R, D)

            if A == 4:
                for dz in order:
                    step(ahead[dz])
                    self.send(dz)
            else:
                loop(4, step)
                for dz in order:
                    self.send(dz)

        def middle(self, *dzs):
            for dz in dzs:
                self.x[dz].wait_recv()
                p = self.grad.at[ahead[dz], x]
                p[...] = (p[...].astype(f32) + self.landing(dz)[...].astype(f32)).astype(bf16)
                if dz:
                    self.far[dz] = links.go(p, r["GZR"].at[self.k, dz - 1], dev(ahead[dz], x, y, c))

        def last(self):
            total = self.grad[z, x].astype(f32)
            for dz in range(1, A):
                self.far[dz].wait_recv()
                total = total + r["GZR"][self.k, dz - 1].astype(f32)
            r["FIN"][self.k, n] = total.astype(bf16)
            p = r["FIN"].at[self.k, n]
            self.core = [links.go(p, p, to_c)]
            self.yy = links.go(p, p, to_y)

        def finish(self):
            self.yy.wait_recv()
            p = r["FIN"].at[self.k, (1 - y) * 2 + c]
            self.core.append(links.go(p, p, to_c))
            for copy in self.core:
                copy.wait_recv()

    reduce_up, reduce_down = WideReduce(WU, 0), WideReduce(WD, 1)
    for part in up:
        part.release()
    reduce_up.start(lambda cols: NT[..., cols].reshape(4 * T, quart), lambda: DG[...].reshape(4 * T, D))
    share_nt.release()
    pl.semaphore_signal(credit.at[1], inc=1, device_id=to_c, device_id_type=MESH)

    reduce_mo = NarrowReduce(ACT, mlp_part, r["YS2"], 1, MO)
    pl.semaphore_wait(credit.at[0], 1)
    links.sent_all(reduce_nt.core)
    reduce_mo.compute(0)
    reduce_up.middle(1)
    reduce_mo.send_far()
    reduce_mo.compute(1)
    reduce_mo.keep_own()
    pl.semaphore_signal(credit.at[2], inc=1, device_id=to_x, device_id_type=MESH)
    for part in down:
        part.release()
    pl.semaphore_wait(credit.at[2], 1)
    reduce_down.start(lambda cols: ACT[..., cols].reshape(4 * T, quart), lambda: MG[...].reshape(4 * T, D))
    reduce_up.middle(2)
    links.sent_all(reduce_mo.core)
    share_mg.release()
    SM[...] = jnp.zeros_like(SM)

    def norm_two_back(s):
        def step(i):
            rows = aligned(s * CAP + i * step_rows, step_rows)
            dy = NG[rows, :] + YR[0, rows, :].astype(f32)
            v = RT[rows, :].astype(f32) + AO[rows, :]
            s2 = R2[rows, :]
            dyg = dy * r["GN"][1:2]
            mean = jnp.mean(dyg * v, axis=-1, keepdims=True)
            grad = s2 * dyg - v * (s2 * s2 * s2 * mean)
            SM[1:2] += jnp.sum(dy * (v * s2), axis=0, keepdims=True)
            NG[rows, :] = grad
            PS[0, rows, :] = (GATE[rows, :] * OG[rows, :].astype(f32) + grad).astype(bf16)

        loop(2, step)

    def mixed_back(s):
        rows = pl.ds(s * CAP, CAP)

        def step(j):
            weight = WA[3, pl.ds(j * (Wd // 2), Wd // 2)].reshape(half, D)
            MG[3, rows, aligned(j * half, half)] = dot(PS[0, rows, :], weight, 1, 1).astype(bf16)

        loop(2, step)

    def attend_back(s):
        def step(i):
            for u in range(group):
                rows, cols = pl.ds(s * CAP, CAP), aligned((i * group + u) * LANES, LANES)
                q, k, v = QKVM[0, rows, cols] * bf16(scale), QKVM[1, rows, cols], QKVM[2, rows, cols]
                dm = MG[3, rows, cols]
                k_t = k.T
                dq, dk, dv = [], [], []
                for h in range(2):
                    p = softmax_of(s, q, k, h)
                    dp = dot(v, pick(h, dm), 1, 1)
                    dl = (p * (dp - jnp.sum(p * dp, axis=0, keepdims=True))).astype(bf16)
                    dq.append(dot(k_t[h * HEAD_DIM : (h + 1) * HEAD_DIM], dl, 1, 0))
                    dk.append(dot(dl, q, 1, 0))
                    dv.append(dot(p.astype(bf16), dm, 1, 0))
                MG[0, rows, cols] = (jnp.concatenate(dq, axis=0) * scale).astype(bf16).T
                MG[1, rows, cols] = jnp.where(low_lanes, dk[0], dk[1]).astype(bf16)
                MG[2, rows, cols] = jnp.where(low_lanes, dv[0], dv[1]).astype(bf16)

        loop(D // LANES // group, step)

    x_first = A // 2

    class AttnReduce:
        def __init__(self, buf, at, k):
            self.buf, self.at, self.k = buf, at, k

        def compute(self, lhs, rhs):
            def step(i):
                cols = aligned(i * quart, quart)
                v = dot(lhs(cols), rhs(), 0, 0)
                self.buf[self.at, pl.ds(i * (A // 4), A // 4)] = v.astype(bf16).reshape(A // 4, 2, 2, RB, D)

            loop(4, step)

        def landing(self, d):
            return PR.at[1, pl.ds((self.k * (A // 2) + d) * RB, RB)]

        def start(self):
            self.core = [links.go(self.buf.at[self.at, :, :, 1 - c], NT.at[self.k], to_c)]

        def part(self, zz, xx, cols=None):
            if cols is None:
                return self.buf.at[self.at, zz, xx, c]
            return self.buf.at[self.at, zz, xx, c, :, aligned(cols * half, half)]

        def first(self):
            self.core[0].wait_recv()

            def step(i):
                p = self.buf.at[self.at, i // 2, i % 2, c]
                p[...] = (p[...].astype(f32) + NT[self.k, i // 2, i % 2].astype(f32)).astype(bf16)

            loop(2 * A, step)
            self.one, self.two, self.far = {}, {}, {}
            for dz in range(A):
                d = (dz + 1) % A
                zz = ahead[d]
                if d < x_first:
                    self.one[d] = links.go(self.part(zz, 1 - x), self.landing(d), to_x)
                else:
                    e = d - x_first
                    cols = aligned((1 - y) * half, half)
                    self.one[d] = links.go(self.buf.at[self.at, zz, :, c, :, cols], r["YRB"].at[self.k, e], to_y)

        def add(self, p, q):
            p[...] = (p[...].astype(f32) + q[...].astype(f32)).astype(bf16)

        def second(self):
            for dz in range(A):
                d = (dz + 1) % A
                zz = ahead[d]
                self.one[d].wait_recv()
                if d < x_first:
                    self.add(self.part(zz, x), self.landing(d))
                    self.two[d] = links.go(self.part(zz, x, 1 - y), r["YRA"].at[self.k, d], to_y)
                else:
                    e = d - x_first
                    p = self.buf.at[self.at, zz, :, c, :, aligned(y * half, half)]
                    self.add(p, r["YRB"].at[self.k, e])
                    self.two[d] = links.go(self.part(zz, 1 - x, y), r["XRB"].at[self.k, e], to_x)

        def third(self):
            for dz in range(A):
                d = (dz + 1) % A
                zz = ahead[d]
                self.two[d].wait_recv()
                p = self.part(zz, x, y)
                self.add(p, r["YRA"].at[self.k, d] if d < x_first else r["XRB"].at[self.k, d - x_first])
                if d:
                    self.far[d] = links.go(p, r["ZR"].at[self.k, d - 1], dev(zz, x, y, c))

        def fin(self, yy):
            return r["FINA"].at[self.k, c, :, aligned(yy * half, half)]

        def last(self):
            total = self.part(z, x, y)[...].astype(f32)
            for d in range(1, A):
                self.far[d].wait_recv()
                total = total + r["ZR"][self.k, d - 1].astype(f32)
            p = self.fin(y)
            p[...] = total.astype(bf16)
            self.core.append(links.go(p, p, to_c))
            self.yy = links.go(p, p, to_y)

        def finish(self):
            self.yy.wait_recv()
            p = self.fin(1 - y)
            self.core.append(links.go(p, p, to_c))
            for copy in self.core[1:]:
                copy.wait_recv()

    reduce_o = AttnReduce(ACT, 0, 3)
    reduce_v = AttnReduce(ACT, 1, 2)
    reduce_k = AttnReduce(DG, 0, 1)
    reduce_q = AttnReduce(DG, 1, 0)
    reduce_nt.far[0].wait_recv()
    norm_two_back(0)
    mixed_back(0)
    attend_back(0)
    reduce_up.middle(3, 0) if A == 4 else reduce_up.middle(*range(3, A), 0)
    reduce_nt.far[1].wait_recv()
    norm_two_back(1)
    mixed_back(1)
    reduce_o.compute(lambda cols: QKVM[3, :, cols], lambda: PS[0])
    pl.semaphore_wait(credit.at[1], 1)
    reduce_o.start()
    attend_back(1)
    reduce_o.first()
    reduce_down.middle(1, 2)
    for k, red in ((2, reduce_v), (1, reduce_k), (0, reduce_q)):
        red.compute(lambda cols: N1[:, cols], lambda k=k: MG[k])
        red.start()
    reduce_v.first()
    reduce_up.last()
    reduce_k.first()
    reduce_down.middle(*range(3, A), 0)
    reduce_q.first()

    def output_step(i):
        rows = aligned(i * step_rows, step_rows)
        v = RT[rows, :].astype(f32)
        g = OG[rows, :].astype(f32)
        gate = GATE[rows, :]
        branch = AO[rows, :] + MO[rows, :] + YR[1, rows, :].astype(f32)
        lg = jnp.sum(g * branch, axis=-1, keepdims=True) * gate * (1.0 - gate)
        LG[rows, :] = lg
        SM[2:3] += jnp.sum(lg * v, axis=0, keepdims=True)
        QKVM[3, rows, :] = (v + gate * branch).astype(bf16)

    for copy in reduce_mo.far:
        copy.wait_recv()
    loop(4, output_step)
    new_copy = pltpu.make_async_copy(QKVM.at[3], r["new_rows"], local.at[0])
    new_copy.start()
    reduce_o.second()

    def norm_one_grad(j):
        rows = pl.ds(j * (Wd // 4), Wd // 4)
        v = dot(MG[0], WA[0, rows].reshape(quart, D), 1, 1)
        v = v + dot(MG[1], WA[1, rows].reshape(quart, D), 1, 1)
        v = v + dot(MG[2], WA[2, rows].reshape(quart, D), 1, 1)
        MO[:, aligned(j * quart, quart)] = v

    loop(4, norm_one_grad)
    reduce_up.finish()
    reduce_v.second()
    reduce_o.third()

    def norm_one_back(i):
        rows = aligned(i * step_rows, step_rows)
        dy = MO[rows, :]
        v = RT[rows, :].astype(f32)
        s1 = R1[rows, :]
        dyg = dy * r["GN"][0:1]
        mean = jnp.mean(dyg * v, axis=-1, keepdims=True)
        SM[0:1] += jnp.sum(dy * (v * s1), axis=0, keepdims=True)
        grad = s1 * dyg - v * (s1 * s1 * s1 * mean)
        grad = OG[rows, :].astype(f32) + NG[rows, :] + grad + LG[rows, :] * router_row
        QKVM[0, rows, :] = grad.astype(bf16)

    loop(4, norm_one_back)
    grad_copy = pltpu.make_async_copy(QKVM.at[0], r["row_grads"], local.at[1])
    grad_copy.start()

    total = lambda v: jnp.sum(jnp.sum(v, axis=1, keepdims=True), axis=0, keepdims=True)
    chosen = total(jnp.sum(SEGR[...], axis=0)[1:2])
    lanes = lax.broadcasted_iota(jnp.int32, (1, D), 1)
    SM[3:4] = (
        jnp.where(lanes == 0, chosen, 0.0)
        + jnp.where(lanes == 1, total(STAT[1:2]), 0.0)
        + jnp.where(lanes == 2, total(STAT[0:1]), 0.0)
    )
    SMS, SMR, SMZ = r["SMS"], r["SMR"], r["SMZ"]
    sums = [links.go(SM, SMR.at[0], to_c)]
    reduce_k.second()
    reduce_v.third()
    reduce_down.last()
    sums[0].wait_recv()
    SMS[0] = SM[...] + SMR[0]
    sums.append(links.go(SMS.at[0], SMR.at[1], to_x))
    reduce_q.second()
    reduce_k.third()
    reduce_o.last()
    sums[1].wait_recv()
    SMS[1] = SMS[0] + SMR[1]
    sums.append(links.go(SMS.at[1], SMR.at[2], to_y))
    reduce_v.last()
    reduce_down.finish()
    reduce_q.third()
    sums[2].wait_recv()
    SMZ[z] = SMS[1] + SMR[2]
    sums = [links.go(SMZ.at[z], SMZ.at[z], dev(ahead[dz], x, y, c)) for dz in range(1, A)]
    reduce_k.last()
    reduce_o.finish()
    reduce_v.finish()
    reduce_q.last()
    for copy in sums:
        copy.wait_recv()
    r["small"][...] = jnp.sum(SMZ[...], axis=0)
    reduce_k.finish()
    reduce_q.finish()
    outs = [
        pltpu.make_async_copy(r["FIN"], r["mlp_grads"], local.at[2]),
        pltpu.make_async_copy(r["FINA"], r["attn_grads"], local.at[3]),
    ]
    for copy in outs:
        copy.start()
    links.drain()
    for copy in outs + [new_copy, grad_copy]:
        copy.wait()
    for k, name in enumerate(DEBUG):
        copy = pltpu.make_async_copy(r[name], r["dbg_" + name], local.at[4])
        copy.start()
        copy.wait()


def finish_kernel(dims, slots, rows, row_grads, attn_grads, mlp_grads, small, base, base_grad,
                  out, out_grad, stats, router, gain_one, gain_two, attn_out, up_out, down_out,
                  attn_stage, up_stage, down_stage, sems):
    S, per, R, Wd, part = dims
    i = pl.program_id(0)
    s, k = i // per, i % per
    size, cap = base.shape[1], slots.shape[1]
    position = lax.broadcasted_iota(jnp.int32, (size, cap), 0) + k * size
    onehot = jnp.where(slots[pl.ds(s, 1), :] == position, 1.0, 0.0)
    hit = jnp.max(onehot, axis=-1, keepdims=True) > 0.5
    onehot = onehot.astype(bf16)
    own = aligned(s * cap, cap)
    for new, old, target in ((rows, base, out), (row_grads, base_grad, out_grad)):
        picked = dot(onehot, new[own, :], 1, 0).astype(bf16)
        target[0] = jnp.where(hit, picked, old[0])

    attn_copies = [
        pltpu.make_async_copy(attn_stage.at[g], attn_out[g], sems.at[g]) for g in range(4)
    ]
    down_copies = [
        pltpu.make_async_copy(down_stage.at[q], down_out.at[pl.ds(q * R, R)], sems.at[4 + q]) for q in range(4)
    ]
    up_copy = pltpu.make_async_copy(up_stage, up_out, sems.at[8])

    @pl.when(i == 0)
    def _():
        for g in range(4):
            attn_stage[g] = attn_grads[g].astype(f32)
            attn_copies[g].start()
        w = lax.axis_index("wide")
        gains = pltpu.roll(small[...], (small.shape[1] - w * R) % small.shape[1], 1)
        gain_one[...] = gains[0:1, :R]
        gain_two[...] = gains[1:2, :R]
        router[...] = small[2:3]
        lane = lax.broadcasted_iota(jnp.int32, (1, small.shape[1]), 1)
        counts = small[3:4]
        valid = jnp.sum(jnp.where(lane == 1, counts, 0.0), axis=1, keepdims=True)
        shifted = jnp.where(lane == 1, pltpu.roll(counts, small.shape[1] - 1, 1), counts)
        stats[...] = (shifted / valid)[:, : stats.shape[1]]

    @pl.when(i == 1)
    def _():
        for q in range(4):
            down_stage[q] = mlp_grads[1, q].astype(f32)
            down_copies[q].start()

    @pl.when(i == 2)
    def _():
        for q in range(4):
            for v in range(Wd):
                at = (v * 4 + q) * part
                up_stage[:, at : at + part] = mlp_grads[0, q, :, v * part : (v + 1) * part].astype(f32)
        up_copy.start()

    @pl.when(i == S * per - 1)
    def _():
        for copy in attn_copies + down_copies + [up_copy]:
            copy.wait()


def finish(mesh, res, slots, block_input, cotangent, R, FF):
    S, SEQ, D = block_input.shape
    Wd = mesh.shape["wide"]
    size = 1024
    per, part = SEQ // size, FF // (4 * Wd)

    def kernel(slots, rows, row_grads, attn, mlp, small, base, base_grad, out, out_grad, stats, router,
               gain_one, gain_two, q, k, v, o, up, down, *scratch):
        finish_kernel((S, per, R, Wd, part), slots, rows, row_grads, attn, mlp, small, base, base_grad,
                      out, out_grad, stats, router, gain_one, gain_two, (q, k, v, o), up, down, *scratch)

    vmem, hbm = pl.BlockSpec(memory_space=pltpu.VMEM), pl.BlockSpec(memory_space=pl.ANY)
    tile = pl.BlockSpec((1, size, D), lambda i: (i // per, i % per, 0))
    shape = jax.ShapeDtypeStruct
    return pl.pallas_call(
        kernel,
        grid=(S * per,),
        out_shape=[shape(block_input.shape, bf16)] * 2
        + [shape((1, 2), f32), shape((1, D), f32), shape((1, R), f32), shape((1, R), f32)]
        + [shape((R, D), f32)] * 4
        + [shape((R, FF), f32), shape((4 * R, D), f32)],
        in_specs=[vmem] * 6 + [tile] * 2,
        out_specs=[tile] * 2 + [vmem] * 4 + [hbm] * 6,
        scratch_shapes=[
            pltpu.VMEM((4, R, D), f32),
            pltpu.VMEM((R, FF), f32),
            pltpu.VMEM((4, R, D), f32),
            pltpu.SemaphoreType.DMA((9,)),
        ],
        compiler_params=pltpu.CompilerParams(vmem_limit_bytes=60 * MIB),
        name="finish_rows",
    )(slots, res["new_rows"], res["row_grads"], res["attn_grads"].reshape(4, R, D), res["mlp_grads"],
      res["small"], block_input, cotangent)


def run_block(mesh, inputs, S, SEQ, CAP, D, R):
    Wd = mesh.shape["wide"]
    A, RB, T = Wd // 2, R // 2, S * CAP
    dims = dict(A=A, R=R, T=T, S=S, CAP=CAP, SEQ=SEQ, D=D, RB=RB)
    out_shapes = {
        "new_rows": ((T, D), bf16),
        "row_grads": ((T, D), bf16),
        "mlp_grads": ((2, 4, R, D), bf16),
        "attn_grads": ((4, 2, RB, D), bf16),
        "small": ((8, D), f32),
    }
    scratch = {
        "WA": ((4, Wd, R, D), bf16),
        "WU": ((A, 2, R, D), bf16),
        "WD": ((A, 2, R, D), bf16),
        "GP": ((Wd, 8, D), f32),
        "GN": ((8, D), f32),
        "NT": ((4, A, 2, RB, D), bf16),
        "MG": ((4, T, D), bf16),
        "ACT": ((2, A, 2, 2, RB, D), bf16),
        "DG": ((2, A, 2, 2, RB, D), bf16),
        "QKVM": ((4, T, D), bf16),
        "N1": ((T, D), bf16),
        "RT": ((T, D), bf16),
        "OG": ((T, D), bf16),
        "AO": ((T, D), f32),
        "NG": ((T, D), f32),
        "MO": ((T, D), f32),
        "PS": ((2, T, D), bf16),
        "PR": ((2, T, D), bf16),
        "YS": ((T, D), bf16),
        "YS2": ((T, D), bf16),
        "YR": ((2, T, D), bf16),
        "GXR": ((A, R, D), bf16),
        "GZR": ((2, A - 1, R, D), bf16),
        "FIN": ((2, 4, R, D), bf16),
        "YRA": ((4, A // 2, RB, D // 2), bf16),
        "YRB": ((4, A // 2, 2, RB, D // 2), bf16),
        "XRB": ((4, A // 2, RB, D // 2), bf16),
        "ZR": ((4, A - 1, RB, D // 2), bf16),
        "FINA": ((4, 2, RB, D), bf16),
        "COLS": ((T, LANES), f32),
        "BIAS": ((S, CAP, CAP), f32),
        "SEGR": ((S, 16, CAP), f32),
        "STAT": ((8, CHUNK), f32),
        "SM": ((8, D), f32),
        "SMS": ((2, 8, D), f32),
        "SMR": ((3, 8, D), f32),
        "SMZ": ((A, 8, D), f32),
    }
    for name in DEBUG:
        out_shapes["dbg_" + name] = scratch[name]
    count = copy_count(A)
    semaphores = {
        "send": pltpu.SemaphoreType.DMA((count,)),
        "recv": pltpu.SemaphoreType.DMA((count,)),
        "local": pltpu.SemaphoreType.DMA((11 + Wd,)),
        "credit": pltpu.SemaphoreType.REGULAR((3,)),
    }
    in_vmem = ("gains", "slots", "segments", "pad_mask")
    hbm, vmem = pl.BlockSpec(memory_space=pl.ANY), pl.BlockSpec(memory_space=pltpu.VMEM)
    names = list(inputs) + list(out_shapes) + list(scratch) + list(semaphores)
    results = pl.pallas_call(
        functools.partial(block_kernel, dims, names),
        out_shape=[jax.ShapeDtypeStruct(*v) for v in out_shapes.values()],
        in_specs=[vmem if k in in_vmem else hbm for k in inputs],
        out_specs=[vmem if k == "small" else hbm for k in out_shapes],
        scratch_shapes=[pltpu.VMEM(*v) for v in scratch.values()] + list(semaphores.values()),
        compiler_params=pltpu.CompilerParams(
            collective_id=0, has_side_effects=True, vmem_limit_bytes=64 * MIB - 65536
        ),
        name="routed_block",
    )(*inputs.values())
    return dict(zip(out_shapes, results))


def body(mesh, block_input, query_weight, key_weight, value_weight, out_weight, up_weight, down_weight,
         attn_gain, mlp_gain, router_weight, slots, segments, pad_mask, cotangent):
    S, SEQ, D = block_input.shape
    CAP = slots.shape[1]
    R, FF = up_weight.shape
    Wd = mesh.shape["wide"]
    w, n = lax.axis_index("wide"), lax.axis_index("narrow")
    part = FF // (4 * Wd)
    assert FF == 4 * D and S == 2 and 4 * CAP == D and part == R and mesh.shape["narrow"] == 4
    if part % LANES:
        up_weight = lax.dynamic_index_in_dim(up_weight.reshape(R, Wd, 4, part), n, axis=2, keepdims=False)
        up_weight = up_weight.reshape(R, D)
    shard = jnp.stack([attn_gain, mlp_gain]).astype(f32)
    line = lax.broadcasted_iota(jnp.int32, (8, D), 0)
    gains = jnp.where(line == 2, router_weight.astype(f32)[None], 0.0)
    gains = lax.dynamic_update_slice(gains, shard, (0, w * R))
    inputs = {
        "block_input": block_input,
        "cotangent": cotangent,
        "w_query": query_weight,
        "w_key": key_weight,
        "w_value": value_weight,
        "w_out": out_weight,
        "w_up": up_weight,
        "w_down": down_weight,
        "gains": gains,
        "slots": slots,
        "segments": segments,
        "pad_mask": pad_mask,
    }
    res = run_block(mesh, inputs, S, SEQ, CAP, D, R)
    outs = finish(mesh, res, slots, block_input, cotangent, R, FF)
    result = (outs[0], outs[1], *outs[6:], outs[4].reshape(R), outs[5].reshape(R), outs[3].reshape(D), outs[2].reshape(2))
    if DEBUG:
        return result, {k: res["dbg_" + k] for k in DEBUG}
    return result


def solution(mesh):
    rows, wide = P(("wide", "narrow")), P("wide")
    return jax.shard_map(
        functools.partial(body, mesh),
        mesh=mesh,
        in_specs=(rows,) + (wide,) * 8 + (P(),) + (rows,) * 4,
        out_specs=(rows, rows) + (wide,) * 8 + (P(), P()),
        check_vma=False,
    )
```
